32 devices in a mesh: seq: 2 (over x), pos: 16 (over z, y, core).
Axes of the slice: x: 2, y: 2, z: 4, core: 2. Of those that a mesh axis runs over, the one named last changes fastest.
Arguments:
- skip_stream_input: bfloat16 [8, 128, 768], P('seq', 'pos'), may hold values from -6 to 6
- lateral_asking_vectors: bfloat16 [8, 128, 768], P('seq', 'pos'), may hold values from -30 to 30
- lateral_matched_vectors: bfloat16 [8, 128, 768], P('seq', 'pos'), may hold values from -6 to 6
- lateral_carried_vectors: bfloat16 [8, 128, 768], P('seq', 'pos'), may hold values from -6 to 6
- lateral_closing_linear: bfloat16 [768, 768], replicated, may hold values from -0.21875 to 0.21875
- upright_normalizer_multiplier: float32 [768], replicated, may hold values from 0.1 to 1.9
- upright_threefold_linear: bfloat16 [768, 2304], P(None, 'seq'), may hold values from -0.21875 to 0.21875
- upright_closing_linear: bfloat16 [768, 768], replicated, may hold values from -0.21875 to 0.21875
- regression_factors: float32 [12], replicated, may hold values from -192 to 192
- regression_offset: float32 [1], replicated, may hold values from -3 to 3
Outputs:
- alignment_output: bfloat16 [8, 128, 768], P('seq', 'pos')
- pairing_chances: float32 [128, 128], P('pos', 'seq')
The draws below stay inside these ranges and needn't reach their ends.
All inputs are finite; a program needn't handle non-finite values.
Results may differ from the reference program's by a relative error of at most 0.004.
Values may be sent and summed in bfloat16 or wider, within the bound.
No kernel may reach another device: no remote copies, remote signals or barrier semaphores. Data moves between devices by JAX's collectives and lax.ppermute only.
A program may use at most 64 MiB of HBM per device.

```python
import jax
import jax.numpy as jnp
from jax import lax

EMBED_BREADTH = 768
FOCUS_GROUPS = 12
HEAD = 64
HOMOLOG_TOTAL = 8
COLUMN_SPAN = 128


def pair_fields(key):
    base_key = jax.random.fold_in(key, 101)
    key_query = jax.random.fold_in(base_key, 1)
    key_keys = jax.random.fold_in(base_key, 2)
    query_field = jnp.clip(jax.random.normal(key_query, (HOMOLOG_TOTAL, COLUMN_SPAN, EMBED_BREADTH), jnp.float32), -5.0, 5.0) * 1.2
    key_field = jnp.clip(jax.random.normal(key_keys, (HOMOLOG_TOTAL, COLUMN_SPAN, EMBED_BREADTH), jnp.float32), -5.0, 5.0) * 1.2
    return (query_field, key_field)


def draw_lateral_asking_vectors(key, part):
    return pair_fields(key)[0].astype(jnp.bfloat16)


def draw_lateral_matched_vectors(key, part):
    return pair_fields(key)[1].astype(jnp.bfloat16)


def block_levels(key, extent, split, smallest, top_value):
    level = 1.0
    for axis_at, blocks in split:
        steps = jax.random.uniform(jax.random.fold_in(jax.random.fold_in(key, 6), axis_at), (blocks,), jnp.float32, smallest / len(split), top_value / len(split))
        level = level * jnp.repeat(jnp.exp(steps), extent[axis_at] // blocks).reshape((-1,) + (1,) * (len(extent) - 1 - axis_at))
    return level


def scatter_about(rng, extent, width, bound, shards=(), dtype=jnp.bfloat16):
    result = width * jax.random.normal(rng, extent, jnp.float32)
    if shards:
        result = result * block_levels(rng, extent, shards, -0.22, 0.18)
    return jnp.clip(result, -bound, bound).astype(dtype)


def setup_inputs(seed: int = 0) -> dict:
    arg_keys = jax.random.split(jax.random.key(seed), 11)
    skip_stream_input = scatter_about(arg_keys[0], (HOMOLOG_TOTAL, COLUMN_SPAN, EMBED_BREADTH), 1.0, 6.0, ((0, 2), (1, 16)))
    lateral_asking_vectors = draw_lateral_asking_vectors(jax.random.fold_in(arg_keys[10], 71), 0)
    lateral_matched_vectors = draw_lateral_matched_vectors(jax.random.fold_in(arg_keys[10], 71), 0)
    lateral_carried_vectors = scatter_about(arg_keys[3], (HOMOLOG_TOTAL, COLUMN_SPAN, EMBED_BREADTH), 1.0, 6.0, ((0, 2), (1, 16)))
    lateral_closing_linear = scatter_about(arg_keys[4], (EMBED_BREADTH, EMBED_BREADTH), EMBED_BREADTH ** -0.5, 0.21875)
    upright_normalizer_multiplier = jnp.clip(1.0 + 0.18 * jax.random.normal(arg_keys[5], (EMBED_BREADTH,), jnp.float32), 0.1, 1.9)
    upright_threefold_linear = scatter_about(arg_keys[6], (EMBED_BREADTH, 3 * EMBED_BREADTH), EMBED_BREADTH ** -0.5, 0.21875, ((1, 2),))
    upright_closing_linear = scatter_about(arg_keys[7], (EMBED_BREADTH, EMBED_BREADTH), EMBED_BREADTH ** -0.5, 0.21875)
    regression_factors = scatter_about(arg_keys[8], (FOCUS_GROUPS,), (COLUMN_SPAN // 4), 192.0, (), jnp.float32)
    regression_offset = scatter_about(arg_keys[9], (1,), 1.0, 3.0, (), jnp.float32)
    return {"skip_stream_input": skip_stream_input, "lateral_asking_vectors": lateral_asking_vectors, "lateral_matched_vectors": lateral_matched_vectors, "lateral_carried_vectors": lateral_carried_vectors, "lateral_closing_linear": lateral_closing_linear, "upright_normalizer_multiplier": upright_normalizer_multiplier, "upright_threefold_linear": upright_threefold_linear, "upright_closing_linear": upright_closing_linear, "regression_factors": regression_factors, "regression_offset": regression_offset}


def layer_norm(values, scaling):
    average = lax.optimization_barrier(jnp.mean(values, axis=-1, keepdims=True))
    centered = values - average
    spread = lax.optimization_barrier(jnp.mean(centered * centered, axis=-1, keepdims=True))
    return centered * lax.rsqrt(spread + 1e-05) * scaling

def softmax_last(scores):
    row_peak = lax.optimization_barrier(jnp.max(scores, axis=-1, keepdims=True))
    exponent = jnp.exp(scores - row_peak)
    return exponent / lax.optimization_barrier(jnp.sum(exponent, axis=-1, keepdims=True))

def softmax_plain(scores):
    exponent = jnp.exp(scores)
    return exponent / lax.optimization_barrier(jnp.sum(exponent, axis=-1, keepdims=True))

def reference(skip_stream_input, lateral_asking_vectors, lateral_matched_vectors, lateral_carried_vectors, lateral_closing_linear, upright_normalizer_multiplier, upright_threefold_linear, upright_closing_linear, regression_factors, regression_offset):
    upper_limit = lax.Precision.HIGHEST
    queries = lateral_asking_vectors.astype(jnp.float32).reshape(HOMOLOG_TOTAL, COLUMN_SPAN, FOCUS_GROUPS, HEAD)
    key_rows = lateral_matched_vectors.astype(jnp.float32).reshape(HOMOLOG_TOTAL, COLUMN_SPAN, FOCUS_GROUPS, HEAD)
    factor = 1.0 / (jnp.sqrt(jnp.float32(HEAD)) * jnp.sqrt(jnp.float32(HOMOLOG_TOTAL)))
    logits = jnp.einsum('rihd,rjhd->hij', queries, key_rows, precision=upper_limit) * factor
    affinity_shares = softmax_last(logits).astype(jnp.bfloat16)
    value_rows = lateral_carried_vectors.astype(jnp.float32).reshape(HOMOLOG_TOTAL, COLUMN_SPAN, FOCUS_GROUPS, HEAD)
    mixture = jnp.einsum('hij,rjhd->rihd', affinity_shares.astype(jnp.float32), value_rows, precision=upper_limit)
    horizontal_mixed_result = mixture.astype(jnp.bfloat16).reshape(HOMOLOG_TOTAL * COLUMN_SPAN, EMBED_BREADTH)
    residue_embedding = skip_stream_input.reshape(HOMOLOG_TOTAL * COLUMN_SPAN, EMBED_BREADTH).astype(jnp.float32) + jnp.dot(horizontal_mixed_result, lateral_closing_linear, preferred_element_type=jnp.float32)
    normed = layer_norm(residue_embedding, upright_normalizer_multiplier).astype(jnp.bfloat16)
    projected = jnp.dot(normed, upright_threefold_linear, preferred_element_type=jnp.float32).astype(jnp.bfloat16)
    projected = projected.reshape(HOMOLOG_TOTAL, COLUMN_SPAN, 3, FOCUS_GROUPS, HEAD).astype(jnp.float32)
    col_query = projected[:, :, 0]
    col_key = projected[:, :, 1]
    col_value = projected[:, :, 2]
    col_scores = jnp.einsum('sphd,tphd->phst', col_query, col_key, precision=upper_limit) * (1.0 / jnp.sqrt(jnp.float32(HEAD)))
    col_weights = softmax_plain(col_scores).astype(jnp.bfloat16)
    column_mixing = jnp.einsum('phst,tphd->sphd', col_weights.astype(jnp.float32), col_value, precision=upper_limit)
    column_mixing = column_mixing.astype(jnp.bfloat16).reshape(HOMOLOG_TOTAL * COLUMN_SPAN, EMBED_BREADTH)
    alignment_output = (residue_embedding + jnp.dot(column_mixing, upright_closing_linear, preferred_element_type=jnp.float32)).astype(jnp.bfloat16)
    affinity_grids = affinity_shares.astype(jnp.float32)
    couple_amount = lax.optimization_barrier(jnp.sum(affinity_grids, axis=1)) + lax.optimization_barrier(jnp.sum(affinity_grids, axis=2))
    focus_group_amount = lax.optimization_barrier(jnp.sum(couple_amount, axis=1))
    combined_groups = jnp.einsum('f,feg->eg', regression_factors, affinity_grids, precision=upper_limit)
    product_adjuster = jnp.einsum('q,qz,qd->zd', regression_factors / focus_group_amount, couple_amount, couple_amount, precision=upper_limit)
    pairing_chances = jax.nn.sigmoid(combined_groups + combined_groups.T - product_adjuster + regression_offset[0])
    return (alignment_output.reshape(HOMOLOG_TOTAL, COLUMN_SPAN, EMBED_BREADTH), pairing_chances)
```

```python
import functools
import math

import jax
import jax.numpy as jnp
from jax import lax
from jax.experimental import pallas as pl
from jax.experimental.pallas import tpu as pltpu
from jax.sharding import PartitionSpec as P

F32 = jnp.float32
BF16 = jnp.bfloat16
HIGHEST = lax.Precision.HIGHEST
LANE_BLOCK = 256


def dot_nn(a, b, precision=None):
    return lax.dot_general(
        a, b, (((1,), (0,)), ((), ())), precision=precision, preferred_element_type=F32
    )


def dot_nt(a, b, precision=None):
    return lax.dot_general(
        a, b, (((1,), (1,)), ((), ())), precision=precision, preferred_element_type=F32
    )


def round_up(n, m):
    return -(-n // m) * m


def lane_block(embed, head):
    return LANE_BLOCK if embed % LANE_BLOCK == 0 and LANE_BLOCK % head == 0 else head


def logits_kernel(head, part_count, *refs):
    q_ref, k_refs, out_ref = refs[0], refs[1 : 1 + part_count], refs[-1]
    rows, sites, embed = q_ref.shape
    width = lane_block(embed, head)
    group = width // head
    lane_head = lax.broadcasted_iota(jnp.int32, (group * sites, width), 1) // head
    row_head = lax.broadcasted_iota(jnp.int32, (group * sites, width), 0) // sites
    own_head = lane_head == row_head
    for block in range(embed // width):
        cols = slice(block * width, (block + 1) * width)
        total = None
        for r in range(rows):
            q = q_ref[r, :, cols].astype(F32)
            q = jnp.where(own_head, jnp.concatenate([q] * group, axis=0), 0.0).astype(BF16)
            keys = jnp.concatenate([k[r, :, cols] for k in k_refs], axis=0)
            term = dot_nt(q, keys)
            total = term if total is None else total + term
        out_ref[block * group * sites : (block + 1) * group * sites, :] = total


def softmax_kernel(factor, heads, part_count, *refs):
    parts, (factor_ref, order_ref, w_ref, pair_ref, held) = refs[:part_count], refs[part_count:]
    rows, length = w_ref.shape
    sites = rows // heads
    logits = parts[0][...]
    for part in parts[1:]:
        logits = logits + part[...]
    logits = logits * factor
    exponent = jnp.exp(logits - jnp.max(logits, axis=1, keepdims=True))
    shares = (exponent / jnp.sum(exponent, axis=1, keepdims=True)).astype(BF16)
    w_ref[...] = shares
    shares = shares.astype(F32)
    row_sum = jnp.sum(shares, axis=1, keepdims=True)
    lane = lax.broadcasted_iota(jnp.int32, (rows, length), 1)
    row = lax.broadcasted_iota(jnp.int32, (rows, length), 0) % sites
    both = (shares + jnp.where(lane == row, row_sum, 0.0)).reshape(heads, sites, length)
    head_rows = round_up(heads, 8)
    held[...] = jnp.zeros_like(held)
    held[0:heads, :] = jnp.sum(both, axis=1)
    merged = shares[0:sites, :] * factor_ref[0]
    for h in range(1, heads):
        merged = merged + shares[h * sites : (h + 1) * sites, :] * factor_ref[h]
    held[head_rows : head_rows + sites, :] = merged
    pair_ref[...] = dot_nn(held[...], order_ref[...], HIGHEST)


def mix_kernel(head, split, v_count, w_count, *refs):
    scalar_ref, w_ref = refs[:2]
    v_refs = refs[2 : 2 + v_count]
    closing_ref, skip_ref, gain_ref = refs[2 + v_count : 5 + v_count]
    weight_refs = refs[5 + v_count : 5 + v_count + w_count]
    hidden_ref, query_ref, kv_ref, mixed, normed, projected = refs[5 + v_count + w_count :]
    rows, sites, embed = skip_ref.shape
    width = lane_block(embed, head)
    group = width // head
    lane_head = lax.broadcasted_iota(jnp.int32, (sites, width), 1) // head
    for block in range(embed // width):
        cols = slice(block * width, (block + 1) * width)
        shares = w_ref[block * group * sites : (block + 1) * group * sites, :]
        for r in range(rows):
            values = jnp.concatenate([v[r, :, cols] for v in v_refs], axis=0)
            product = dot_nn(shares, values)
            own = product[0:sites, :]
            for g in range(1, group):
                own = jnp.where(lane_head == g, product[g * sites : (g + 1) * sites, :], own)
            mixed[r * sites : (r + 1) * sites, cols] = own
    hidden = skip_ref[...].astype(F32).reshape(rows * sites, embed) + dot_nn(
        mixed[...].astype(BF16), closing_ref[...]
    )
    hidden_ref[...] = hidden
    centered = hidden - jnp.mean(hidden, axis=1, keepdims=True)
    spread = jnp.mean(centered * centered, axis=1, keepdims=True)
    unit = (centered * lax.rsqrt(spread + 1e-05) * gain_ref[...]).astype(BF16)
    if split:
        own_ref, first_ref, second_ref = weight_refs
        columns, half = own_ref.shape[1], first_ref.shape[0]
        normed[...] = unit
        own_at = pl.multiple_of(scalar_ref[0] * columns, 128)
        other_at = pl.multiple_of((1 - scalar_ref[0]) * columns, 128)
        first = normed[:, pl.ds(pl.multiple_of(scalar_ref[1] * half, 128), half)]
        second = normed[:, pl.ds(pl.multiple_of((1 - scalar_ref[1]) * half, 128), half)]
        projected[:, pl.ds(own_at, columns)] = dot_nn(unit, own_ref[...]).astype(BF16)
        projected[:, pl.ds(other_at, columns)] = (
            dot_nn(first, first_ref[...]) + dot_nn(second, second_ref[...])
        ).astype(BF16)
    else:
        projected[...] = dot_nn(unit, weight_refs[0][...]).astype(BF16)
    query_ref[...] = projected[:, 0:embed]
    kv_ref[...] = projected[:, embed:]


def column_kernel(head, factor, part_count, *refs):
    q_ref, kv_refs = refs[0], refs[1 : 1 + part_count]
    hidden_ref, closing_ref, out_ref, products, mixed = refs[1 + part_count :]
    rows, sites, embed = out_ref.shape
    heads = embed // head
    padded = round_up(heads, 128)
    pick = (
        lax.broadcasted_iota(jnp.int32, (embed, padded), 0) // head
        == lax.broadcasted_iota(jnp.int32, (embed, padded), 1)
    ).astype(BF16)
    spread = (
        lax.broadcasted_iota(jnp.int32, (padded, embed), 1) // head
        == lax.broadcasted_iota(jnp.int32, (padded, embed), 0)
    ).astype(BF16)
    query = q_ref[...].astype(F32)
    key_values = [kv[...].astype(F32) for kv in kv_refs]
    keys, values = [], []
    for kv in key_values:
        for t in range(kv.shape[0] // sites):
            keys.append(kv[t * sites : (t + 1) * sites, 0:embed])
            values.append(kv[t * sites : (t + 1) * sites, embed:])
    seqs = len(keys)
    for s in range(rows):
        for t in range(seqs):
            at = (s * seqs + t) * sites
            products[at : at + sites, :] = query[s * sites : (s + 1) * sites, :] * keys[t]
    product = products[...]
    high = product.astype(BF16)
    low = (product - high.astype(F32)).astype(BF16)
    scores = (dot_nn(high, pick) + dot_nn(low, pick)) * factor
    exponent = jnp.exp(scores).reshape(rows, seqs, sites, padded)
    shares = (exponent / jnp.sum(exponent, axis=1, keepdims=True)).astype(BF16)
    wide = dot_nn(shares.reshape(rows * seqs * sites, padded), spread)
    for s in range(rows):
        total = None
        for t in range(seqs):
            at = (s * seqs + t) * sites
            term = wide[at : at + sites, :] * values[t]
            total = term if total is None else total + term
        mixed[s * sites : (s + 1) * sites, :] = total
    out = hidden_ref[...] + dot_nn(mixed[...].astype(BF16), closing_ref[...])
    out_ref[...] = out.reshape(rows, sites, embed).astype(BF16)


def contact_kernel(heads, sites, part_count, *refs):
    parts = refs[:part_count]
    factor_ref, offset_ref, own_ref, slab_ref, arrival_ref, out_ref, held, table = refs[part_count:]
    head_rows = round_up(heads, 8)
    step = head_rows + sites
    total, block = None, 0
    for part in parts:
        for at in range(0, part.shape[0], step):
            sums = part[at : at + head_rows, :]
            total = sums if total is None else total + sums
            table[block * sites : (block + 1) * sites, :] = part[at + head_rows : at + step, :]
            block += 1
    amount = jnp.sum(total, axis=1, keepdims=True)
    real = lax.broadcasted_iota(jnp.int32, (head_rows, 1), 0) < heads
    share = jnp.where(real, factor_ref[:, 0:1] / jnp.where(real, amount, 1.0), 0.0)
    held[0:head_rows, :] = total
    held[head_rows:step, :] = table[0:sites, :]
    slab = dot_nn(held[...], slab_ref[...], HIGHEST)
    own = dot_nt(own_ref[...], total * share, HIGHEST)
    mirrored = dot_nn(dot_nt(own_ref[...], table[...], HIGHEST), arrival_ref[...], HIGHEST)
    adjuster = dot_nn(own, slab[0:head_rows, :], HIGHEST)
    out_ref[...] = jax.nn.sigmoid(
        slab[head_rows:step, :] + mirrored - adjuster + offset_ref[0]
    )


def call(kernel, out_shape, operands, smem=(), scratch=(), flops=1000000, bytes_accessed=1000000):
    vmem = pl.BlockSpec(memory_space=pltpu.VMEM)
    specs = [
        pl.BlockSpec(memory_space=pltpu.SMEM) if i in smem else vmem for i in range(len(operands))
    ]
    return pl.pallas_call(
        kernel,
        out_shape=out_shape,
        in_specs=specs,
        out_specs=jax.tree.map(lambda _: vmem, out_shape),
        scratch_shapes=list(scratch),
        compiler_params=pltpu.CompilerParams(vmem_limit_bytes=24 * 1024 * 1024),
        cost_estimate=pl.CostEstimate(
            flops=flops, bytes_accessed=bytes_accessed, transcendentals=0
        ),
    )(*operands)


def stages_of(count):
    stages, stride = [], 1
    while count > 1 and len(stages) < 2 and count % 2 == 0:
        stages.append((stride, 2))
        stride, count = stride * 2, count // 2
    if count > 1:
        stages.append((stride, count))
    return stages[::-1]


def staged_gather(array, axis, count):
    parts = [array]
    for at, (stride, size) in enumerate(stages_of(count)):
        array = parts[0] if len(parts) == 1 else jnp.concatenate(parts, axis=axis)
        parts = [array]
        for delta in range(1, size):
            pairs = []
            for p in range(count):
                a = (p // stride) % size
                pairs.append((p, p + ((a + delta) % size - a) * stride))
            parts.append(lax.ppermute(array, "pos", pairs))
    return parts


def arrival_order(index, count):
    sources = [index]
    for stride, size in stages_of(count):
        grown = []
        for delta in range(size):
            for source in sources:
                a = (source // stride) % size
                grown.append(source + ((a - delta) % size - a) * stride)
        sources = grown
    return jnp.stack(sources)


def per_device(
    skip_stream_input,
    lateral_asking_vectors,
    lateral_matched_vectors,
    lateral_carried_vectors,
    lateral_closing_linear,
    upright_normalizer_multiplier,
    upright_threefold_linear,
    upright_closing_linear,
    regression_factors,
    regression_offset,
):
    rows, sites, embed = lateral_asking_vectors.shape
    heads = regression_factors.shape[0]
    head = embed // heads
    seq_count = lax.axis_size("seq")
    pos_count = lax.axis_size("pos")
    length = sites * pos_count
    slab_width = length // seq_count
    pos_index = lax.axis_index("pos").astype(jnp.int32)
    seq_index = lax.axis_index("seq").astype(jnp.int32)
    swap = [(s, 1 - s) for s in range(2)]
    embed_in, columns = upright_threefold_linear.shape
    split = seq_count == 2 and pos_count % 2 == 0 and columns % 128 == 0 and embed_in % 256 == 0

    key_parts = staged_gather(lateral_matched_vectors, 1, pos_count)
    value_parts = staged_gather(lateral_carried_vectors, 1, pos_count)

    origin = arrival_order(pos_index, pos_count)
    place = (origin[:, None] * sites + jnp.arange(sites, dtype=jnp.int32)[None, :]).reshape(length)
    every = jnp.arange(length, dtype=jnp.int32)
    slab_at = seq_index * slab_width + jnp.arange(slab_width, dtype=jnp.int32)
    order = (place[:, None] == every[None, :]).astype(F32)
    own_rows = pos_index * sites + jnp.arange(sites, dtype=jnp.int32)
    own_select = (own_rows[:, None] == every[None, :]).astype(F32)
    slab_select = (every[:, None] == slab_at[None, :]).astype(F32)
    arrival_select = (place[:, None] == slab_at[None, :]).astype(F32)
    scalars = jnp.stack([seq_index, pos_index % 2])

    if split:
        half = embed_in // 2
        sent = lax.dynamic_slice_in_dim(
            upright_threefold_linear, (pos_index % 2) * half, half, 0
        )
        first = lax.ppermute(sent, "seq", swap)
        second = lax.ppermute(first, "pos", [(p, p ^ 1) for p in range(pos_count)])
        weights = [upright_threefold_linear, first, second]
    else:
        weights = [lax.all_gather(upright_threefold_linear, "seq", axis=1, tiled=True)]

    partial = call(
        functools.partial(logits_kernel, head, len(key_parts)),
        jax.ShapeDtypeStruct((heads * sites, length), F32),
        [lateral_asking_vectors, *key_parts],
    )
    if seq_count == 2:
        partials = [partial, lax.ppermute(partial, "seq", swap)]
    else:
        partials = [lax.psum(partial, "seq")]
    head_rows = round_up(heads, 8)
    shares, pair_local = call(
        functools.partial(
            softmax_kernel,
            1.0 / (math.sqrt(head) * math.sqrt(rows * seq_count)),
            heads,
            len(partials),
        ),
        (
            jax.ShapeDtypeStruct((heads * sites, length), BF16),
            jax.ShapeDtypeStruct((head_rows + sites, length), F32),
        ),
        [*partials, regression_factors, order],
        smem=(len(partials),),
        scratch=[pltpu.VMEM((head_rows + sites, length), F32)],
    )
    pair_parts = staged_gather(pair_local, 0, pos_count)

    cells = rows * sites
    hidden, query, key_value = call(
        functools.partial(mix_kernel, head, split, len(value_parts), len(weights)),
        (
            jax.ShapeDtypeStruct((cells, embed), F32),
            jax.ShapeDtypeStruct((cells, embed), BF16),
            jax.ShapeDtypeStruct((cells, 2 * embed), BF16),
        ),
        [
            scalars,
            shares,
            *value_parts,
            lateral_closing_linear,
            skip_stream_input,
            upright_normalizer_multiplier.reshape(1, embed),
            *weights,
        ],
        smem=(0,),
        scratch=[
            pltpu.VMEM((cells, embed), F32),
            pltpu.VMEM((cells, embed), BF16),
            pltpu.VMEM((cells, 3 * embed), BF16),
        ],
    )
    if seq_count == 2:
        kv_parts = [key_value, lax.ppermute(key_value, "seq", swap)]
    else:
        kv_parts = [lax.all_gather(key_value, "seq", axis=0, tiled=True)]
    alignment_output = call(
        functools.partial(column_kernel, head, 1.0 / math.sqrt(head), len(kv_parts)),
        jax.ShapeDtypeStruct((rows, sites, embed), BF16),
        [query, *kv_parts, hidden, upright_closing_linear],
        scratch=[
            pltpu.VMEM((cells * rows * seq_count, embed), F32),
            pltpu.VMEM((cells, embed), F32),
        ],
    )

    factor_column = jnp.zeros((head_rows, 128), F32).at[:heads, :].set(regression_factors[:, None])
    n = len(pair_parts)
    pairing_chances = call(
        functools.partial(contact_kernel, heads, sites, n),
        jax.ShapeDtypeStruct((sites, slab_width), F32),
        [*pair_parts, factor_column, regression_offset, own_select, slab_select, arrival_select],
        smem=(n + 1,),
        scratch=[
            pltpu.VMEM((head_rows + sites, length), F32),
            pltpu.VMEM((length, length), F32),
        ],
    )
    return alignment_output, pairing_chances


def solution(mesh):
    cells = P("seq", "pos", None)
    return jax.shard_map(
        per_device,
        mesh=mesh,
        in_specs=(cells, cells, cells, cells, P(), P(), P(None, "seq"), P(), P(), P()),
        out_specs=(cells, P("pos", "seq")),
        check_vma=False,
    )
```

```python
import functools
import math

import jax
import jax.numpy as jnp
import numpy as np
from jax import lax
from jax.experimental import pallas as pl
from jax.experimental.pallas import tpu as pltpu
from jax.sharding import PartitionSpec as P

F32 = jnp.float32
BF16 = jnp.bfloat16
HIGHEST = lax.Precision.HIGHEST
LANE_BLOCK = 256


def dot_nn(a, b, precision=None):
    return lax.dot_general(
        a, b, (((1,), (0,)), ((), ())), precision=precision, preferred_element_type=F32
    )


def dot_nt(a, b, precision=None):
    return lax.dot_general(
        a, b, (((1,), (1,)), ((), ())), precision=precision, preferred_element_type=F32
    )


def round_up(n, m):
    return -(-n // m) * m


def lane_block(embed, head):
    return LANE_BLOCK if embed % LANE_BLOCK == 0 and LANE_BLOCK % head == 0 else head


def logits_kernel(head, part_count, *refs):
    q_ref, k_refs, out_ref = refs[0], refs[1 : 1 + part_count], refs[-1]
    rows, sites, embed = q_ref.shape
    width = lane_block(embed, head)
    group = width // head
    lane_head = lax.broadcasted_iota(jnp.int32, (group * sites, width), 1) // head
    row_head = lax.broadcasted_iota(jnp.int32, (group * sites, width), 0) // sites
    own_head = lane_head == row_head
    for block in range(embed // width):
        cols = slice(block * width, (block + 1) * width)
        total = None
        for r in range(rows):
            q = q_ref[r, :, cols].astype(F32)
            q = jnp.where(own_head, jnp.concatenate([q] * group, axis=0), 0.0).astype(BF16)
            keys = jnp.concatenate([k[r, :, cols] for k in k_refs], axis=0)
            term = dot_nt(q, keys)
            total = term if total is None else total + term
        out_ref[block * group * sites : (block + 1) * group * sites, :] = total


def softmax_kernel(factor, heads, part_count, *refs):
    parts, (factor_ref, order_ref, w_ref, pair_ref, held) = refs[:part_count], refs[part_count:]
    rows, length = w_ref.shape
    sites = rows // heads
    logits = parts[0][...]
    for part in parts[1:]:
        logits = logits + part[...]
    logits = logits * factor
    exponent = jnp.exp(logits - jnp.max(logits, axis=1, keepdims=True))
    shares = (exponent / jnp.sum(exponent, axis=1, keepdims=True)).astype(BF16)
    w_ref[...] = shares
    shares = shares.astype(F32)
    row_sum = jnp.sum(shares, axis=1, keepdims=True)
    lane = lax.broadcasted_iota(jnp.int32, (rows, length), 1)
    row = lax.broadcasted_iota(jnp.int32, (rows, length), 0) % sites
    both = (shares + jnp.where(lane == row, row_sum, 0.0)).reshape(heads, sites, length)
    head_rows = round_up(heads, 8)
    held[...] = jnp.zeros_like(held)
    held[0:heads, :] = jnp.sum(both, axis=1)
    merged = shares[0:sites, :] * factor_ref[0]
    for h in range(1, heads):
        merged = merged + shares[h * sites : (h + 1) * sites, :] * factor_ref[h]
    held[head_rows : head_rows + sites, :] = merged
    pair_ref[...] = jnp.broadcast_to(
        dot_nn(held[...], order_ref[...], HIGHEST)[None], pair_ref.shape
    )


def mix_kernel(head, v_count, *refs):
    w_ref, v_refs = refs[0], refs[1 : 1 + v_count]
    closing_ref, skip_ref, gain_ref, hidden_ref, normed_ref, mixed = refs[1 + v_count :]
    rows, sites, embed = skip_ref.shape
    width = lane_block(embed, head)
    group = width // head
    lane_head = lax.broadcasted_iota(jnp.int32, (sites, width), 1) // head
    for block in range(embed // width):
        cols = slice(block * width, (block + 1) * width)
        shares = w_ref[block * group * sites : (block + 1) * group * sites, :]
        for r in range(rows):
            values = jnp.concatenate([v[r, :, cols] for v in v_refs], axis=0)
            product = dot_nn(shares, values)
            own = product[0:sites, :]
            for g in range(1, group):
                own = jnp.where(lane_head == g, product[g * sites : (g + 1) * sites, :], own)
            mixed[r * sites : (r + 1) * sites, cols] = own
    hidden = skip_ref[...].astype(F32).reshape(rows * sites, embed) + dot_nn(
        mixed[...].astype(BF16), closing_ref[...]
    )
    hidden_ref[...] = hidden
    centered = hidden - jnp.mean(hidden, axis=1, keepdims=True)
    spread = jnp.mean(centered * centered, axis=1, keepdims=True)
    normed_ref[...] = (centered * lax.rsqrt(spread + 1e-05) * gain_ref[...]).astype(BF16)


def project_kernel(part_count, *refs):
    parts, (weight_ref, out_ref) = refs[:part_count], refs[part_count:]
    normed = jnp.concatenate([part[...] for part in parts], axis=0)
    out_ref[...] = dot_nn(normed, weight_ref[...]).astype(BF16)


def column_kernel(head, factor, swapped, *refs):
    if swapped:
        scalar_ref, own_ref, other_ref = refs[:3]
        full = refs[-1]
        hidden_ref, closing_ref, out_ref, products, mixed = refs[3:-1]
        cells, columns = own_ref.shape
        own_at = pl.multiple_of(scalar_ref[0] * columns, 128)
        other_at = pl.multiple_of((1 - scalar_ref[0]) * columns, 128)
        full[:, pl.ds(own_at, columns)] = own_ref[...]
        full[0 : cells // 2, pl.ds(other_at, columns)] = other_ref[cells // 2 :, :]
        full[cells // 2 :, pl.ds(other_at, columns)] = other_ref[0 : cells // 2, :]
    else:
        query_ref, full = refs[:2]
        hidden_ref, closing_ref, out_ref, products, mixed = refs[2:]
    rows, sites, embed = out_ref.shape
    own_rows = rows * sites
    heads = embed // head
    padded = round_up(heads, 128)
    pick = (
        lax.broadcasted_iota(jnp.int32, (embed, padded), 0) // head
        == lax.broadcasted_iota(jnp.int32, (embed, padded), 1)
    ).astype(BF16)
    spread = (
        lax.broadcasted_iota(jnp.int32, (padded, embed), 1) // head
        == lax.broadcasted_iota(jnp.int32, (padded, embed), 0)
    ).astype(BF16)
    if swapped:
        query = full[0:own_rows, 0:embed].astype(F32)
        key, value = full[:, embed : 2 * embed].astype(F32), full[:, 2 * embed :].astype(F32)
    else:
        query = query_ref[...].astype(F32)
        key, value = full[:, 0:embed].astype(F32), full[:, embed:].astype(F32)
    seqs = key.shape[0] // sites
    keys = [key[t * sites : (t + 1) * sites, :] for t in range(seqs)]
    values = [value[t * sites : (t + 1) * sites, :] for t in range(seqs)]
    for s in range(rows):
        for t in range(seqs):
            at = (s * seqs + t) * sites
            products[at : at + sites, :] = query[s * sites : (s + 1) * sites, :] * keys[t]
    product = products[...]
    high = product.astype(BF16)
    low = (product - high.astype(F32)).astype(BF16)
    scores = (dot_nn(high, pick) + dot_nn(low, pick)) * factor
    exponent = jnp.exp(scores).reshape(rows, seqs, sites, padded)
    shares = (exponent / jnp.sum(exponent, axis=1, keepdims=True)).astype(BF16)
    wide = dot_nn(shares.reshape(rows * seqs * sites, padded), spread)
    for s in range(rows):
        total = None
        for t in range(seqs):
            at = (s * seqs + t) * sites
            term = wide[at : at + sites, :] * values[t]
            total = term if total is None else total + term
        mixed[s * sites : (s + 1) * sites, :] = total
    out = hidden_ref[...] + dot_nn(mixed[...].astype(BF16), closing_ref[...])
    out_ref[...] = out.reshape(rows, sites, embed).astype(BF16)


def contact_kernel(heads, scalar_ref, pair_ref, factor_ref, offset_ref, own_ref, slab_ref, out_ref, held):
    count, step, length = pair_ref.shape
    head_rows = round_up(heads, 8)
    sites = step - head_rows
    blocks = slab_ref.shape[1] // sites
    total = pair_ref[0, 0:head_rows, :]
    for n in range(1, count):
        total = total + pair_ref[n, 0:head_rows, :]
    held[0:head_rows, :] = total
    held[head_rows:step, :] = pair_ref[scalar_ref[1], head_rows:step, :]
    first = scalar_ref[0] * blocks
    table = jnp.concatenate(
        [pair_ref[first + n, head_rows:step, :] for n in range(blocks)], axis=0
    )
    amount = jnp.sum(total, axis=1, keepdims=True)
    real = lax.broadcasted_iota(jnp.int32, (head_rows, 1), 0) < heads
    share = jnp.where(real, factor_ref[:, 0:1] / jnp.where(real, amount, 1.0), 0.0)
    slab = dot_nn(held[...], slab_ref[...], HIGHEST)
    own = dot_nt(own_ref[...], total * share, HIGHEST)
    mirrored = dot_nt(own_ref[...], table, HIGHEST)
    adjuster = dot_nn(own, slab[0:head_rows, :], HIGHEST)
    out_ref[...] = jax.nn.sigmoid(
        slab[head_rows:step, :] + mirrored - adjuster + offset_ref[0]
    )


def call(kernel, out_shape, operands, smem=(), scratch=(), flops=1000000, bytes_accessed=1000000):
    vmem = pl.BlockSpec(memory_space=pltpu.VMEM)
    specs = [
        pl.BlockSpec(memory_space=pltpu.SMEM) if i in smem else vmem for i in range(len(operands))
    ]
    return pl.pallas_call(
        kernel,
        out_shape=out_shape,
        in_specs=specs,
        out_specs=jax.tree.map(lambda _: vmem, out_shape),
        scratch_shapes=list(scratch),
        compiler_params=pltpu.CompilerParams(vmem_limit_bytes=24 * 1024 * 1024),
        cost_estimate=pl.CostEstimate(
            flops=flops, bytes_accessed=bytes_accessed, transcendentals=0
        ),
    )(*operands)


def stages_of(count):
    stages, stride = [], 1
    while count > 1 and len(stages) < 2 and count % 2 == 0:
        stages.append((stride, 2))
        stride, count = stride * 2, count // 2
    if count > 1:
        stages.append((stride, count))
    return stages[::-1]


def send_pos(array, count, stride, size, delta):
    pairs = []
    for p in range(count):
        a = (p // stride) % size
        pairs.append((p, p + ((a + delta) % size - a) * stride))
    return lax.ppermute(array, "pos", pairs)


def staged_gather(array, axis, count):
    parts = [array]
    for at, (stride, size) in enumerate(stages_of(count)):
        if at == 1:
            parts = [jnp.concatenate(parts, axis=axis)]
        parts = parts + [
            send_pos(part, count, stride, size, delta)
            for delta in range(1, size)
            for part in parts
        ]
    return parts


def arrival_order(index, count):
    digits = [()]
    for stage in stages_of(count):
        digits = [d + (delta,) for delta in range(stage[1]) for d in digits]
    origin = jnp.zeros((count,), jnp.int32)
    for at, (stride, size) in enumerate(stages_of(count)):
        delta = np.array([d[at] for d in digits], np.int32)
        origin = origin + ((index // stride) % size + size - delta) % size * stride
    return origin


def after(array, *others):
    return lax.optimization_barrier((array, *others))[0]


def per_device(
    skip_stream_input,
    lateral_asking_vectors,
    lateral_matched_vectors,
    lateral_carried_vectors,
    lateral_closing_linear,
    upright_normalizer_multiplier,
    upright_threefold_linear,
    upright_closing_linear,
    regression_factors,
    regression_offset,
):
    rows, sites, embed = lateral_asking_vectors.shape
    heads = regression_factors.shape[0]
    head = embed // heads
    seq_count = lax.axis_size("seq")
    pos_count = lax.axis_size("pos")
    length = sites * pos_count
    slab_width = length // seq_count
    cells = rows * sites
    pos_index = lax.axis_index("pos").astype(jnp.int32)
    seq_index = lax.axis_index("seq").astype(jnp.int32)
    swap = [(s, 1 - s) for s in range(2)]
    columns = upright_threefold_linear.shape[1]
    swapped = seq_count == 2 and columns % 128 == 0

    key_parts = staged_gather(lateral_matched_vectors, 1, pos_count)
    value_parts = staged_gather(
        after(lateral_carried_vectors, key_parts[0]), 1, pos_count
    )

    origin = arrival_order(pos_index, pos_count)
    place = (origin[:, None] * sites + jnp.arange(sites, dtype=jnp.int32)[None, :]).reshape(length)
    every = jnp.arange(length, dtype=jnp.int32)
    slab_at = seq_index * slab_width + jnp.arange(slab_width, dtype=jnp.int32)
    order = (place[:, None] == every[None, :]).astype(F32)
    own_rows = pos_index * sites + jnp.arange(sites, dtype=jnp.int32)
    own_select = (own_rows[:, None] == every[None, :]).astype(F32)
    slab_select = (every[:, None] == slab_at[None, :]).astype(F32)
    scalars = jnp.stack([seq_index, pos_index])

    partial = call(
        functools.partial(logits_kernel, head, len(key_parts)),
        jax.ShapeDtypeStruct((heads * sites, length), F32),
        [lateral_asking_vectors, *key_parts],
    )
    if seq_count == 2:
        partials = [partial, lax.ppermute(partial, "seq", swap)]
    else:
        partials = [lax.psum(partial, "seq")]
    head_rows = round_up(heads, 8)
    shares, pair_local = call(
        functools.partial(
            softmax_kernel,
            1.0 / (math.sqrt(head) * math.sqrt(rows * seq_count)),
            heads,
            len(partials),
        ),
        (
            jax.ShapeDtypeStruct((heads * sites, length), BF16),
            jax.ShapeDtypeStruct((pos_count, head_rows + sites, length), F32),
        ),
        [*partials, regression_factors, order],
        smem=(len(partials),),
        scratch=[pltpu.VMEM((head_rows + sites, length), F32)],
    )
    pair_all = lax.all_to_all(pair_local, "pos", split_axis=0, concat_axis=0, tiled=True)

    hidden, normed = call(
        functools.partial(mix_kernel, head, len(value_parts)),
        (
            jax.ShapeDtypeStruct((cells, embed), F32),
            jax.ShapeDtypeStruct((cells, embed), BF16),
        ),
        [
            shares,
            *value_parts,
            lateral_closing_linear,
            skip_stream_input,
            upright_normalizer_multiplier.reshape(1, embed),
        ],
        scratch=[pltpu.VMEM((cells, embed), F32)],
    )
    if swapped:
        normed_all = [normed, lax.ppermute(normed, "seq", swap)]
        weight = upright_threefold_linear
    else:
        normed_all = [normed]
        weight = lax.all_gather(upright_threefold_linear, "seq", axis=1, tiled=True)
    projected = call(
        functools.partial(project_kernel, len(normed_all)),
        jax.ShapeDtypeStruct((cells * len(normed_all), weight.shape[1]), BF16),
        [*normed_all, weight],
    )
    if swapped:
        column_inputs = [scalars, projected, lax.ppermute(projected, "seq", swap)]
    else:
        key_value = lax.all_gather(projected[:, embed:], "seq", axis=0, tiled=True)
        column_inputs = [projected[:, :embed], key_value]
    scratch = [
        pltpu.VMEM((cells * rows * seq_count, embed), F32),
        pltpu.VMEM((cells, embed), F32),
    ]
    if swapped:
        scratch.append(pltpu.VMEM((cells * 2, columns * 2), BF16))
    alignment_output = call(
        functools.partial(column_kernel, head, 1.0 / math.sqrt(head), swapped),
        jax.ShapeDtypeStruct((rows, sites, embed), BF16),
        [*column_inputs, hidden, upright_closing_linear],
        smem=(0,) if swapped else (),
        scratch=scratch,
    )

    factor_column = jnp.zeros((head_rows, 128), F32).at[:heads, :].set(regression_factors[:, None])
    pairing_chances = call(
        functools.partial(contact_kernel, heads),
        jax.ShapeDtypeStruct((sites, slab_width), F32),
        [scalars, pair_all, factor_column, regression_offset, own_select, slab_select],
        smem=(0, 3),
        scratch=[pltpu.VMEM((head_rows + sites, length), F32)],
    )
    return alignment_output, pairing_chances


def solution(mesh):
    cells = P("seq", "pos", None)
    return jax.shard_map(
        per_device,
        mesh=mesh,
        in_specs=(cells, cells, cells, cells, P(), P(), P(None, "seq"), P(), P(), P()),
        out_specs=(cells, P("pos", "seq")),
        check_vma=False,
    )
```

```python
import functools
import math

import jax
import jax.numpy as jnp
import numpy as np
from jax import lax
from jax.experimental import pallas as pl
from jax.experimental.pallas import tpu as pltpu
from jax.sharding import PartitionSpec as P

F32 = jnp.float32
BF16 = jnp.bfloat16
HIGHEST = lax.Precision.HIGHEST
LANE_BLOCK = 256


def dot_nn(a, b, precision=None):
    return lax.dot_general(
        a, b, (((1,), (0,)), ((), ())), precision=precision, preferred_element_type=F32
    )


def dot_nt(a, b, precision=None):
    return lax.dot_general(
        a, b, (((1,), (1,)), ((), ())), precision=precision, preferred_element_type=F32
    )


def round_up(n, m):
    return -(-n // m) * m


def lane_block(embed, head):
    return LANE_BLOCK if embed % LANE_BLOCK == 0 and LANE_BLOCK % head == 0 else head


def arrival_place(index, column, stages, sites):
    block, place, span = column // sites, column % sites, 1
    for stride, size in stages:
        digit = (block // span) % size
        place = place + ((index // stride) % size + size - digit) % size * (stride * sites)
        span *= size
    return place


def prepare_kernel(head, stages, scalar_ref, q_ref, skip_ref, gain_ref, factor_ref, *outs):
    masked_ref, wide_skip_ref, wide_gain_ref, head_ref, order_ref, turn_ref, own_ref, slab_ref = outs
    rows, sites, embed = q_ref.shape
    heads = embed // head
    width = masked_ref.shape[2]
    group = width // head
    span = group * sites
    lane_head = lax.broadcasted_iota(jnp.int32, (span, width), 1) // head
    row_head = lax.broadcasted_iota(jnp.int32, (span, width), 0) // sites
    own_head = lane_head == row_head
    for block in range(embed // width):
        for r in range(rows):
            q = q_ref[r, :, block * width : (block + 1) * width].astype(F32)
            q = jnp.where(own_head, jnp.concatenate([q] * group, axis=0), 0.0).astype(BF16)
            masked_ref[r, block * span : (block + 1) * span, :] = q
    wide_skip_ref[...] = skip_ref[...].astype(F32).reshape(rows * sites, embed)
    wide_gain_ref[...] = jnp.broadcast_to(gain_ref[...], wide_gain_ref.shape)
    row = lax.broadcasted_iota(jnp.int32, head_ref.shape, 0)
    factors = jnp.zeros(head_ref.shape, F32)
    for h in range(heads):
        factors = jnp.where(row == h, factor_ref[h], factors)
    head_ref[...] = factors
    seq_index, pos_index = scalar_ref[0], scalar_ref[1]
    length = order_ref.shape[0]
    row = lax.broadcasted_iota(jnp.int32, (length, length), 0)
    lane = lax.broadcasted_iota(jnp.int32, (length, length), 1)
    order_ref[...] = (arrival_place(pos_index, row, stages, sites) == lane).astype(F32)
    if len(stages) > 1:
        outer, middle = stages[0][1], stages[1][1]
        block, inside = row // sites, row % sites
        first, second, rest = block % outer, (block // outer) % middle, block // (outer * middle)
        turned = (rest * outer * middle + first * middle + second) * sites + inside
    else:
        turned = row
    turn_ref[...] = (turned == lane).astype(BF16)
    row = lax.broadcasted_iota(jnp.int32, own_ref.shape, 0)
    lane = lax.broadcasted_iota(jnp.int32, own_ref.shape, 1)
    own_ref[...] = (row + pos_index * sites == lane).astype(F32)
    row = lax.broadcasted_iota(jnp.int32, slab_ref.shape, 0)
    lane = lax.broadcasted_iota(jnp.int32, slab_ref.shape, 1)
    slab_ref[...] = (row == lane + seq_index * slab_ref.shape[1]).astype(F32)


def logits_kernel(part_count, *refs):
    q_ref, k_refs, done_refs, out_ref = refs[0], refs[1 : 1 + part_count], refs[1 + part_count : -1], refs[-1]
    rows, _, width = q_ref.shape
    blocks = k_refs[0].shape[2] // width
    span = q_ref.shape[1] // blocks
    for block in range(blocks):
        cols = slice(block * width, (block + 1) * width)
        lines = slice(block * span, (block + 1) * span)
        total = None
        for r in range(rows):
            keys = jnp.concatenate([k[r, :, cols] for k in k_refs], axis=0)
            term = dot_nt(q_ref[r, lines, :], keys)
            total = term if total is None else total + term
        out_ref[lines, :] = jnp.concatenate([done[lines, :] for done in done_refs] + [total], axis=1)


def softmax_kernel(factor, *refs):
    parts, (turn_ref, w_ref, turned_ref) = refs[:-3], refs[-3:]
    logits = parts[0][...]
    for part in parts[1:]:
        logits = logits + part[...]
    logits = logits * factor
    exponent = jnp.exp(logits - jnp.max(logits, axis=1, keepdims=True))
    shares = (exponent / jnp.sum(exponent, axis=1, keepdims=True)).astype(BF16)
    w_ref[...] = shares
    turned_ref[...] = dot_nn(shares, turn_ref[...]).astype(BF16)


def pair_kernel(heads, w_ref, head_ref, order_ref, pair_ref, held):
    rows, length = w_ref.shape
    sites = rows // heads
    shares = w_ref[...].astype(F32)
    row_sum = jnp.sum(shares, axis=1, keepdims=True)
    lane = lax.broadcasted_iota(jnp.int32, (rows, length), 1)
    row = lax.broadcasted_iota(jnp.int32, (rows, length), 0) % sites
    both = (shares + jnp.where(lane == row, row_sum, 0.0)).reshape(heads, sites, length)
    head_rows = round_up(heads, 8)
    held[...] = jnp.zeros_like(held)
    held[0:heads, :] = jnp.sum(both, axis=1)
    merged = None
    for h in range(heads):
        term = shares[h * sites : (h + 1) * sites, :] * head_ref[h : h + 1, 0:1]
        merged = term if merged is None else merged + term
    held[head_rows : head_rows + sites, :] = merged
    pair_ref[...] = jnp.broadcast_to(
        dot_nn(held[...], order_ref[...], HIGHEST)[None], pair_ref.shape
    )


def mix_kernel(head, v_count, *refs):
    w_ref, v_refs = refs[0], refs[1 : 1 + v_count]
    closing_ref, skip_ref, gain_ref, hidden_ref, normed_ref, mixed = refs[1 + v_count :]
    rows, _, embed = v_refs[0].shape
    sites = skip_ref.shape[0] // rows
    width = lane_block(embed, head)
    group = width // head
    lane_head = lax.broadcasted_iota(jnp.int32, (sites, width), 1) // head
    for block in range(embed // width):
        cols = slice(block * width, (block + 1) * width)
        shares = w_ref[block * group * sites : (block + 1) * group * sites, :]
        for r in range(rows):
            values = jnp.concatenate([v[r, :, cols] for v in v_refs], axis=0)
            product = dot_nn(shares, values)
            own = product[0:sites, :]
            for g in range(1, group):
                own = jnp.where(lane_head == g, product[g * sites : (g + 1) * sites, :], own)
            mixed[r * sites : (r + 1) * sites, cols] = own
    hidden = skip_ref[...] + dot_nn(mixed[...].astype(BF16), closing_ref[...])
    hidden_ref[...] = hidden
    centered = hidden - jnp.mean(hidden, axis=1, keepdims=True)
    spread = jnp.mean(centered * centered, axis=1, keepdims=True)
    normed_ref[...] = (centered * lax.rsqrt(spread + 1e-05) * gain_ref[0:1, :]).astype(BF16)


def project_kernel(part_count, *refs):
    parts, (weight_ref, out_ref) = refs[:part_count], refs[part_count:]
    normed = jnp.concatenate([part[...] for part in parts], axis=0)
    out_ref[...] = dot_nn(normed, weight_ref[...]).astype(BF16)


def column_kernel(head, factor, swapped, *refs):
    if swapped:
        scalar_ref, own_ref, other_ref = refs[:3]
        full = refs[-1]
        hidden_ref, closing_ref, out_ref, products, mixed = refs[3:-1]
        cells, columns = own_ref.shape
        own_at = pl.multiple_of(scalar_ref[0] * columns, 128)
        other_at = pl.multiple_of((1 - scalar_ref[0]) * columns, 128)
        full[:, pl.ds(own_at, columns)] = own_ref[...]
        full[0 : cells // 2, pl.ds(other_at, columns)] = other_ref[cells // 2 :, :]
        full[cells // 2 :, pl.ds(other_at, columns)] = other_ref[0 : cells // 2, :]
    else:
        query_ref, full = refs[:2]
        hidden_ref, closing_ref, out_ref, products, mixed = refs[2:]
    rows, sites, embed = out_ref.shape
    own_rows = rows * sites
    heads = embed // head
    padded = round_up(heads, 128)
    pick = (
        lax.broadcasted_iota(jnp.int32, (embed, padded), 0) // head
        == lax.broadcasted_iota(jnp.int32, (embed, padded), 1)
    ).astype(BF16)
    spread = (
        lax.broadcasted_iota(jnp.int32, (padded, embed), 1) // head
        == lax.broadcasted_iota(jnp.int32, (padded, embed), 0)
    ).astype(BF16)
    if swapped:
        query = full[0:own_rows, 0:embed].astype(F32)
        key, value = full[:, embed : 2 * embed].astype(F32), full[:, 2 * embed :].astype(F32)
    else:
        query = query_ref[...].astype(F32)
        key, value = full[:, 0:embed].astype(F32), full[:, embed:].astype(F32)
    seqs = key.shape[0] // sites
    keys = [key[t * sites : (t + 1) * sites, :] for t in range(seqs)]
    values = [value[t * sites : (t + 1) * sites, :] for t in range(seqs)]
    for s in range(rows):
        for t in range(seqs):
            at = (s * seqs + t) * sites
            products[at : at + sites, :] = query[s * sites : (s + 1) * sites, :] * keys[t]
    product = products[...]
    high = product.astype(BF16)
    low = (product - high.astype(F32)).astype(BF16)
    scores = (dot_nn(high, pick) + dot_nn(low, pick)) * factor
    exponent = jnp.exp(scores).reshape(rows, seqs, sites, padded)
    shares = (exponent / jnp.sum(exponent, axis=1, keepdims=True)).astype(BF16)
    wide = dot_nn(shares.reshape(rows * seqs * sites, padded), spread)
    for s in range(rows):
        total = None
        for t in range(seqs):
            at = (s * seqs + t) * sites
            term = wide[at : at + sites, :] * values[t]
            total = term if total is None else total + term
        mixed[s * sites : (s + 1) * sites, :] = total
    out = hidden_ref[...] + dot_nn(mixed[...].astype(BF16), closing_ref[...])
    out_ref[...] = out.reshape(rows, sites, embed).astype(BF16)


def contact_kernel(heads, scalar_ref, pair_ref, factor_ref, offset_ref, own_ref, slab_ref, out_ref, held):
    count, step, length = pair_ref.shape
    head_rows = round_up(heads, 8)
    sites = step - head_rows
    blocks = slab_ref.shape[1] // sites
    total = pair_ref[0, 0:head_rows, :]
    for n in range(1, count):
        total = total + pair_ref[n, 0:head_rows, :]
    held[0:head_rows, :] = total
    held[head_rows:step, :] = pair_ref[scalar_ref[1], head_rows:step, :]
    first = scalar_ref[0] * blocks
    table = jnp.concatenate(
        [pair_ref[first + n, head_rows:step, :] for n in range(blocks)], axis=0
    )
    amount = jnp.sum(total, axis=1, keepdims=True)
    real = lax.broadcasted_iota(jnp.int32, (head_rows, 1), 0) < heads
    share = jnp.where(real, factor_ref[:, 0:1] / jnp.where(real, amount, 1.0), 0.0)
    slab = dot_nn(held[...], slab_ref[...], HIGHEST)
    own = dot_nt(own_ref[...], total * share, HIGHEST)
    mirrored = dot_nt(own_ref[...], table, HIGHEST)
    adjuster = dot_nn(own, slab[0:head_rows, :], HIGHEST)
    out_ref[...] = jax.nn.sigmoid(
        slab[head_rows:step, :] + mirrored - adjuster + offset_ref[0]
    )


def call(kernel, out_shape, operands, smem=(), scratch=(), flops=1000000, bytes_accessed=1000000):
    vmem = pl.BlockSpec(memory_space=pltpu.VMEM)
    held = sum(math.prod(a.shape) * a.dtype.itemsize for a in [*operands, *jax.tree.leaves(out_shape)])
    held += sum(math.prod(a.shape) * np.dtype(a.dtype).itemsize for a in scratch)
    limit = 2 * held + 4 * 1024 * 1024
    specs = [
        pl.BlockSpec(memory_space=pltpu.SMEM) if i in smem else vmem for i in range(len(operands))
    ]
    return pl.pallas_call(
        kernel,
        out_shape=out_shape,
        in_specs=specs,
        out_specs=jax.tree.map(lambda _: vmem, out_shape),
        scratch_shapes=list(scratch),
        compiler_params=pltpu.CompilerParams(vmem_limit_bytes=limit),
        cost_estimate=pl.CostEstimate(
            flops=flops, bytes_accessed=bytes_accessed, transcendentals=0
        ),
    )(*operands)


def stages_of(count):
    stages, stride = [], 1
    while count > 1 and len(stages) < 2 and count % 2 == 0:
        stages.append((stride, 2))
        stride, count = stride * 2, count // 2
    if count > 1:
        stages.append((stride, count))
    return stages[::-1]


def send_pos(array, count, stride, size, delta):
    pairs = []
    for p in range(count):
        a = (p // stride) % size
        pairs.append((p, p + ((a + delta) % size - a) * stride))
    return lax.ppermute(array, "pos", pairs)


def send_all(parts, count, stage):
    stride, size = stage
    return [send_pos(part, count, stride, size, delta) for delta in range(1, size) for part in parts]


def after(array, *others):
    return lax.optimization_barrier((array, *others))[0]


def per_device(
    skip_stream_input,
    lateral_asking_vectors,
    lateral_matched_vectors,
    lateral_carried_vectors,
    lateral_closing_linear,
    upright_normalizer_multiplier,
    upright_threefold_linear,
    upright_closing_linear,
    regression_factors,
    regression_offset,
):
    rows, sites, embed = lateral_asking_vectors.shape
    heads = regression_factors.shape[0]
    head = embed // heads
    seq_count = lax.axis_size("seq")
    pos_count = lax.axis_size("pos")
    length = sites * pos_count
    slab_width = length // seq_count
    cells = rows * sites
    pos_index = lax.axis_index("pos").astype(jnp.int32)
    seq_index = lax.axis_index("seq").astype(jnp.int32)
    swap = [(s, 1 - s) for s in range(2)]
    columns = upright_threefold_linear.shape[1]
    swapped = seq_count == 2 and columns % 128 == 0

    stages = stages_of(pos_count)
    outer = stages[0]
    middle = stages[1] if len(stages) > 1 else None

    scalars = jnp.stack([seq_index, pos_index])
    head_rows = round_up(heads, 8)
    width = lane_block(embed, head)
    masked, skip, gain, head_factors, order, turn, own_select, slab_select = call(
        functools.partial(prepare_kernel, head, stages),
        (
            jax.ShapeDtypeStruct((rows, heads * sites, width), BF16),
            jax.ShapeDtypeStruct((cells, embed), F32),
            jax.ShapeDtypeStruct((8, embed), F32),
            jax.ShapeDtypeStruct((head_rows, 128), F32),
            jax.ShapeDtypeStruct((length, length), F32),
            jax.ShapeDtypeStruct((length, length), BF16),
            jax.ShapeDtypeStruct((sites, length), F32),
            jax.ShapeDtypeStruct((length, slab_width), F32),
        ),
        [
            scalars,
            lateral_asking_vectors,
            skip_stream_input,
            upright_normalizer_multiplier.reshape(1, embed),
            regression_factors,
        ],
        smem=(0, 4),
    )

    value_first = [lateral_carried_vectors]
    if middle:
        value_first += send_all(value_first, pos_count, middle)
    key_first = [lateral_matched_vectors]
    key_first += send_all(key_first, pos_count, outer)
    key_first[-1] = after(key_first[-1], value_first[-1], masked)
    key_parts = [jnp.concatenate(key_first, axis=1)]
    if middle:
        key_parts += send_all(key_parts, pos_count, middle)
    value_parts = [after(jnp.concatenate(value_first, axis=1), key_parts[0])]
    value_outer = send_all(value_parts, pos_count, outer)

    near = sum(part.shape[1] for part in key_parts)
    partial = call(
        functools.partial(logits_kernel, len(key_parts)),
        jax.ShapeDtypeStruct((heads * sites, near), F32),
        [masked, *key_parts],
        bytes_accessed=20000000,
    )
    if len(stages) > 2:
        far_parts = send_all(key_parts, pos_count, stages[2])
        partial = call(
            functools.partial(logits_kernel, len(far_parts)),
            jax.ShapeDtypeStruct((heads * sites, length), F32),
            [masked, *far_parts, partial],
        )
    if seq_count == 2:
        partials = [partial, lax.ppermute(partial, "seq", swap)]
    else:
        partials = [lax.psum(partial, "seq")]
    value_parts += [after(part, partials[-1]) for part in value_outer]
    if len(stages) > 2:
        value_parts += send_all(value_parts, pos_count, stages[2])
    shares, shares_turned = call(
        functools.partial(
            softmax_kernel, 1.0 / (math.sqrt(head) * math.sqrt(rows * seq_count))
        ),
        (
            jax.ShapeDtypeStruct((heads * sites, length), BF16),
            jax.ShapeDtypeStruct((heads * sites, length), BF16),
        ),
        [*partials, turn],
    )

    hidden, normed = call(
        functools.partial(mix_kernel, head, len(value_parts)),
        (
            jax.ShapeDtypeStruct((cells, embed), F32),
            jax.ShapeDtypeStruct((cells, embed), BF16),
        ),
        [shares_turned, *value_parts, lateral_closing_linear, skip, gain],
        scratch=[pltpu.VMEM((cells, embed), F32)],
    )
    pair_local = call(
        functools.partial(pair_kernel, heads),
        jax.ShapeDtypeStruct((pos_count, head_rows + sites, length), F32),
        [after(shares, normed), head_factors, order],
        scratch=[pltpu.VMEM((head_rows + sites, length), F32)],
    )
    pair_all = lax.all_to_all(pair_local, "pos", split_axis=0, concat_axis=0, tiled=True)
    pairing_chances = call(
        functools.partial(contact_kernel, heads),
        jax.ShapeDtypeStruct((sites, slab_width), F32),
        [scalars, pair_all, head_factors, regression_offset, own_select, slab_select],
        smem=(0, 3),
        scratch=[pltpu.VMEM((head_rows + sites, length), F32)],
    )
    if swapped:
        normed_all = [normed, lax.ppermute(normed, "seq", swap)]
        weight = upright_threefold_linear
    else:
        normed_all = [normed]
        weight = lax.all_gather(upright_threefold_linear, "seq", axis=1, tiled=True)
    projected = call(
        functools.partial(project_kernel, len(normed_all)),
        jax.ShapeDtypeStruct((cells * len(normed_all), weight.shape[1]), BF16),
        [*normed_all, weight],
    )
    if swapped:
        column_inputs = [scalars, projected, lax.ppermute(projected, "seq", swap)]
    else:
        key_value = lax.all_gather(projected[:, embed:], "seq", axis=0, tiled=True)
        column_inputs = [projected[:, :embed], key_value]
    scratch = [
        pltpu.VMEM((cells * rows * seq_count, embed), F32),
        pltpu.VMEM((cells, embed), F32),
    ]
    if swapped:
        scratch.append(pltpu.VMEM((cells * 2, columns * 2), BF16))
    alignment_output = call(
        functools.partial(column_kernel, head, 1.0 / math.sqrt(head), swapped),
        jax.ShapeDtypeStruct((rows, sites, embed), BF16),
        [*column_inputs, after(hidden, pairing_chances), upright_closing_linear],
        smem=(0,) if swapped else (),
        scratch=scratch,
    )

    return alignment_output, pairing_chances


def solution(mesh):
    cells = P("seq", "pos", None)
    return jax.shard_map(
        per_device,
        mesh=mesh,
        in_specs=(cells, cells, cells, cells, P(), P(), P(None, "seq"), P(), P(), P()),
        out_specs=(cells, P("pos", "seq")),
        check_vma=False,
    )
```

```python
import functools
import math

import jax
import jax.numpy as jnp
import numpy as np
from jax import lax
from jax.experimental import pallas as pl
from jax.experimental.pallas import tpu as pltpu
from jax.sharding import PartitionSpec as P

F32 = jnp.float32
BF16 = jnp.bfloat16
HIGHEST = lax.Precision.HIGHEST
LANE_BLOCK = 256


def dot_nn(a, b, precision=None):
    return lax.dot_general(
        a, b, (((1,), (0,)), ((), ())), precision=precision, preferred_element_type=F32
    )


def dot_nt(a, b, precision=None):
    return lax.dot_general(
        a, b, (((1,), (1,)), ((), ())), precision=precision, preferred_element_type=F32
    )


def round_up(n, m):
    return -(-n // m) * m


def lane_block(embed, head):
    return LANE_BLOCK if embed % LANE_BLOCK == 0 and LANE_BLOCK % head == 0 else head


def arrival_place(index, column, stages, sites):
    block, place, span = column // sites, column % sites, 1
    for stride, size in stages:
        digit = (block // span) % size
        place = place + ((index // stride) % size + size - digit) % size * (stride * sites)
        span *= size
    return place


def fetch(pairs, sems):
    copies = [pltpu.make_async_copy(src, dst, sems.at[i]) for i, (src, dst) in enumerate(pairs)]
    for copy in copies:
        copy.start()
    for copy in copies:
        copy.wait()


def query_kernel(head, q_hbm, masked_ref, q_ref, sems):
    rows, sites, embed = q_ref.shape
    width = masked_ref.shape[2]
    group = width // head
    span = group * sites
    fetch([(q_hbm, q_ref)], sems)
    lane_head = lax.broadcasted_iota(jnp.int32, (span, width), 1) // head
    row_head = lax.broadcasted_iota(jnp.int32, (span, width), 0) // sites
    own_head = lane_head == row_head
    for block in range(embed // width):
        for r in range(rows):
            q = q_ref[r, :, block * width : (block + 1) * width].astype(F32)
            q = jnp.where(own_head, jnp.concatenate([q] * group, axis=0), 0.0).astype(BF16)
            masked_ref[r, block * span : (block + 1) * span, :] = q


def prepare_kernel(heads, stages, scalar_ref, skip_hbm, gain_ref, factor_ref, *refs):
    wide_skip_ref, wide_gain_ref, head_ref, order_ref, own_ref, slab_ref, skip_ref, sems = refs
    _, sites, embed = skip_ref.shape
    copy = pltpu.make_async_copy(skip_hbm, skip_ref, sems.at[0])
    copy.start()
    wide_gain_ref[...] = jnp.broadcast_to(gain_ref[...].reshape(1, embed), wide_gain_ref.shape)
    row = lax.broadcasted_iota(jnp.int32, head_ref.shape, 0)
    factors = jnp.zeros(head_ref.shape, F32)
    for h in range(heads):
        factors = jnp.where(row == h, factor_ref[h], factors)
    head_ref[...] = factors
    seq_index, pos_index = scalar_ref[0], scalar_ref[1]
    length = order_ref.shape[0]
    row = lax.broadcasted_iota(jnp.int32, (length, length), 0)
    lane = lax.broadcasted_iota(jnp.int32, (length, length), 1)
    order_ref[...] = (arrival_place(pos_index, row, stages, sites) == lane).astype(F32)
    row = lax.broadcasted_iota(jnp.int32, own_ref.shape, 0)
    lane = lax.broadcasted_iota(jnp.int32, own_ref.shape, 1)
    own_ref[...] = (row + pos_index * sites == lane).astype(F32)
    row = lax.broadcasted_iota(jnp.int32, slab_ref.shape, 0)
    lane = lax.broadcasted_iota(jnp.int32, slab_ref.shape, 1)
    slab_ref[...] = (row == lane + seq_index * slab_ref.shape[1]).astype(F32)
    copy.wait()
    wide_skip_ref[...] = skip_ref[...].astype(F32).reshape(wide_skip_ref.shape)


def logits_kernel(part_count, *refs):
    q_ref, k_refs, done_refs, out_ref = refs[0], refs[1 : 1 + part_count], refs[1 + part_count : -1], refs[-1]
    rows, _, width = q_ref.shape
    blocks = k_refs[0].shape[2] // width
    span = q_ref.shape[1] // blocks
    for block in range(blocks):
        cols = slice(block * width, (block + 1) * width)
        lines = slice(block * span, (block + 1) * span)
        total = None
        for r in range(rows):
            keys = jnp.concatenate([k[r, :, cols] for k in k_refs], axis=0)
            term = dot_nt(q_ref[r, lines, :], keys)
            total = term if total is None else total + term
        out_ref[lines, :] = jnp.concatenate([done[lines, :] for done in done_refs] + [total], axis=1)


def softmax_kernel(factor, *refs):
    parts, w_ref = refs[:-1], refs[-1]
    logits = parts[0][...]
    for part in parts[1:]:
        logits = logits + part[...]
    logits = logits * factor
    exponent = jnp.exp(logits - jnp.max(logits, axis=1, keepdims=True))
    shares = (exponent / jnp.sum(exponent, axis=1, keepdims=True)).astype(BF16)
    w_ref[...] = shares


def pair_kernel(heads, w_ref, head_ref, order_ref, pair_ref, held):
    rows, length = w_ref.shape
    sites = rows // heads
    shares = w_ref[...].astype(F32)
    row_sum = jnp.sum(shares, axis=1, keepdims=True)
    lane = lax.broadcasted_iota(jnp.int32, (rows, length), 1)
    row = lax.broadcasted_iota(jnp.int32, (rows, length), 0) % sites
    both = (shares + jnp.where(lane == row, row_sum, 0.0)).reshape(heads, sites, length)
    head_rows = round_up(heads, 8)
    held[...] = jnp.zeros_like(held)
    held[0:heads, :] = jnp.sum(both, axis=1)
    merged = None
    for h in range(heads):
        term = shares[h * sites : (h + 1) * sites, :] * head_ref[h : h + 1, 0:1]
        merged = term if merged is None else merged + term
    held[head_rows : head_rows + sites, :] = merged
    pair_ref[...] = jnp.broadcast_to(
        dot_nn(held[...], order_ref[...], HIGHEST)[None], pair_ref.shape
    )


def mix_kernel(head, v_count, *refs):
    w_ref, v_refs = refs[0], refs[1 : 1 + v_count]
    closing_ref, skip_ref, gain_ref, hidden_ref, normed_ref, mixed = refs[1 + v_count :]
    rows, _, embed = v_refs[0].shape
    sites = skip_ref.shape[0] // rows
    width = lane_block(embed, head)
    group = width // head
    lane_head = lax.broadcasted_iota(jnp.int32, (sites, width), 1) // head
    for block in range(embed // width):
        cols = slice(block * width, (block + 1) * width)
        shares = w_ref[block * group * sites : (block + 1) * group * sites, :]
        for r in range(rows):
            values = jnp.concatenate([v[r, :, cols] for v in v_refs], axis=0)
            product = dot_nn(shares, values)
            own = product[0:sites, :]
            for g in range(1, group):
                own = jnp.where(lane_head == g, product[g * sites : (g + 1) * sites, :], own)
            mixed[r * sites : (r + 1) * sites, cols] = own
    hidden = skip_ref[...] + dot_nn(mixed[...].astype(BF16), closing_ref[...])
    hidden_ref[...] = hidden
    centered = hidden - jnp.mean(hidden, axis=1, keepdims=True)
    spread = jnp.mean(centered * centered, axis=1, keepdims=True)
    normed_ref[...] = (centered * lax.rsqrt(spread + 1e-05) * gain_ref[0:1, :]).astype(BF16)


def project_kernel(part_count, *refs):
    parts, (weight_ref, out_ref) = refs[:part_count], refs[part_count:]
    normed = jnp.concatenate([part[...] for part in parts], axis=0)
    out_ref[...] = dot_nn(normed, weight_ref[...]).astype(BF16)


def column_attend(head, factor, query, keys, values, hidden_ref, closing_ref, out_ref, products, mixed):
    rows, sites, embed = out_ref.shape
    padded = round_up(embed // head, 128)
    pick = (
        lax.broadcasted_iota(jnp.int32, (embed, padded), 0) // head
        == lax.broadcasted_iota(jnp.int32, (embed, padded), 1)
    ).astype(BF16)
    spread = (
        lax.broadcasted_iota(jnp.int32, (padded, embed), 1) // head
        == lax.broadcasted_iota(jnp.int32, (padded, embed), 0)
    ).astype(BF16)
    seqs = len(keys)
    for s in range(rows):
        for t in range(seqs):
            at = (s * seqs + t) * sites
            products[at : at + sites, :] = query[s * sites : (s + 1) * sites, :] * keys[t]
    product = products[...]
    high = product.astype(BF16)
    low = (product - high.astype(F32)).astype(BF16)
    scores = (dot_nn(high, pick) + dot_nn(low, pick)) * factor
    exponent = jnp.exp(scores).reshape(rows, seqs, sites, padded)
    shares = (exponent / jnp.sum(exponent, axis=1, keepdims=True)).astype(BF16)
    wide = dot_nn(shares.reshape(rows * seqs * sites, padded), spread)
    for s in range(rows):
        total = None
        for t in range(seqs):
            at = (s * seqs + t) * sites
            term = wide[at : at + sites, :] * values[t]
            total = term if total is None else total + term
        mixed[s * sites : (s + 1) * sites, :] = total
    out = hidden_ref[...] + dot_nn(mixed[...].astype(BF16), closing_ref[...])
    out_ref[...] = out.reshape(rows, sites, embed).astype(BF16)


def column_kernel(head, factor, query_ref, kv_ref, *refs):
    rows, sites, embed = refs[2].shape
    kv = kv_ref[...].astype(F32)
    seqs = kv.shape[0] // sites
    keys = [kv[t * sites : (t + 1) * sites, 0:embed] for t in range(seqs)]
    values = [kv[t * sites : (t + 1) * sites, embed:] for t in range(seqs)]
    column_attend(head, factor, query_ref[...].astype(F32), keys, values, *refs)


def swapped_column_kernel(head, factor, scalar_ref, own_ref, other_ref, *refs):
    rows, sites, embed = refs[2].shape
    cells, columns = own_ref.shape
    half = cells // 2

    def piece(first_is_own, start, stop, at, size):
        found = []
        for block in range(2):
            lo, hi = max(start, block * columns), min(stop, (block + 1) * columns)
            if lo < hi:
                cols = slice(lo - block * columns, hi - block * columns)
                if (block == 0) == first_is_own:
                    found.append(own_ref[at : at + size, cols])
                else:
                    turned = (at + half) % cells
                    found.append(other_ref[turned : turned + size, cols])
        return jnp.concatenate(found, axis=1).astype(F32)

    def attend(first_is_own):
        query = piece(first_is_own, 0, embed, 0, half)
        keys, values = [], []
        for at in (0, half):
            key = piece(first_is_own, embed, 2 * embed, at, half)
            value = piece(first_is_own, 2 * embed, 3 * embed, at, half)
            for t in range(half // sites):
                keys.append(key[t * sites : (t + 1) * sites, :])
                values.append(value[t * sites : (t + 1) * sites, :])
        column_attend(head, factor, query, keys, values, *refs)

    pl.when(scalar_ref[0] == 0)(functools.partial(attend, True))
    pl.when(scalar_ref[0] == 1)(functools.partial(attend, False))


def contact_kernel(heads, scalar_ref, pair_ref, factor_ref, offset_ref, own_ref, slab_ref, out_ref, held):
    count, step, length = pair_ref.shape
    head_rows = round_up(heads, 8)
    sites = step - head_rows
    blocks = slab_ref.shape[1] // sites
    total = pair_ref[0, 0:head_rows, :]
    for n in range(1, count):
        total = total + pair_ref[n, 0:head_rows, :]
    held[0:head_rows, :] = total
    held[head_rows:step, :] = pair_ref[scalar_ref[1], head_rows:step, :]
    first = scalar_ref[0] * blocks
    table = jnp.concatenate(
        [pair_ref[first + n, head_rows:step, :] for n in range(blocks)], axis=0
    )
    amount = jnp.sum(total, axis=1, keepdims=True)
    real = lax.broadcasted_iota(jnp.int32, (head_rows, 1), 0) < heads
    share = jnp.where(real, factor_ref[:, 0:1] / jnp.where(real, amount, 1.0), 0.0)
    slab = dot_nn(held[...], slab_ref[...], HIGHEST)
    own = dot_nt(own_ref[...], total * share, HIGHEST)
    mirrored = dot_nt(own_ref[...], table, HIGHEST)
    adjuster = dot_nn(own, slab[0:head_rows, :], HIGHEST)
    out_ref[...] = jax.nn.sigmoid(
        slab[head_rows:step, :] + mirrored - adjuster + offset_ref[0]
    )


def call(kernel, out_shape, operands, smem=(), hbm=(), scratch=(), bytes_accessed=1000000):
    vmem = pl.BlockSpec(memory_space=pltpu.VMEM)
    held = sum(math.prod(a.shape) * a.dtype.itemsize for a in [*operands, *jax.tree.leaves(out_shape)])
    held += sum(
        math.prod(a.shape) * np.dtype(a.dtype).itemsize
        for a in scratch
        if a.memory_space == pltpu.VMEM
    )
    limit = 2 * held + 4 * 1024 * 1024
    specs = [
        pl.BlockSpec(memory_space=pltpu.SMEM if i in smem else pl.ANY if i in hbm else pltpu.VMEM)
        for i in range(len(operands))
    ]
    return pl.pallas_call(
        kernel,
        out_shape=out_shape,
        in_specs=specs,
        out_specs=jax.tree.map(lambda _: vmem, out_shape),
        scratch_shapes=list(scratch),
        compiler_params=pltpu.CompilerParams(vmem_limit_bytes=limit),
        cost_estimate=pl.CostEstimate(
            flops=1000000, bytes_accessed=bytes_accessed, transcendentals=0
        ),
    )(*operands)


def stages_of(count):
    stages, stride = [], 1
    while count > 1 and len(stages) < 2 and count % 2 == 0:
        stages.append((stride, 2))
        stride, count = stride * 2, count // 2
    if count > 1:
        stages.append((stride, count))
    return stages[::-1]


def send_pos(array, count, stride, size, delta):
    pairs = []
    for p in range(count):
        a = (p // stride) % size
        pairs.append((p, p + ((a + delta) % size - a) * stride))
    return lax.ppermute(array, "pos", pairs)


def send_all(parts, count, stage):
    stride, size = stage
    return [send_pos(part, count, stride, size, delta) for delta in range(1, size) for part in parts]


def after(array, *others):
    return lax.optimization_barrier((array, *others))[0]


def per_device(
    skip_stream_input,
    lateral_asking_vectors,
    lateral_matched_vectors,
    lateral_carried_vectors,
    lateral_closing_linear,
    upright_normalizer_multiplier,
    upright_threefold_linear,
    upright_closing_linear,
    regression_factors,
    regression_offset,
):
    rows, sites, embed = lateral_asking_vectors.shape
    heads = regression_factors.shape[0]
    head = embed // heads
    seq_count = lax.axis_size("seq")
    pos_count = lax.axis_size("pos")
    length = sites * pos_count
    slab_width = length // seq_count
    cells = rows * sites
    pos_index = lax.axis_index("pos").astype(jnp.int32)
    seq_index = lax.axis_index("seq").astype(jnp.int32)
    swap = [(s, 1 - s) for s in range(2)]
    columns = upright_threefold_linear.shape[1]
    swapped = seq_count == 2 and columns % 128 == 0

    stages = stages_of(pos_count)
    outer = stages[0]
    middle = stages[1] if len(stages) > 1 else None

    scalars = jnp.stack([seq_index, pos_index])
    head_rows = round_up(heads, 8)
    width = lane_block(embed, head)
    masked = call(
        functools.partial(query_kernel, head),
        jax.ShapeDtypeStruct((rows, heads * sites, width), BF16),
        [lateral_asking_vectors],
        hbm=(0,),
        scratch=[pltpu.VMEM((rows, sites, embed), BF16), pltpu.SemaphoreType.DMA((1,))],
    )

    key_first = [lateral_matched_vectors]
    key_first += send_all(key_first, pos_count, outer)
    key_first[-1] = after(key_first[-1], masked)
    key_parts = [jnp.concatenate(key_first, axis=1)]
    if middle:
        key_parts += send_all(key_parts, pos_count, middle)
    value_first = [after(lateral_carried_vectors, key_parts[0])]
    value_first += send_all(value_first, pos_count, outer)
    near = sum(part.shape[1] for part in key_parts)
    partial = call(
        functools.partial(logits_kernel, len(key_parts)),
        jax.ShapeDtypeStruct((heads * sites, near), F32),
        [masked, *key_parts],
    )
    value_first = [value_first[0]] + [after(part, partial) for part in value_first[1:]]
    value_parts = [jnp.concatenate(value_first, axis=1)]
    if middle:
        value_parts += send_all(value_parts, pos_count, middle)
    if len(stages) > 2:
        far_parts = send_all(key_parts, pos_count, stages[2])
        partial = call(
            functools.partial(logits_kernel, len(far_parts)),
            jax.ShapeDtypeStruct((heads * sites, length), F32),
            [masked, *far_parts, partial],
        )
    skip, gain, head_factors, order, own_select, slab_select = call(
        functools.partial(prepare_kernel, heads, stages),
        (
            jax.ShapeDtypeStruct((cells, embed), F32),
            jax.ShapeDtypeStruct((8, embed), F32),
            jax.ShapeDtypeStruct((head_rows, 128), F32),
            jax.ShapeDtypeStruct((length, length), F32),
            jax.ShapeDtypeStruct((sites, length), F32),
            jax.ShapeDtypeStruct((length, slab_width), F32),
        ),
        [
            after(scalars, partial),
            skip_stream_input,
            upright_normalizer_multiplier,
            regression_factors,
        ],
        smem=(0, 3),
        hbm=(1,),
        scratch=[pltpu.VMEM((rows, sites, embed), BF16), pltpu.SemaphoreType.DMA((1,))],
    )
    if len(stages) > 2:
        value_parts = value_parts[:1] + [after(part, skip) for part in value_parts[1:]]
        value_parts += send_all(value_parts, pos_count, stages[2])
    if seq_count == 2:
        partials = [partial, after(lax.ppermute(partial, "seq", swap), skip)]
    else:
        partials = [lax.psum(partial, "seq")]
    shares = call(
        functools.partial(
            softmax_kernel, 1.0 / (math.sqrt(head) * math.sqrt(rows * seq_count))
        ),
        jax.ShapeDtypeStruct((heads * sites, length), BF16),
        partials,
    )

    hidden, normed = call(
        functools.partial(mix_kernel, head, len(value_parts)),
        (
            jax.ShapeDtypeStruct((cells, embed), F32),
            jax.ShapeDtypeStruct((cells, embed), BF16),
        ),
        [shares, *value_parts, lateral_closing_linear, skip, gain],
        scratch=[pltpu.VMEM((cells, embed), F32)],
    )
    pair_local = call(
        functools.partial(pair_kernel, heads),
        jax.ShapeDtypeStruct((pos_count, head_rows + sites, length), F32),
        [after(shares, normed), head_factors, order],
        bytes_accessed=10000000,
        scratch=[pltpu.VMEM((head_rows + sites, length), F32)],
    )
    pair_all = lax.all_to_all(pair_local, "pos", split_axis=0, concat_axis=0, tiled=True)
    pairing_chances = call(
        functools.partial(contact_kernel, heads),
        jax.ShapeDtypeStruct((sites, slab_width), F32),
        [scalars, pair_all, head_factors, regression_offset, own_select, slab_select],
        smem=(0, 3),
        scratch=[pltpu.VMEM((head_rows + sites, length), F32)],
    )
    if swapped:
        normed_all = [normed, lax.ppermute(normed, "seq", swap)]
        weight = upright_threefold_linear
    else:
        normed_all = [normed]
        weight = lax.all_gather(upright_threefold_linear, "seq", axis=1, tiled=True)
    projected = call(
        functools.partial(project_kernel, len(normed_all)),
        jax.ShapeDtypeStruct((cells * len(normed_all), weight.shape[1]), BF16),
        [*normed_all, weight],
    )
    if swapped:
        column, column_inputs = swapped_column_kernel, [
            scalars,
            projected,
            lax.ppermute(projected, "seq", swap),
        ]
    else:
        key_value = lax.all_gather(projected[:, embed:], "seq", axis=0, tiled=True)
        column, column_inputs = column_kernel, [projected[:, :embed], key_value]
    alignment_output = call(
        functools.partial(column, head, 1.0 / math.sqrt(head)),
        jax.ShapeDtypeStruct((rows, sites, embed), BF16),
        [*column_inputs, after(hidden, pairing_chances), upright_closing_linear],
        smem=(0,) if swapped else (),
        scratch=[
            pltpu.VMEM((cells * rows * seq_count, embed), F32),
            pltpu.VMEM((cells, embed), F32),
        ],
    )
    return alignment_output, pairing_chances


def solution(mesh):
    cells = P("seq", "pos", None)
    return jax.shard_map(
        per_device,
        mesh=mesh,
        in_specs=(cells, cells, cells, cells, P(), P(), P(None, "seq"), P(), P(), P()),
        out_specs=(cells, P("pos", "seq")),
        check_vma=False,
    )
```

```python
import functools
import math

import jax
import jax.numpy as jnp
import numpy as np
from jax import lax
from jax.experimental import pallas as pl
from jax.experimental.pallas import tpu as pltpu
from jax.sharding import PartitionSpec as P

F32 = jnp.float32
BF16 = jnp.bfloat16
HIGHEST = lax.Precision.HIGHEST
LANE_BLOCK = 256


def dot_nn(a, b, precision=None):
    return lax.dot_general(
        a, b, (((1,), (0,)), ((), ())), precision=precision, preferred_element_type=F32
    )


def dot_nt(a, b, precision=None):
    return lax.dot_general(
        a, b, (((1,), (1,)), ((), ())), precision=precision, preferred_element_type=F32
    )


def round_up(n, m):
    return -(-n // m) * m


def lane_block(embed, head):
    return LANE_BLOCK if embed % LANE_BLOCK == 0 and LANE_BLOCK % head == 0 else head


def arrival_place(index, column, stages, sites):
    block, place, span = column // sites, column % sites, 1
    for stride, size in stages:
        digit = (block // span) % size
        place = place + ((index // stride) % size + size - digit) % size * (stride * sites)
        span *= size
    return place


def fetch(pairs, sems):
    copies = [pltpu.make_async_copy(src, dst, sems.at[i]) for i, (src, dst) in enumerate(pairs)]
    for copy in copies:
        copy.start()
    for copy in copies:
        copy.wait()


def query_kernel(head, q_hbm, masked_ref, q_ref, sems):
    rows, sites, embed = q_ref.shape
    width = masked_ref.shape[2]
    group = width // head
    span = group * sites
    fetch([(q_hbm, q_ref)], sems)
    lane_head = lax.broadcasted_iota(jnp.int32, (span, width), 1) // head
    row_head = lax.broadcasted_iota(jnp.int32, (span, width), 0) // sites
    own_head = lane_head == row_head
    for block in range(embed // width):
        for r in range(rows):
            q = q_ref[r, :, block * width : (block + 1) * width].astype(F32)
            q = jnp.where(own_head, jnp.concatenate([q] * group, axis=0), 0.0).astype(BF16)
            masked_ref[r, block * span : (block + 1) * span, :] = q


def prepare_kernel(heads, stages, scalar_ref, skip_hbm, gain_ref, factor_ref, offset_ref, *refs):
    wide_skip_ref, wide_gain_ref, head_ref, order_ref, own_ref, slab_ref, skip_ref, sems = refs
    _, sites, embed = skip_ref.shape
    copy = pltpu.make_async_copy(skip_hbm, skip_ref, sems.at[0])
    copy.start()
    wide_gain_ref[...] = jnp.broadcast_to(gain_ref[...].reshape(1, embed), wide_gain_ref.shape)
    row = lax.broadcasted_iota(jnp.int32, head_ref.shape, 0)
    factors = jnp.zeros(head_ref.shape, F32)
    for h in range(heads):
        factors = jnp.where(row == h, factor_ref[h], factors)
    head_ref[...] = jnp.where(row == round_up(heads, 8), offset_ref[0], factors)
    seq_index, pos_index = scalar_ref[0], scalar_ref[1]
    length = order_ref.shape[0]
    row = lax.broadcasted_iota(jnp.int32, (length, length), 0)
    lane = lax.broadcasted_iota(jnp.int32, (length, length), 1)
    order_ref[...] = (arrival_place(pos_index, row, stages, sites) == lane).astype(F32)
    row = lax.broadcasted_iota(jnp.int32, own_ref.shape, 0)
    lane = lax.broadcasted_iota(jnp.int32, own_ref.shape, 1)
    own_ref[...] = (row + pos_index * sites == lane).astype(F32)
    row = lax.broadcasted_iota(jnp.int32, slab_ref.shape, 0)
    lane = lax.broadcasted_iota(jnp.int32, slab_ref.shape, 1)
    slab_ref[...] = (row == lane + seq_index * slab_ref.shape[1]).astype(F32)
    copy.wait()
    wide_skip_ref[...] = skip_ref[...].astype(F32).reshape(wide_skip_ref.shape)


def logits_kernel(part_count, *refs):
    q_ref, k_refs, done_refs, out_ref = refs[0], refs[1 : 1 + part_count], refs[1 + part_count : -1], refs[-1]
    rows, _, width = q_ref.shape
    blocks = k_refs[0].shape[2] // width
    span = q_ref.shape[1] // blocks
    for block in range(blocks):
        cols = slice(block * width, (block + 1) * width)
        lines = slice(block * span, (block + 1) * span)
        total = None
        for r in range(rows):
            keys = jnp.concatenate([k[r, :, cols] for k in k_refs], axis=0)
            term = dot_nt(q_ref[r, lines, :], keys)
            total = term if total is None else total + term
        out_ref[lines, :] = jnp.concatenate([done[lines, :] for done in done_refs] + [total], axis=1)


def softmax_kernel(factor, *refs):
    parts, w_ref = refs[:-1], refs[-1]
    logits = parts[0][...]
    for part in parts[1:]:
        logits = logits + part[...]
    logits = logits * factor
    exponent = jnp.exp(logits - jnp.max(logits, axis=1, keepdims=True))
    shares = (exponent / jnp.sum(exponent, axis=1, keepdims=True)).astype(BF16)
    w_ref[...] = shares


def pair_kernel(heads, w_ref, head_ref, order_ref, pair_ref, held):
    rows, length = w_ref.shape
    sites = rows // heads
    shares = w_ref[...].astype(F32)
    row_sum = jnp.sum(shares, axis=1, keepdims=True)
    lane = lax.broadcasted_iota(jnp.int32, (rows, length), 1)
    row = lax.broadcasted_iota(jnp.int32, (rows, length), 0) % sites
    both = (shares + jnp.where(lane == row, row_sum, 0.0)).reshape(heads, sites, length)
    head_rows = round_up(heads, 8)
    held[...] = jnp.zeros_like(held)
    held[0:heads, :] = jnp.sum(both, axis=1)
    merged = None
    for h in range(heads):
        term = shares[h * sites : (h + 1) * sites, :] * head_ref[h : h + 1, 0:1]
        merged = term if merged is None else merged + term
    held[head_rows : head_rows + sites, :] = merged
    pair_ref[...] = jnp.broadcast_to(
        dot_nn(held[...], order_ref[...], HIGHEST)[None], pair_ref.shape
    )


def mix_kernel(head, v_count, *refs):
    w_ref, v_refs = refs[0], refs[1 : 1 + v_count]
    closing_ref, skip_ref, gain_ref, hidden_ref, normed_ref, mixed = refs[1 + v_count :]
    rows, _, embed = v_refs[0].shape
    sites = skip_ref.shape[0] // rows
    width = lane_block(embed, head)
    group = width // head
    lane_head = lax.broadcasted_iota(jnp.int32, (sites, width), 1) // head
    for block in range(embed // width):
        cols = slice(block * width, (block + 1) * width)
        shares = w_ref[block * group * sites : (block + 1) * group * sites, :]
        for r in range(rows):
            values = jnp.concatenate([v[r, :, cols] for v in v_refs], axis=0)
            product = dot_nn(shares, values)
            own = product[0:sites, :]
            for g in range(1, group):
                own = jnp.where(lane_head == g, product[g * sites : (g + 1) * sites, :], own)
            mixed[r * sites : (r + 1) * sites, cols] = own
    hidden = skip_ref[...] + dot_nn(mixed[...].astype(BF16), closing_ref[...])
    hidden_ref[...] = hidden
    centered = hidden - jnp.mean(hidden, axis=1, keepdims=True)
    spread = jnp.mean(centered * centered, axis=1, keepdims=True)
    normed_ref[...] = (centered * lax.rsqrt(spread + 1e-05) * gain_ref[0:1, :]).astype(BF16)


def project_kernel(part_count, *refs):
    parts, (weight_ref, out_ref) = refs[:part_count], refs[part_count:]
    normed = jnp.concatenate([part[...] for part in parts], axis=0)
    out_ref[...] = dot_nn(normed, weight_ref[...]).astype(BF16)


def column_attend(head, factor, query, keys, values, hidden_ref, closing_ref, out_ref, products, mixed):
    rows, sites, embed = out_ref.shape
    padded = round_up(embed // head, 128)
    pick = (
        lax.broadcasted_iota(jnp.int32, (embed, padded), 0) // head
        == lax.broadcasted_iota(jnp.int32, (embed, padded), 1)
    ).astype(BF16)
    spread = (
        lax.broadcasted_iota(jnp.int32, (padded, embed), 1) // head
        == lax.broadcasted_iota(jnp.int32, (padded, embed), 0)
    ).astype(BF16)
    seqs = len(keys)
    for s in range(rows):
        for t in range(seqs):
            at = (s * seqs + t) * sites
            products[at : at + sites, :] = query[s * sites : (s + 1) * sites, :] * keys[t]
    product = products[...]
    high = product.astype(BF16)
    low = (product - high.astype(F32)).astype(BF16)
    scores = (dot_nn(high, pick) + dot_nn(low, pick)) * factor
    exponent = jnp.exp(scores).reshape(rows, seqs, sites, padded)
    shares = (exponent / jnp.sum(exponent, axis=1, keepdims=True)).astype(BF16)
    wide = dot_nn(shares.reshape(rows * seqs * sites, padded), spread)
    for s in range(rows):
        total = None
        for t in range(seqs):
            at = (s * seqs + t) * sites
            term = wide[at : at + sites, :] * values[t]
            total = term if total is None else total + term
        mixed[s * sites : (s + 1) * sites, :] = total
    out = hidden_ref[...] + dot_nn(mixed[...].astype(BF16), closing_ref[...])
    out_ref[...] = out.reshape(rows, sites, embed).astype(BF16)


def column_kernel(head, factor, query_ref, kv_ref, *refs):
    rows, sites, embed = refs[2].shape
    kv = kv_ref[...].astype(F32)
    seqs = kv.shape[0] // sites
    keys = [kv[t * sites : (t + 1) * sites, 0:embed] for t in range(seqs)]
    values = [kv[t * sites : (t + 1) * sites, embed:] for t in range(seqs)]
    column_attend(head, factor, query_ref[...].astype(F32), keys, values, *refs)


def swapped_column_kernel(head, factor, own_ref, other_ref, *refs):
    rows, sites, embed = refs[2].shape
    cells, columns = own_ref.shape
    half = cells // 2

    def piece(first_is_own, start, stop, at, size):
        found = []
        for block in range(2):
            lo, hi = max(start, block * columns), min(stop, (block + 1) * columns)
            if lo < hi:
                cols = slice(lo - block * columns, hi - block * columns)
                if (block == 0) == first_is_own:
                    found.append(own_ref[at : at + size, cols])
                else:
                    turned = (at + half) % cells
                    found.append(other_ref[turned : turned + size, cols])
        return jnp.concatenate(found, axis=1).astype(F32)

    def attend(first_is_own):
        query = piece(first_is_own, 0, embed, 0, half)
        keys, values = [], []
        for at in (0, half):
            key = piece(first_is_own, embed, 2 * embed, at, half)
            value = piece(first_is_own, 2 * embed, 3 * embed, at, half)
            for t in range(half // sites):
                keys.append(key[t * sites : (t + 1) * sites, :])
                values.append(value[t * sites : (t + 1) * sites, :])
        column_attend(head, factor, query, keys, values, *refs)

    seq_index = lax.axis_index("seq")
    pl.when(seq_index == 0)(functools.partial(attend, True))
    pl.when(seq_index == 1)(functools.partial(attend, False))


def contact_kernel(heads, pair_ref, factor_ref, own_ref, slab_ref, out_ref, held):
    count, step, length = pair_ref.shape
    head_rows = round_up(heads, 8)
    sites = step - head_rows
    blocks = slab_ref.shape[1] // sites
    total = pair_ref[0, 0:head_rows, :]
    for n in range(1, count):
        total = total + pair_ref[n, 0:head_rows, :]
    held[0:head_rows, :] = total
    held[head_rows:step, :] = pair_ref[lax.axis_index("pos"), head_rows:step, :]
    first = lax.axis_index("seq") * blocks
    table = jnp.concatenate(
        [pair_ref[first + n, head_rows:step, :] for n in range(blocks)], axis=0
    )
    amount = jnp.sum(total, axis=1, keepdims=True)
    real = lax.broadcasted_iota(jnp.int32, (head_rows, 1), 0) < heads
    share = jnp.where(real, factor_ref[0:head_rows, 0:1] / jnp.where(real, amount, 1.0), 0.0)
    slab = dot_nn(held[...], slab_ref[...], HIGHEST)
    own = dot_nt(own_ref[...], total * share, HIGHEST)
    mirrored = dot_nt(own_ref[...], table, HIGHEST)
    adjuster = dot_nn(own, slab[0:head_rows, :], HIGHEST)
    out_ref[...] = jax.nn.sigmoid(
        slab[head_rows:step, :] + mirrored - adjuster + factor_ref[head_rows : head_rows + 1, 0:1]
    )


def call(kernel, out_shape, operands, smem=(), hbm=(), scratch=(), bytes_accessed=1000000):
    vmem = pl.BlockSpec(memory_space=pltpu.VMEM)
    held = sum(math.prod(a.shape) * a.dtype.itemsize for a in [*operands, *jax.tree.leaves(out_shape)])
    held += sum(
        math.prod(a.shape) * np.dtype(a.dtype).itemsize
        for a in scratch
        if a.memory_space == pltpu.VMEM
    )
    limit = 2 * held + 4 * 1024 * 1024
    specs = [
        pl.BlockSpec(memory_space=pltpu.SMEM if i in smem else pl.ANY if i in hbm else pltpu.VMEM)
        for i in range(len(operands))
    ]
    return pl.pallas_call(
        kernel,
        out_shape=out_shape,
        in_specs=specs,
        out_specs=jax.tree.map(lambda _: vmem, out_shape),
        scratch_shapes=list(scratch),
        compiler_params=pltpu.CompilerParams(vmem_limit_bytes=limit),
        cost_estimate=pl.CostEstimate(
            flops=1000000, bytes_accessed=bytes_accessed, transcendentals=0
        ),
    )(*operands)


def stages_of(count):
    stages, stride = [], 1
    while count > 1 and len(stages) < 2 and count % 2 == 0:
        stages.append((stride, 2))
        stride, count = stride * 2, count // 2
    if count > 1:
        stages.append((stride, count))
    return stages[::-1]


def send_pos(array, count, stride, size, delta):
    pairs = []
    for p in range(count):
        a = (p // stride) % size
        pairs.append((p, p + ((a + delta) % size - a) * stride))
    return lax.ppermute(array, "pos", pairs)


def send_all(parts, count, stage):
    stride, size = stage
    return [send_pos(part, count, stride, size, delta) for delta in range(1, size) for part in parts]


def after(array, *others):
    return lax.optimization_barrier((array, *others))[0]


def per_device(
    skip_stream_input,
    lateral_asking_vectors,
    lateral_matched_vectors,
    lateral_carried_vectors,
    lateral_closing_linear,
    upright_normalizer_multiplier,
    upright_threefold_linear,
    upright_closing_linear,
    regression_factors,
    regression_offset,
):
    rows, sites, embed = lateral_asking_vectors.shape
    heads = regression_factors.shape[0]
    head = embed // heads
    seq_count = lax.axis_size("seq")
    pos_count = lax.axis_size("pos")
    length = sites * pos_count
    slab_width = length // seq_count
    cells = rows * sites
    pos_index = lax.axis_index("pos").astype(jnp.int32)
    seq_index = lax.axis_index("seq").astype(jnp.int32)
    swap = [(s, 1 - s) for s in range(2)]
    columns = upright_threefold_linear.shape[1]
    swapped = seq_count == 2 and columns % 128 == 0

    stages = stages_of(pos_count)
    outer = stages[0]
    middle = stages[1] if len(stages) > 1 else None

    scalars = jnp.stack([seq_index, pos_index])
    head_rows = round_up(heads, 8)
    width = lane_block(embed, head)
    masked = call(
        functools.partial(query_kernel, head),
        jax.ShapeDtypeStruct((rows, heads * sites, width), BF16),
        [lateral_asking_vectors],
        hbm=(0,),
        scratch=[pltpu.VMEM((rows, sites, embed), BF16), pltpu.SemaphoreType.DMA((1,))],
    )

    both = jnp.concatenate([lateral_matched_vectors, lateral_carried_vectors], axis=0)
    arrived = send_all([both], pos_count, outer)
    arrived[-1] = after(arrived[-1], masked)
    key_first = [lateral_matched_vectors] + [part[:rows] for part in arrived]
    key_parts = [jnp.concatenate(key_first, axis=1)]
    if middle:
        key_parts += send_all(key_parts, pos_count, middle)
    arrived[-1] = after(arrived[-1], key_parts[0])
    value_first = [lateral_carried_vectors] + [part[rows:] for part in arrived]
    value_parts = [jnp.concatenate(value_first, axis=1)]
    if middle:
        value_parts += send_all(value_parts, pos_count, middle)
    near = sum(part.shape[1] for part in key_parts)
    partial = call(
        functools.partial(logits_kernel, len(key_parts)),
        jax.ShapeDtypeStruct((heads * sites, near), F32),
        [masked, *key_parts],
    )
    if len(stages) > 2:
        far_parts = send_all(key_parts, pos_count, stages[2])
        partial = call(
            functools.partial(logits_kernel, len(far_parts)),
            jax.ShapeDtypeStruct((heads * sites, length), F32),
            [masked, *far_parts, partial],
        )
    skip, gain, head_factors, order, own_select, slab_select = call(
        functools.partial(prepare_kernel, heads, stages),
        (
            jax.ShapeDtypeStruct((cells, embed), F32),
            jax.ShapeDtypeStruct((8, embed), F32),
            jax.ShapeDtypeStruct((head_rows + 8, 128), F32),
            jax.ShapeDtypeStruct((length, length), F32),
            jax.ShapeDtypeStruct((sites, length), F32),
            jax.ShapeDtypeStruct((length, slab_width), F32),
        ),
        [
            after(scalars, partial),
            skip_stream_input,
            upright_normalizer_multiplier,
            regression_factors,
            regression_offset,
        ],
        smem=(0, 3, 4),
        hbm=(1,),
        scratch=[pltpu.VMEM((rows, sites, embed), BF16), pltpu.SemaphoreType.DMA((1,))],
    )
    if seq_count == 2:
        partials = [partial, after(lax.ppermute(partial, "seq", swap), skip)]
    else:
        partials = [lax.psum(partial, "seq")]
    if len(stages) > 2:
        value_parts = value_parts[:1] + [after(part, partials[-1]) for part in value_parts[1:]]
        value_parts += send_all(value_parts, pos_count, stages[2])
    shares = call(
        functools.partial(
            softmax_kernel, 1.0 / (math.sqrt(head) * math.sqrt(rows * seq_count))
        ),
        jax.ShapeDtypeStruct((heads * sites, length), BF16),
        partials,
    )

    hidden, normed = call(
        functools.partial(mix_kernel, head, len(value_parts)),
        (
            jax.ShapeDtypeStruct((cells, embed), F32),
            jax.ShapeDtypeStruct((cells, embed), BF16),
        ),
        [shares, *value_parts, lateral_closing_linear, skip, gain],
        scratch=[pltpu.VMEM((cells, embed), F32)],
    )
    pair_local = call(
        functools.partial(pair_kernel, heads),
        jax.ShapeDtypeStruct((pos_count, head_rows + sites, length), F32),
        [after(shares, normed), head_factors, order],
        bytes_accessed=10000000,
        scratch=[pltpu.VMEM((head_rows + sites, length), F32)],
    )
    pair_all = lax.all_to_all(pair_local, "pos", split_axis=0, concat_axis=0, tiled=True)
    pairing_chances = call(
        functools.partial(contact_kernel, heads),
        jax.ShapeDtypeStruct((sites, slab_width), F32),
        [pair_all, head_factors, own_select, slab_select],
        scratch=[pltpu.VMEM((head_rows + sites, length), F32)],
    )
    if swapped:
        normed_all = [normed, lax.ppermute(normed, "seq", swap)]
        weight = upright_threefold_linear
    else:
        normed_all = [normed]
        weight = lax.all_gather(upright_threefold_linear, "seq", axis=1, tiled=True)
    projected = call(
        functools.partial(project_kernel, len(normed_all)),
        jax.ShapeDtypeStruct((cells * len(normed_all), weight.shape[1]), BF16),
        [*normed_all, weight],
        bytes_accessed=10000000,
    )
    if swapped:
        column, column_inputs = swapped_column_kernel, [
            projected,
            lax.ppermute(projected, "seq", swap),
        ]
    else:
        key_value = lax.all_gather(projected[:, embed:], "seq", axis=0, tiled=True)
        column, column_inputs = column_kernel, [projected[:, :embed], key_value]
    alignment_output = call(
        functools.partial(column, head, 1.0 / math.sqrt(head)),
        jax.ShapeDtypeStruct((rows, sites, embed), BF16),
        [*column_inputs, after(hidden, pairing_chances), upright_closing_linear],
        scratch=[
            pltpu.VMEM((cells * rows * seq_count, embed), F32),
            pltpu.VMEM((cells, embed), F32),
        ],
    )
    return alignment_output, pairing_chances


def solution(mesh):
    cells = P("seq", "pos", None)
    return jax.shard_map(
        per_device,
        mesh=mesh,
        in_specs=(cells, cells, cells, cells, P(), P(), P(None, "seq"), P(), P(), P()),
        out_specs=(cells, P("pos", "seq")),
        check_vma=False,
    )
```

```python
import functools
import math

import jax
import jax.numpy as jnp
import numpy as np
from jax import lax
from jax.experimental import pallas as pl
from jax.experimental.pallas import tpu as pltpu
from jax.sharding import PartitionSpec as P

F32 = jnp.float32
BF16 = jnp.bfloat16
HIGHEST = lax.Precision.HIGHEST
LANE_BLOCK = 256


def dot_nn(a, b, precision=None):
    return lax.dot_general(
        a, b, (((1,), (0,)), ((), ())), precision=precision, preferred_element_type=F32
    )


def dot_nt(a, b, precision=None):
    return lax.dot_general(
        a, b, (((1,), (1,)), ((), ())), precision=precision, preferred_element_type=F32
    )


def round_up(n, m):
    return -(-n // m) * m


def lane_block(embed, head):
    return LANE_BLOCK if embed % LANE_BLOCK == 0 and LANE_BLOCK % head == 0 else head


def arrival_place(index, column, stages, sites):
    block, place, span = column // sites, column % sites, 1
    for stride, size in stages:
        digit = (block // span) % size
        place = place + ((index // stride) % size + size - digit) % size * (stride * sites)
        span *= size
    return place


def fetch(pairs, sems):
    copies = [pltpu.make_async_copy(src, dst, sems.at[i]) for i, (src, dst) in enumerate(pairs)]
    for copy in copies:
        copy.start()
    for copy in copies:
        copy.wait()


def query_kernel(head, q_hbm, masked_ref, q_ref, sems):
    rows, sites, embed = q_ref.shape
    width = masked_ref.shape[2]
    group = width // head
    span = group * sites
    fetch([(q_hbm, q_ref)], sems)
    lane_head = lax.broadcasted_iota(jnp.int32, (span, width), 1) // head
    row_head = lax.broadcasted_iota(jnp.int32, (span, width), 0) // sites
    own_head = lane_head == row_head
    for block in range(embed // width):
        for r in range(rows):
            q = q_ref[r, :, block * width : (block + 1) * width].astype(F32)
            q = jnp.where(own_head, jnp.concatenate([q] * group, axis=0), 0.0).astype(BF16)
            masked_ref[r, block * span : (block + 1) * span, :] = q


def prepare_kernel(heads, stages, scalar_ref, skip_hbm, gain_ref, factor_ref, offset_ref, *refs):
    wide_skip_ref, wide_gain_ref, head_ref, order_ref, own_ref, slab_ref, skip_ref, sems = refs
    _, sites, embed = skip_ref.shape
    copy = pltpu.make_async_copy(skip_hbm, skip_ref, sems.at[0])
    copy.start()
    wide_gain_ref[...] = jnp.broadcast_to(gain_ref[...].reshape(1, embed), wide_gain_ref.shape)
    row = lax.broadcasted_iota(jnp.int32, head_ref.shape, 0)
    factors = jnp.zeros(head_ref.shape, F32)
    for h in range(heads):
        factors = jnp.where(row == h, factor_ref[h], factors)
    head_ref[...] = jnp.where(row == round_up(heads, 8), offset_ref[0], factors)
    seq_index, pos_index = scalar_ref[0], scalar_ref[1]
    length = order_ref.shape[0]
    row = lax.broadcasted_iota(jnp.int32, (length, length), 0)
    lane = lax.broadcasted_iota(jnp.int32, (length, length), 1)
    order_ref[...] = (arrival_place(pos_index, row, stages, sites) == lane).astype(F32)
    row = lax.broadcasted_iota(jnp.int32, own_ref.shape, 0)
    lane = lax.broadcasted_iota(jnp.int32, own_ref.shape, 1)
    own_ref[...] = (row + pos_index * sites == lane).astype(F32)
    row = lax.broadcasted_iota(jnp.int32, slab_ref.shape, 0)
    lane = lax.broadcasted_iota(jnp.int32, slab_ref.shape, 1)
    slab_ref[...] = (row == lane + seq_index * slab_ref.shape[1]).astype(F32)
    copy.wait()
    wide_skip_ref[...] = skip_ref[...].astype(F32).reshape(wide_skip_ref.shape)


def logits_kernel(part_count, *refs):
    q_ref, k_refs, done_refs, out_ref = refs[0], refs[1 : 1 + part_count], refs[1 + part_count : -1], refs[-1]
    rows, _, width = q_ref.shape
    blocks = k_refs[0].shape[2] // width
    span = q_ref.shape[1] // blocks
    for block in range(blocks):
        cols = slice(block * width, (block + 1) * width)
        lines = slice(block * span, (block + 1) * span)
        total = None
        for r in range(rows):
            keys = jnp.concatenate([k[r, :, cols] for k in k_refs], axis=0)
            term = dot_nt(q_ref[r, lines, :], keys)
            total = term if total is None else total + term
        out_ref[lines, :] = jnp.concatenate([done[lines, :] for done in done_refs] + [total], axis=1)


def softmax_kernel(factor, *refs):
    parts, w_ref = refs[:-1], refs[-1]
    logits = parts[0][...]
    for part in parts[1:]:
        logits = logits + part[...]
    logits = logits * factor
    exponent = jnp.exp(logits - jnp.max(logits, axis=1, keepdims=True))
    shares = (exponent / jnp.sum(exponent, axis=1, keepdims=True)).astype(BF16)
    w_ref[...] = shares


def pair_kernel(heads, w_ref, head_ref, order_ref, pair_ref, held):
    rows, length = w_ref.shape
    sites = rows // heads
    shares = w_ref[...].astype(F32)
    row_sum = jnp.sum(shares, axis=1, keepdims=True)
    lane = lax.broadcasted_iota(jnp.int32, (rows, length), 1)
    row = lax.broadcasted_iota(jnp.int32, (rows, length), 0) % sites
    both = (shares + jnp.where(lane == row, row_sum, 0.0)).reshape(heads, sites, length)
    head_rows = round_up(heads, 8)
    held[...] = jnp.zeros_like(held)
    held[0:heads, :] = jnp.sum(both, axis=1)
    merged = None
    for h in range(heads):
        term = shares[h * sites : (h + 1) * sites, :] * head_ref[h : h + 1, 0:1]
        merged = term if merged is None else merged + term
    held[head_rows : head_rows + sites, :] = merged
    pair_ref[...] = jnp.broadcast_to(
        dot_nn(held[...], order_ref[...], HIGHEST)[None], pair_ref.shape
    )


def mix_kernel(head, v_count, *refs):
    w_ref, v_refs = refs[0], refs[1 : 1 + v_count]
    closing_ref, skip_ref, gain_ref, hidden_ref, normed_ref, mixed = refs[1 + v_count :]
    rows, _, embed = v_refs[0].shape
    sites = skip_ref.shape[0] // rows
    width = lane_block(embed, head)
    group = width // head
    lane_head = lax.broadcasted_iota(jnp.int32, (sites, width), 1) // head
    for block in range(embed // width):
        cols = slice(block * width, (block + 1) * width)
        shares = w_ref[block * group * sites : (block + 1) * group * sites, :]
        for r in range(rows):
            values = jnp.concatenate([v[r, :, cols] for v in v_refs], axis=0)
            product = dot_nn(shares, values)
            own = product[0:sites, :]
            for g in range(1, group):
                own = jnp.where(lane_head == g, product[g * sites : (g + 1) * sites, :], own)
            mixed[r * sites : (r + 1) * sites, cols] = own
    hidden = skip_ref[...] + dot_nn(mixed[...].astype(BF16), closing_ref[...])
    hidden_ref[...] = hidden
    centered = hidden - jnp.mean(hidden, axis=1, keepdims=True)
    spread = jnp.mean(centered * centered, axis=1, keepdims=True)
    normed_ref[...] = (centered * lax.rsqrt(spread + 1e-05) * gain_ref[0:1, :]).astype(BF16)


def project_kernel(part_count, *refs):
    parts, (weight_ref, out_ref) = refs[:part_count], refs[part_count:]
    normed = jnp.concatenate([part[...] for part in parts], axis=0)
    out_ref[...] = dot_nn(normed, weight_ref[...]).astype(BF16)


def column_attend(head, factor, query, keys, values, hidden_ref, closing_ref, out_ref, products, mixed):
    rows, sites, embed = out_ref.shape
    padded = round_up(embed // head, 128)
    pick = (
        lax.broadcasted_iota(jnp.int32, (embed, padded), 0) // head
        == lax.broadcasted_iota(jnp.int32, (embed, padded), 1)
    ).astype(BF16)
    spread = (
        lax.broadcasted_iota(jnp.int32, (padded, embed), 1) // head
        == lax.broadcasted_iota(jnp.int32, (padded, embed), 0)
    ).astype(BF16)
    seqs = len(keys)
    for s in range(rows):
        for t in range(seqs):
            at = (s * seqs + t) * sites
            products[at : at + sites, :] = query[s * sites : (s + 1) * sites, :] * keys[t]
    product = products[...]
    high = product.astype(BF16)
    low = (product - high.astype(F32)).astype(BF16)
    scores = (dot_nn(high, pick) + dot_nn(low, pick)) * factor
    exponent = jnp.exp(scores).reshape(rows, seqs, sites, padded)
    shares = (exponent / jnp.sum(exponent, axis=1, keepdims=True)).astype(BF16)
    wide = dot_nn(shares.reshape(rows * seqs * sites, padded), spread)
    for s in range(rows):
        total = None
        for t in range(seqs):
            at = (s * seqs + t) * sites
            term = wide[at : at + sites, :] * values[t]
            total = term if total is None else total + term
        mixed[s * sites : (s + 1) * sites, :] = total
    out = hidden_ref[...] + dot_nn(mixed[...].astype(BF16), closing_ref[...])
    out_ref[...] = out.reshape(rows, sites, embed).astype(BF16)


def column_kernel(head, factor, query_ref, kv_ref, *refs):
    rows, sites, embed = refs[2].shape
    kv = kv_ref[...].astype(F32)
    seqs = kv.shape[0] // sites
    keys = [kv[t * sites : (t + 1) * sites, 0:embed] for t in range(seqs)]
    values = [kv[t * sites : (t + 1) * sites, embed:] for t in range(seqs)]
    column_attend(head, factor, query_ref[...].astype(F32), keys, values, *refs)


def swapped_column_kernel(head, factor, own_ref, other_ref, *refs):
    rows, sites, embed = refs[2].shape
    cells, columns = own_ref.shape
    half = cells // 2

    def piece(first_is_own, start, stop, at, size):
        found = []
        for block in range(2):
            lo, hi = max(start, block * columns), min(stop, (block + 1) * columns)
            if lo < hi:
                cols = slice(lo - block * columns, hi - block * columns)
                if (block == 0) == first_is_own:
                    found.append(own_ref[at : at + size, cols])
                else:
                    turned = (at + half) % cells
                    found.append(other_ref[turned : turned + size, cols])
        return jnp.concatenate(found, axis=1).astype(F32)

    def attend(first_is_own):
        query = piece(first_is_own, 0, embed, 0, half)
        keys, values = [], []
        for at in (0, half):
            key = piece(first_is_own, embed, 2 * embed, at, half)
            value = piece(first_is_own, 2 * embed, 3 * embed, at, half)
            for t in range(half // sites):
                keys.append(key[t * sites : (t + 1) * sites, :])
                values.append(value[t * sites : (t + 1) * sites, :])
        column_attend(head, factor, query, keys, values, *refs)

    seq_index = lax.axis_index("seq")
    pl.when(seq_index == 0)(functools.partial(attend, True))
    pl.when(seq_index == 1)(functools.partial(attend, False))


def contact_kernel(heads, pair_ref, factor_ref, own_ref, slab_ref, out_ref, held):
    count, step, length = pair_ref.shape
    head_rows = round_up(heads, 8)
    sites = step - head_rows
    blocks = slab_ref.shape[1] // sites
    total = pair_ref[0, 0:head_rows, :]
    for n in range(1, count):
        total = total + pair_ref[n, 0:head_rows, :]
    held[0:head_rows, :] = total
    held[head_rows:step, :] = pair_ref[lax.axis_index("pos"), head_rows:step, :]
    first = lax.axis_index("seq") * blocks
    table = jnp.concatenate(
        [pair_ref[first + n, head_rows:step, :] for n in range(blocks)], axis=0
    )
    amount = jnp.sum(total, axis=1, keepdims=True)
    real = lax.broadcasted_iota(jnp.int32, (head_rows, 1), 0) < heads
    share = jnp.where(real, factor_ref[0:head_rows, 0:1] / jnp.where(real, amount, 1.0), 0.0)
    slab = dot_nn(held[...], slab_ref[...], HIGHEST)
    own = dot_nt(own_ref[...], total * share, HIGHEST)
    mirrored = dot_nt(own_ref[...], table, HIGHEST)
    adjuster = dot_nn(own, slab[0:head_rows, :], HIGHEST)
    out_ref[...] = jax.nn.sigmoid(
        slab[head_rows:step, :] + mirrored - adjuster + factor_ref[head_rows : head_rows + 1, 0:1]
    )


def call(kernel, out_shape, operands, smem=(), hbm=(), scratch=(), bytes_accessed=1000000):
    vmem = pl.BlockSpec(memory_space=pltpu.VMEM)
    held = sum(math.prod(a.shape) * a.dtype.itemsize for a in [*operands, *jax.tree.leaves(out_shape)])
    held += sum(
        math.prod(a.shape) * np.dtype(a.dtype).itemsize
        for a in scratch
        if a.memory_space == pltpu.VMEM
    )
    limit = 2 * held + 4 * 1024 * 1024
    specs = [
        pl.BlockSpec(memory_space=pltpu.SMEM if i in smem else pl.ANY if i in hbm else pltpu.VMEM)
        for i in range(len(operands))
    ]
    return pl.pallas_call(
        kernel,
        out_shape=out_shape,
        in_specs=specs,
        out_specs=jax.tree.map(lambda _: vmem, out_shape),
        scratch_shapes=list(scratch),
        compiler_params=pltpu.CompilerParams(vmem_limit_bytes=limit),
        cost_estimate=pl.CostEstimate(
            flops=1000000, bytes_accessed=bytes_accessed, transcendentals=0
        ),
    )(*operands)


def stages_of(count):
    stages, stride = [], 1
    while count > 1 and len(stages) < 2 and count % 2 == 0:
        stages.append((stride, 2))
        stride, count = stride * 2, count // 2
    if count > 1:
        stages.append((stride, count))
    return stages[::-1]


def send_pos(array, count, stride, size, delta):
    pairs = []
    for p in range(count):
        a = (p // stride) % size
        pairs.append((p, p + ((a + delta) % size - a) * stride))
    return lax.ppermute(array, "pos", pairs)


def send_all(parts, count, stage):
    stride, size = stage
    return [send_pos(part, count, stride, size, delta) for delta in range(1, size) for part in parts]


def after(array, *others):
    return lax.optimization_barrier((array, *others))[0]


def per_device(
    skip_stream_input,
    lateral_asking_vectors,
    lateral_matched_vectors,
    lateral_carried_vectors,
    lateral_closing_linear,
    upright_normalizer_multiplier,
    upright_threefold_linear,
    upright_closing_linear,
    regression_factors,
    regression_offset,
):
    rows, sites, embed = lateral_asking_vectors.shape
    heads = regression_factors.shape[0]
    head = embed // heads
    seq_count = lax.axis_size("seq")
    pos_count = lax.axis_size("pos")
    length = sites * pos_count
    slab_width = length // seq_count
    cells = rows * sites
    pos_index = lax.axis_index("pos").astype(jnp.int32)
    seq_index = lax.axis_index("seq").astype(jnp.int32)
    swap = [(s, 1 - s) for s in range(2)]
    columns = upright_threefold_linear.shape[1]
    swapped = seq_count == 2 and columns % 128 == 0

    stages = stages_of(pos_count)
    outer = stages[0]
    middle = stages[1] if len(stages) > 1 else None

    scalars = jnp.stack([seq_index, pos_index])
    head_rows = round_up(heads, 8)
    width = lane_block(embed, head)
    value_first = [lateral_carried_vectors] + send_all([lateral_carried_vectors], pos_count, outer)
    key_first = [lateral_matched_vectors] + send_all([lateral_matched_vectors], pos_count, outer)
    key_parts = [jnp.concatenate(key_first, axis=1)]
    masked = call(
        functools.partial(query_kernel, head),
        jax.ShapeDtypeStruct((rows, heads * sites, width), BF16),
        [after(lateral_asking_vectors, key_parts[0])],
        hbm=(0,),
        scratch=[pltpu.VMEM((rows, sites, embed), BF16), pltpu.SemaphoreType.DMA((1,))],
    )
    if middle:
        key_parts += send_all(key_parts, pos_count, middle)
    near = sum(part.shape[1] for part in key_parts)
    partial = call(
        functools.partial(logits_kernel, len(key_parts)),
        jax.ShapeDtypeStruct((heads * sites, near), F32),
        [masked, *key_parts],
    )
    value_first[1] = after(value_first[1], masked)
    value_parts = [jnp.concatenate(value_first, axis=1)]
    if middle:
        value_parts += send_all(value_parts, pos_count, middle)
    if len(stages) > 2:
        far_parts = send_all(key_parts, pos_count, stages[2])
        partial = call(
            functools.partial(logits_kernel, len(far_parts)),
            jax.ShapeDtypeStruct((heads * sites, length), F32),
            [masked, *far_parts, partial],
        )
    skip, gain, head_factors, order, own_select, slab_select = call(
        functools.partial(prepare_kernel, heads, stages),
        (
            jax.ShapeDtypeStruct((cells, embed), F32),
            jax.ShapeDtypeStruct((8, embed), F32),
            jax.ShapeDtypeStruct((head_rows + 8, 128), F32),
            jax.ShapeDtypeStruct((length, length), F32),
            jax.ShapeDtypeStruct((sites, length), F32),
            jax.ShapeDtypeStruct((length, slab_width), F32),
        ),
        [
            after(scalars, partial),
            skip_stream_input,
            upright_normalizer_multiplier,
            regression_factors,
            regression_offset,
        ],
        smem=(0, 3, 4),
        hbm=(1,),
        scratch=[pltpu.VMEM((rows, sites, embed), BF16), pltpu.SemaphoreType.DMA((1,))],
    )
    if seq_count == 2:
        partials = [partial, after(lax.ppermute(partial, "seq", swap), skip)]
    else:
        partials = [lax.psum(partial, "seq")]
    if len(stages) > 2:
        value_parts = value_parts[:1] + [after(part, partials[-1]) for part in value_parts[1:]]
        value_parts += send_all(value_parts, pos_count, stages[2])
    shares = call(
        functools.partial(
            softmax_kernel, 1.0 / (math.sqrt(head) * math.sqrt(rows * seq_count))
        ),
        jax.ShapeDtypeStruct((heads * sites, length), BF16),
        partials,
    )

    hidden, normed = call(
        functools.partial(mix_kernel, head, len(value_parts)),
        (
            jax.ShapeDtypeStruct((cells, embed), F32),
            jax.ShapeDtypeStruct((cells, embed), BF16),
        ),
        [shares, *value_parts, lateral_closing_linear, skip, gain],
        scratch=[pltpu.VMEM((cells, embed), F32)],
    )
    pair_local = call(
        functools.partial(pair_kernel, heads),
        jax.ShapeDtypeStruct((pos_count, head_rows + sites, length), F32),
        [after(shares, normed), head_factors, order],
        bytes_accessed=10000000,
        scratch=[pltpu.VMEM((head_rows + sites, length), F32)],
    )
    pair_all = lax.all_to_all(pair_local, "pos", split_axis=0, concat_axis=0, tiled=True)
    pairing_chances = call(
        functools.partial(contact_kernel, heads),
        jax.ShapeDtypeStruct((sites, slab_width), F32),
        [pair_all, head_factors, own_select, slab_select],
        scratch=[pltpu.VMEM((head_rows + sites, length), F32)],
    )
    if swapped:
        normed_all = [normed, lax.ppermute(normed, "seq", swap)]
        weight = upright_threefold_linear
    else:
        normed_all = [normed]
        weight = lax.all_gather(upright_threefold_linear, "seq", axis=1, tiled=True)
    projected = call(
        functools.partial(project_kernel, len(normed_all)),
        jax.ShapeDtypeStruct((cells * len(normed_all), weight.shape[1]), BF16),
        [*normed_all, weight],
        bytes_accessed=10000000,
    )
    if swapped:
        column, column_inputs = swapped_column_kernel, [
            projected,
            lax.ppermute(projected, "seq", swap),
        ]
    else:
        key_value = lax.all_gather(projected[:, embed:], "seq", axis=0, tiled=True)
        column, column_inputs = column_kernel, [projected[:, :embed], key_value]
    alignment_output = call(
        functools.partial(column, head, 1.0 / math.sqrt(head)),
        jax.ShapeDtypeStruct((rows, sites, embed), BF16),
        [*column_inputs, after(hidden, pairing_chances), upright_closing_linear],
        scratch=[
            pltpu.VMEM((cells * rows * seq_count, embed), F32),
            pltpu.VMEM((cells, embed), F32),
        ],
    )
    return alignment_output, pairing_chances


def solution(mesh):
    cells = P("seq", "pos", None)
    return jax.shard_map(
        per_device,
        mesh=mesh,
        in_specs=(cells, cells, cells, cells, P(), P(), P(None, "seq"), P(), P(), P()),
        out_specs=(cells, P("pos", "seq")),
        check_vma=False,
    )
```

```python
import functools
import math

import jax
import jax.numpy as jnp
import numpy as np
from jax import lax
from jax.experimental import pallas as pl
from jax.experimental.pallas import tpu as pltpu
from jax.sharding import PartitionSpec as P

F32 = jnp.float32
BF16 = jnp.bfloat16
HIGHEST = lax.Precision.HIGHEST
LANE_BLOCK = 256


def dot_nn(a, b, precision=None):
    return lax.dot_general(
        a, b, (((1,), (0,)), ((), ())), precision=precision, preferred_element_type=F32
    )


def dot_nt(a, b, precision=None):
    return lax.dot_general(
        a, b, (((1,), (1,)), ((), ())), precision=precision, preferred_element_type=F32
    )


def round_up(n, m):
    return -(-n // m) * m


def lane_block(embed, head):
    return LANE_BLOCK if embed % LANE_BLOCK == 0 and LANE_BLOCK % head == 0 else head


def arrival_place(index, column, stages, sites):
    block, place, span = column // sites, column % sites, 1
    for stride, size in stages:
        digit = (block // span) % size
        place = place + ((index // stride) % size + size - digit) % size * (stride * sites)
        span *= size
    return place


def fetch(pairs, sems):
    copies = [pltpu.make_async_copy(src, dst, sems.at[i]) for i, (src, dst) in enumerate(pairs)]
    for copy in copies:
        copy.start()
    for copy in copies:
        copy.wait()


def query_kernel(head, q_hbm, masked_ref, q_ref, sems):
    rows, sites, embed = q_ref.shape
    width = masked_ref.shape[2]
    group = width // head
    span = group * sites
    fetch([(q_hbm, q_ref)], sems)
    lane_head = lax.broadcasted_iota(jnp.int32, (span, width), 1) // head
    row_head = lax.broadcasted_iota(jnp.int32, (span, width), 0) // sites
    own_head = lane_head == row_head
    for block in range(embed // width):
        for r in range(rows):
            q = q_ref[r, :, block * width : (block + 1) * width].astype(F32)
            q = jnp.where(own_head, jnp.concatenate([q] * group, axis=0), 0.0).astype(BF16)
            masked_ref[r, block * span : (block + 1) * span, :] = q


def prepare_kernel(heads, stages, scalar_ref, skip_hbm, gain_ref, factor_ref, offset_ref, *refs):
    wide_skip_ref, wide_gain_ref, head_ref, order_ref, own_ref, slab_ref, skip_ref, sems = refs
    _, sites, embed = skip_ref.shape
    copy = pltpu.make_async_copy(skip_hbm, skip_ref, sems.at[0])
    copy.start()
    wide_gain_ref[...] = jnp.broadcast_to(gain_ref[...].reshape(1, embed), wide_gain_ref.shape)
    row = lax.broadcasted_iota(jnp.int32, head_ref.shape, 0)
    factors = jnp.zeros(head_ref.shape, F32)
    for h in range(heads):
        factors = jnp.where(row == h, factor_ref[h], factors)
    head_ref[...] = jnp.where(row == round_up(heads, 8), offset_ref[0], factors)
    seq_index, pos_index = scalar_ref[0], scalar_ref[1]
    length = order_ref.shape[0]
    row = lax.broadcasted_iota(jnp.int32, (length, length), 0)
    lane = lax.broadcasted_iota(jnp.int32, (length, length), 1)
    order_ref[...] = (arrival_place(pos_index, row, stages, sites) == lane).astype(F32)
    row = lax.broadcasted_iota(jnp.int32, own_ref.shape, 0)
    lane = lax.broadcasted_iota(jnp.int32, own_ref.shape, 1)
    own_ref[...] = (row + pos_index * sites == lane).astype(F32)
    row = lax.broadcasted_iota(jnp.int32, slab_ref.shape, 0)
    lane = lax.broadcasted_iota(jnp.int32, slab_ref.shape, 1)
    slab_ref[...] = (row == lane + seq_index * slab_ref.shape[1]).astype(F32)
    copy.wait()
    wide_skip_ref[...] = skip_ref[...].astype(F32).reshape(wide_skip_ref.shape)


def logits_kernel(part_count, *refs):
    q_ref, k_refs, done_refs, out_ref = refs[0], refs[1 : 1 + part_count], refs[1 + part_count : -1], refs[-1]
    rows, _, width = q_ref.shape
    blocks = k_refs[0].shape[2] // width
    span = q_ref.shape[1] // blocks
    for block in range(blocks):
        cols = slice(block * width, (block + 1) * width)
        lines = slice(block * span, (block + 1) * span)
        total = None
        for r in range(rows):
            keys = jnp.concatenate([k[r, :, cols] for k in k_refs], axis=0)
            term = dot_nt(q_ref[r, lines, :], keys)
            total = term if total is None else total + term
        out_ref[lines, :] = jnp.concatenate([done[lines, :] for done in done_refs] + [total], axis=1)


def softmax_kernel(factor, *refs):
    parts, w_ref = refs[:-1], refs[-1]
    logits = parts[0][...]
    for part in parts[1:]:
        logits = logits + part[...]
    logits = logits * factor
    exponent = jnp.exp(logits - jnp.max(logits, axis=1, keepdims=True))
    shares = (exponent / jnp.sum(exponent, axis=1, keepdims=True)).astype(BF16)
    w_ref[...] = shares


def pair_kernel(heads, w_ref, head_ref, order_ref, pair_ref, held):
    rows, length = w_ref.shape
    sites = rows // heads
    shares = w_ref[...].astype(F32)
    row_sum = jnp.sum(shares, axis=1, keepdims=True)
    lane = lax.broadcasted_iota(jnp.int32, (rows, length), 1)
    row = lax.broadcasted_iota(jnp.int32, (rows, length), 0) % sites
    both = (shares + jnp.where(lane == row, row_sum, 0.0)).reshape(heads, sites, length)
    head_rows = round_up(heads, 8)
    held[...] = jnp.zeros_like(held)
    held[0:heads, :] = jnp.sum(both, axis=1)
    merged = None
    for h in range(heads):
        term = shares[h * sites : (h + 1) * sites, :] * head_ref[h : h + 1, 0:1]
        merged = term if merged is None else merged + term
    held[head_rows : head_rows + sites, :] = merged
    pair_ref[...] = jnp.broadcast_to(
        dot_nn(held[...], order_ref[...], HIGHEST)[None], pair_ref.shape
    )


def mix_kernel(head, v_count, *refs):
    w_ref, v_refs = refs[0], refs[1 : 1 + v_count]
    closing_ref, skip_ref, gain_ref, hidden_ref, normed_ref, mixed = refs[1 + v_count :]
    rows, _, embed = v_refs[0].shape
    sites = skip_ref.shape[0] // rows
    width = lane_block(embed, head)
    group = width // head
    lane_head = lax.broadcasted_iota(jnp.int32, (sites, width), 1) // head
    for block in range(embed // width):
        cols = slice(block * width, (block + 1) * width)
        shares = w_ref[block * group * sites : (block + 1) * group * sites, :]
        for r in range(rows):
            values = jnp.concatenate([v[r, :, cols] for v in v_refs], axis=0)
            product = dot_nn(shares, values)
            own = product[0:sites, :]
            for g in range(1, group):
                own = jnp.where(lane_head == g, product[g * sites : (g + 1) * sites, :], own)
            mixed[r * sites : (r + 1) * sites, cols] = own
    hidden = skip_ref[...] + dot_nn(mixed[...].astype(BF16), closing_ref[...])
    hidden_ref[...] = hidden
    centered = hidden - jnp.mean(hidden, axis=1, keepdims=True)
    spread = jnp.mean(centered * centered, axis=1, keepdims=True)
    normed_ref[...] = (centered * lax.rsqrt(spread + 1e-05) * gain_ref[0:1, :]).astype(BF16)


def project_kernel(part_count, *refs):
    parts, (weight_ref, out_ref) = refs[:part_count], refs[part_count:]
    normed = jnp.concatenate([part[...] for part in parts], axis=0)
    out_ref[...] = dot_nn(normed, weight_ref[...]).astype(BF16)


def column_attend(head, factor, query, keys, values, hidden_ref, closing_ref, out_ref, products, mixed):
    rows, sites, embed = out_ref.shape
    padded = round_up(embed // head, 128)
    pick = (
        lax.broadcasted_iota(jnp.int32, (embed, padded), 0) // head
        == lax.broadcasted_iota(jnp.int32, (embed, padded), 1)
    ).astype(BF16)
    spread = (
        lax.broadcasted_iota(jnp.int32, (padded, embed), 1) // head
        == lax.broadcasted_iota(jnp.int32, (padded, embed), 0)
    ).astype(BF16)
    seqs = len(keys)
    for s in range(rows):
        for t in range(seqs):
            at = (s * seqs + t) * sites
            products[at : at + sites, :] = query[s * sites : (s + 1) * sites, :] * keys[t]
    product = products[...]
    high = product.astype(BF16)
    low = (product - high.astype(F32)).astype(BF16)
    scores = (dot_nn(high, pick) + dot_nn(low, pick)) * factor
    exponent = jnp.exp(scores).reshape(rows, seqs, sites, padded)
    shares = (exponent / jnp.sum(exponent, axis=1, keepdims=True)).astype(BF16)
    wide = dot_nn(shares.reshape(rows * seqs * sites, padded), spread)
    for s in range(rows):
        total = None
        for t in range(seqs):
            at = (s * seqs + t) * sites
            term = wide[at : at + sites, :] * values[t]
            total = term if total is None else total + term
        mixed[s * sites : (s + 1) * sites, :] = total
    out = hidden_ref[...] + dot_nn(mixed[...].astype(BF16), closing_ref[...])
    out_ref[...] = out.reshape(rows, sites, embed).astype(BF16)


def column_kernel(head, factor, query_ref, kv_ref, *refs):
    rows, sites, embed = refs[2].shape
    kv = kv_ref[...].astype(F32)
    seqs = kv.shape[0] // sites
    keys = [kv[t * sites : (t + 1) * sites, 0:embed] for t in range(seqs)]
    values = [kv[t * sites : (t + 1) * sites, embed:] for t in range(seqs)]
    column_attend(head, factor, query_ref[...].astype(F32), keys, values, *refs)


def swapped_column_kernel(head, factor, own_ref, other_ref, *refs):
    rows, sites, embed = refs[2].shape
    cells, columns = own_ref.shape
    half = cells // 2

    def piece(first_is_own, start, stop, at, size):
        found = []
        for block in range(2):
            lo, hi = max(start, block * columns), min(stop, (block + 1) * columns)
            if lo < hi:
                cols = slice(lo - block * columns, hi - block * columns)
                if (block == 0) == first_is_own:
                    found.append(own_ref[at : at + size, cols])
                else:
                    turned = (at + half) % cells
                    found.append(other_ref[turned : turned + size, cols])
        return jnp.concatenate(found, axis=1).astype(F32)

    def attend(first_is_own):
        query = piece(first_is_own, 0, embed, 0, half)
        keys, values = [], []
        for at in (0, half):
            key = piece(first_is_own, embed, 2 * embed, at, half)
            value = piece(first_is_own, 2 * embed, 3 * embed, at, half)
            for t in range(half // sites):
                keys.append(key[t * sites : (t + 1) * sites, :])
                values.append(value[t * sites : (t + 1) * sites, :])
        column_attend(head, factor, query, keys, values, *refs)

    seq_index = lax.axis_index("seq")
    pl.when(seq_index == 0)(functools.partial(attend, True))
    pl.when(seq_index == 1)(functools.partial(attend, False))


def contact_kernel(heads, pair_ref, factor_ref, own_ref, slab_ref, out_ref, held):
    count, step, length = pair_ref.shape
    head_rows = round_up(heads, 8)
    sites = step - head_rows
    blocks = slab_ref.shape[1] // sites
    total = pair_ref[0, 0:head_rows, :]
    for n in range(1, count):
        total = total + pair_ref[n, 0:head_rows, :]
    held[0:head_rows, :] = total
    held[head_rows:step, :] = pair_ref[lax.axis_index("pos"), head_rows:step, :]
    first = lax.axis_index("seq") * blocks
    table = jnp.concatenate(
        [pair_ref[first + n, head_rows:step, :] for n in range(blocks)], axis=0
    )
    amount = jnp.sum(total, axis=1, keepdims=True)
    real = lax.broadcasted_iota(jnp.int32, (head_rows, 1), 0) < heads
    share = jnp.where(real, factor_ref[0:head_rows, 0:1] / jnp.where(real, amount, 1.0), 0.0)
    slab = dot_nn(held[...], slab_ref[...], HIGHEST)
    own = dot_nt(own_ref[...], total * share, HIGHEST)
    mirrored = dot_nt(own_ref[...], table, HIGHEST)
    adjuster = dot_nn(own, slab[0:head_rows, :], HIGHEST)
    out_ref[...] = jax.nn.sigmoid(
        slab[head_rows:step, :] + mirrored - adjuster + factor_ref[head_rows : head_rows + 1, 0:1]
    )


def call(kernel, out_shape, operands, smem=(), hbm=(), scratch=(), bytes_accessed=1000000):
    vmem = pl.BlockSpec(memory_space=pltpu.VMEM)
    held = sum(math.prod(a.shape) * a.dtype.itemsize for a in [*operands, *jax.tree.leaves(out_shape)])
    held += sum(
        math.prod(a.shape) * np.dtype(a.dtype).itemsize
        for a in scratch
        if a.memory_space == pltpu.VMEM
    )
    limit = 2 * held + 4 * 1024 * 1024
    specs = [
        pl.BlockSpec(memory_space=pltpu.SMEM if i in smem else pl.ANY if i in hbm else pltpu.VMEM)
        for i in range(len(operands))
    ]
    return pl.pallas_call(
        kernel,
        out_shape=out_shape,
        in_specs=specs,
        out_specs=jax.tree.map(lambda _: vmem, out_shape),
        scratch_shapes=list(scratch),
        compiler_params=pltpu.CompilerParams(vmem_limit_bytes=limit),
        cost_estimate=pl.CostEstimate(
            flops=1000000, bytes_accessed=bytes_accessed, transcendentals=0
        ),
    )(*operands)


def stages_of(count):
    stages, stride = [], 1
    while count > 1 and len(stages) < 2 and count % 2 == 0:
        stages.append((stride, 2))
        stride, count = stride * 2, count // 2
    if count > 1:
        stages.append((stride, count))
    return stages[::-1]


def send_pos(array, count, stride, size, delta):
    pairs = []
    for p in range(count):
        a = (p // stride) % size
        pairs.append((p, p + ((a + delta) % size - a) * stride))
    return lax.ppermute(array, "pos", pairs)


def send_all(parts, count, stage):
    stride, size = stage
    return [send_pos(part, count, stride, size, delta) for delta in range(1, size) for part in parts]


def after(array, *others):
    return lax.optimization_barrier((array, *others))[0]


def per_device(
    skip_stream_input,
    lateral_asking_vectors,
    lateral_matched_vectors,
    lateral_carried_vectors,
    lateral_closing_linear,
    upright_normalizer_multiplier,
    upright_threefold_linear,
    upright_closing_linear,
    regression_factors,
    regression_offset,
):
    rows, sites, embed = lateral_asking_vectors.shape
    heads = regression_factors.shape[0]
    head = embed // heads
    seq_count = lax.axis_size("seq")
    pos_count = lax.axis_size("pos")
    length = sites * pos_count
    slab_width = length // seq_count
    cells = rows * sites
    pos_index = lax.axis_index("pos").astype(jnp.int32)
    seq_index = lax.axis_index("seq").astype(jnp.int32)
    swap = [(s, 1 - s) for s in range(2)]
    columns = upright_threefold_linear.shape[1]
    swapped = seq_count == 2 and columns % 128 == 0

    stages = stages_of(pos_count)
    outer = stages[0]
    middle = stages[1] if len(stages) > 1 else None

    scalars = jnp.stack([seq_index, pos_index])
    head_rows = round_up(heads, 8)
    width = lane_block(embed, head)
    key_first = [lateral_matched_vectors] + send_all([lateral_matched_vectors], pos_count, outer)
    key_parts = [jnp.concatenate(key_first, axis=1)]
    later_value = after(lateral_carried_vectors, key_parts[0])
    value_first = [later_value]
    for delta in range(1, outer[1]):
        sent = lateral_carried_vectors if delta in (1, outer[1] - 1) else later_value
        value_first.append(send_pos(sent, pos_count, *outer, delta))
    masked = call(
        functools.partial(query_kernel, head),
        jax.ShapeDtypeStruct((rows, heads * sites, width), BF16),
        [after(lateral_asking_vectors, key_parts[0])],
        hbm=(0,),
        scratch=[pltpu.VMEM((rows, sites, embed), BF16), pltpu.SemaphoreType.DMA((1,))],
    )
    if middle:
        key_parts += send_all(key_parts, pos_count, middle)
    near = sum(part.shape[1] for part in key_parts)
    partial = call(
        functools.partial(logits_kernel, len(key_parts)),
        jax.ShapeDtypeStruct((heads * sites, near), F32),
        [masked, *key_parts],
    )
    value_first[1] = after(value_first[1], masked)
    value_parts = [jnp.concatenate(value_first, axis=1)]
    if middle:
        value_parts += send_all(value_parts, pos_count, middle)
    if len(stages) > 2:
        far_parts = send_all(key_parts, pos_count, stages[2])
        partial = call(
            functools.partial(logits_kernel, len(far_parts)),
            jax.ShapeDtypeStruct((heads * sites, length), F32),
            [masked, *far_parts, partial],
        )
    skip, gain, head_factors, order, own_select, slab_select = call(
        functools.partial(prepare_kernel, heads, stages),
        (
            jax.ShapeDtypeStruct((cells, embed), F32),
            jax.ShapeDtypeStruct((8, embed), F32),
            jax.ShapeDtypeStruct((head_rows + 8, 128), F32),
            jax.ShapeDtypeStruct((length, length), F32),
            jax.ShapeDtypeStruct((sites, length), F32),
            jax.ShapeDtypeStruct((length, slab_width), F32),
        ),
        [
            after(scalars, partial),
            skip_stream_input,
            upright_normalizer_multiplier,
            regression_factors,
            regression_offset,
        ],
        smem=(0, 3, 4),
        hbm=(1,),
        scratch=[pltpu.VMEM((rows, sites, embed), BF16), pltpu.SemaphoreType.DMA((1,))],
    )
    if seq_count == 2:
        partials = [partial, after(lax.ppermute(partial, "seq", swap), skip)]
    else:
        partials = [lax.psum(partial, "seq")]
    shares = call(
        functools.partial(
            softmax_kernel, 1.0 / (math.sqrt(head) * math.sqrt(rows * seq_count))
        ),
        jax.ShapeDtypeStruct((heads * sites, length), BF16),
        partials,
    )

    pair_local = call(
        functools.partial(pair_kernel, heads),
        jax.ShapeDtypeStruct((pos_count, head_rows + sites, length), F32),
        [shares, head_factors, order],
        bytes_accessed=10000000,
        scratch=[pltpu.VMEM((head_rows + sites, length), F32)],
    )
    if len(stages) > 2:
        value_parts = value_parts[:1] + [after(part, pair_local) for part in value_parts[1:]]
        value_parts += send_all(value_parts, pos_count, stages[2])
    hidden, normed = call(
        functools.partial(mix_kernel, head, len(value_parts)),
        (
            jax.ShapeDtypeStruct((cells, embed), F32),
            jax.ShapeDtypeStruct((cells, embed), BF16),
        ),
        [shares, *value_parts, lateral_closing_linear, skip, gain],
        scratch=[pltpu.VMEM((cells, embed), F32)],
    )
    pair_all = lax.all_to_all(pair_local, "pos", split_axis=0, concat_axis=0, tiled=True)
    pairing_chances = call(
        functools.partial(contact_kernel, heads),
        jax.ShapeDtypeStruct((sites, slab_width), F32),
        [pair_all, head_factors, own_select, slab_select],
        scratch=[pltpu.VMEM((head_rows + sites, length), F32)],
    )
    if swapped:
        normed_all = [normed, lax.ppermute(normed, "seq", swap)]
        weight = upright_threefold_linear
    else:
        normed_all = [normed]
        weight = lax.all_gather(upright_threefold_linear, "seq", axis=1, tiled=True)
    projected = call(
        functools.partial(project_kernel, len(normed_all)),
        jax.ShapeDtypeStruct((cells * len(normed_all), weight.shape[1]), BF16),
        [*normed_all, weight],
        bytes_accessed=30000000,
    )
    if swapped:
        column, column_inputs = swapped_column_kernel, [
            projected,
            lax.ppermute(projected, "seq", swap),
        ]
    else:
        key_value = lax.all_gather(projected[:, embed:], "seq", axis=0, tiled=True)
        column, column_inputs = column_kernel, [projected[:, :embed], key_value]
    alignment_output = call(
        functools.partial(column, head, 1.0 / math.sqrt(head)),
        jax.ShapeDtypeStruct((rows, sites, embed), BF16),
        [*column_inputs, after(hidden, pairing_chances), upright_closing_linear],
        scratch=[
            pltpu.VMEM((cells * rows * seq_count, embed), F32),
            pltpu.VMEM((cells, embed), F32),
        ],
    )
    return alignment_output, pairing_chances


def solution(mesh):
    cells = P("seq", "pos", None)
    return jax.shard_map(
        per_device,
        mesh=mesh,
        in_specs=(cells, cells, cells, cells, P(), P(), P(None, "seq"), P(), P(), P()),
        out_specs=(cells, P("pos", "seq")),
        check_vma=False,
    )
```

```python
import functools
import math

import jax
import jax.numpy as jnp
import numpy as np
from jax import lax
from jax.experimental import pallas as pl
from jax.experimental.pallas import tpu as pltpu
from jax.sharding import PartitionSpec as P

F32 = jnp.float32
BF16 = jnp.bfloat16
HIGHEST = lax.Precision.HIGHEST
LANE_BLOCK = 256


def dot_nn(a, b, precision=None):
    return lax.dot_general(
        a, b, (((1,), (0,)), ((), ())), precision=precision, preferred_element_type=F32
    )


def dot_nt(a, b, precision=None):
    return lax.dot_general(
        a, b, (((1,), (1,)), ((), ())), precision=precision, preferred_element_type=F32
    )


def round_up(n, m):
    return -(-n // m) * m


def lane_block(embed, head):
    return LANE_BLOCK if embed % LANE_BLOCK == 0 and LANE_BLOCK % head == 0 else head


def arrival_place(index, column, stages, sites):
    block, place, span = column // sites, column % sites, 1
    for stride, size in stages:
        digit = (block // span) % size
        place = place + ((index // stride) % size + size - digit) % size * (stride * sites)
        span *= size
    return place


def fetch(pairs, sems):
    copies = [pltpu.make_async_copy(src, dst, sems.at[i]) for i, (src, dst) in enumerate(pairs)]
    for copy in copies:
        copy.start()
    for copy in copies:
        copy.wait()


def query_kernel(head, q_hbm, masked_ref, q_ref, sems):
    rows, sites, embed = q_ref.shape
    width = masked_ref.shape[2]
    group = width // head
    span = group * sites
    fetch([(q_hbm, q_ref)], sems)
    lane_head = lax.broadcasted_iota(jnp.int32, (span, width), 1) // head
    row_head = lax.broadcasted_iota(jnp.int32, (span, width), 0) // sites
    own_head = lane_head == row_head
    for block in range(embed // width):
        for r in range(rows):
            q = q_ref[r, :, block * width : (block + 1) * width].astype(F32)
            q = jnp.where(own_head, jnp.concatenate([q] * group, axis=0), 0.0).astype(BF16)
            masked_ref[r, block * span : (block + 1) * span, :] = q


def prepare_kernel(heads, stages, scalar_ref, skip_hbm, gain_ref, factor_ref, offset_ref, *refs):
    wide_skip_ref, wide_gain_ref, head_ref, order_ref, own_ref, slab_ref, skip_ref, sems = refs
    _, sites, embed = skip_ref.shape
    copy = pltpu.make_async_copy(skip_hbm, skip_ref, sems.at[0])
    copy.start()
    wide_gain_ref[...] = jnp.broadcast_to(gain_ref[...].reshape(1, embed), wide_gain_ref.shape)
    row = lax.broadcasted_iota(jnp.int32, head_ref.shape, 0)
    factors = jnp.zeros(head_ref.shape, F32)
    for h in range(heads):
        factors = jnp.where(row == h, factor_ref[h], factors)
    head_ref[...] = jnp.where(row == round_up(heads, 8), offset_ref[0], factors)
    seq_index, pos_index = scalar_ref[0], scalar_ref[1]
    length = order_ref.shape[0]
    row = lax.broadcasted_iota(jnp.int32, (length, length), 0)
    lane = lax.broadcasted_iota(jnp.int32, (length, length), 1)
    order_ref[...] = (arrival_place(pos_index, row, stages, sites) == lane).astype(F32)
    row = lax.broadcasted_iota(jnp.int32, own_ref.shape, 0)
    lane = lax.broadcasted_iota(jnp.int32, own_ref.shape, 1)
    own_ref[...] = (row + pos_index * sites == lane).astype(F32)
    row = lax.broadcasted_iota(jnp.int32, slab_ref.shape, 0)
    lane = lax.broadcasted_iota(jnp.int32, slab_ref.shape, 1)
    slab_ref[...] = (row == lane + seq_index * slab_ref.shape[1]).astype(F32)
    copy.wait()
    wide_skip_ref[...] = skip_ref[...].astype(F32).reshape(wide_skip_ref.shape)


def logits_kernel(part_count, *refs):
    q_ref, k_refs, done_refs, out_ref = refs[0], refs[1 : 1 + part_count], refs[1 + part_count : -1], refs[-1]
    rows, _, width = q_ref.shape
    blocks = k_refs[0].shape[2] // width
    span = q_ref.shape[1] // blocks
    for block in range(blocks):
        cols = slice(block * width, (block + 1) * width)
        lines = slice(block * span, (block + 1) * span)
        total = None
        for r in range(rows):
            keys = jnp.concatenate([k[r, :, cols] for k in k_refs], axis=0)
            term = dot_nt(q_ref[r, lines, :], keys)
            total = term if total is None else total + term
        out_ref[lines, :] = jnp.concatenate([done[lines, :] for done in done_refs] + [total], axis=1)


def softmax_kernel(factor, *refs):
    parts, w_ref = refs[:-1], refs[-1]
    logits = parts[0][...]
    for part in parts[1:]:
        logits = logits + part[...]
    logits = logits * factor
    exponent = jnp.exp(logits - jnp.max(logits, axis=1, keepdims=True))
    shares = (exponent / jnp.sum(exponent, axis=1, keepdims=True)).astype(BF16)
    w_ref[...] = shares


def pair_kernel(heads, w_ref, head_ref, order_ref, pair_ref, held):
    rows, length = w_ref.shape
    sites = rows // heads
    shares = w_ref[...].astype(F32)
    row_sum = jnp.sum(shares, axis=1, keepdims=True)
    lane = lax.broadcasted_iota(jnp.int32, (rows, length), 1)
    row = lax.broadcasted_iota(jnp.int32, (rows, length), 0) % sites
    both = (shares + jnp.where(lane == row, row_sum, 0.0)).reshape(heads, sites, length)
    head_rows = round_up(heads, 8)
    held[...] = jnp.zeros_like(held)
    held[0:heads, :] = jnp.sum(both, axis=1)
    merged = None
    for h in range(heads):
        term = shares[h * sites : (h + 1) * sites, :] * head_ref[h : h + 1, 0:1]
        merged = term if merged is None else merged + term
    held[head_rows : head_rows + sites, :] = merged
    pair_ref[...] = jnp.broadcast_to(
        dot_nn(held[...], order_ref[...], HIGHEST)[None], pair_ref.shape
    )


def mix_kernel(head, v_count, *refs):
    w_ref, v_refs = refs[0], refs[1 : 1 + v_count]
    closing_ref, skip_ref, gain_ref, hidden_ref, normed_ref, mixed = refs[1 + v_count :]
    rows, _, embed = v_refs[0].shape
    sites = skip_ref.shape[0] // rows
    width = lane_block(embed, head)
    group = width // head
    lane_head = lax.broadcasted_iota(jnp.int32, (sites, width), 1) // head
    for block in range(embed // width):
        cols = slice(block * width, (block + 1) * width)
        shares = w_ref[block * group * sites : (block + 1) * group * sites, :]
        for r in range(rows):
            values = jnp.concatenate([v[r, :, cols] for v in v_refs], axis=0)
            product = dot_nn(shares, values)
            own = product[0:sites, :]
            for g in range(1, group):
                own = jnp.where(lane_head == g, product[g * sites : (g + 1) * sites, :], own)
            mixed[r * sites : (r + 1) * sites, cols] = own
    hidden = skip_ref[...] + dot_nn(mixed[...].astype(BF16), closing_ref[...])
    hidden_ref[...] = hidden
    centered = hidden - jnp.mean(hidden, axis=1, keepdims=True)
    spread = jnp.mean(centered * centered, axis=1, keepdims=True)
    normed_ref[...] = (centered * lax.rsqrt(spread + 1e-05) * gain_ref[0:1, :]).astype(BF16)


def project_kernel(part_count, *refs):
    parts, (weight_ref, out_ref) = refs[:part_count], refs[part_count:]
    normed = jnp.concatenate([part[...] for part in parts], axis=0)
    out_ref[...] = dot_nn(normed, weight_ref[...]).astype(BF16)


def column_attend(head, factor, query, keys, values, hidden_ref, closing_ref, out_ref, products, mixed):
    rows, sites, embed = out_ref.shape
    padded = round_up(embed // head, 128)
    pick = (
        lax.broadcasted_iota(jnp.int32, (embed, padded), 0) // head
        == lax.broadcasted_iota(jnp.int32, (embed, padded), 1)
    ).astype(BF16)
    spread = (
        lax.broadcasted_iota(jnp.int32, (padded, embed), 1) // head
        == lax.broadcasted_iota(jnp.int32, (padded, embed), 0)
    ).astype(BF16)
    seqs = len(keys)
    for s in range(rows):
        for t in range(seqs):
            at = (s * seqs + t) * sites
            products[at : at + sites, :] = query[s * sites : (s + 1) * sites, :] * keys[t]
    product = products[...]
    high = product.astype(BF16)
    low = (product - high.astype(F32)).astype(BF16)
    scores = (dot_nn(high, pick) + dot_nn(low, pick)) * factor
    exponent = jnp.exp(scores).reshape(rows, seqs, sites, padded)
    shares = (exponent / jnp.sum(exponent, axis=1, keepdims=True)).astype(BF16)
    wide = dot_nn(shares.reshape(rows * seqs * sites, padded), spread)
    for s in range(rows):
        total = None
        for t in range(seqs):
            at = (s * seqs + t) * sites
            term = wide[at : at + sites, :] * values[t]
            total = term if total is None else total + term
        mixed[s * sites : (s + 1) * sites, :] = total
    out = hidden_ref[...] + dot_nn(mixed[...].astype(BF16), closing_ref[...])
    out_ref[...] = out.reshape(rows, sites, embed).astype(BF16)


def column_kernel(head, factor, query_ref, kv_ref, *refs):
    rows, sites, embed = refs[2].shape
    kv = kv_ref[...].astype(F32)
    seqs = kv.shape[0] // sites
    keys = [kv[t * sites : (t + 1) * sites, 0:embed] for t in range(seqs)]
    values = [kv[t * sites : (t + 1) * sites, embed:] for t in range(seqs)]
    column_attend(head, factor, query_ref[...].astype(F32), keys, values, *refs)


def swapped_column_kernel(head, factor, own_ref, other_ref, *refs):
    rows, sites, embed = refs[2].shape
    cells, columns = own_ref.shape
    half = cells // 2

    def piece(first_is_own, start, stop, at, size):
        found = []
        for block in range(2):
            lo, hi = max(start, block * columns), min(stop, (block + 1) * columns)
            if lo < hi:
                cols = slice(lo - block * columns, hi - block * columns)
                if (block == 0) == first_is_own:
                    found.append(own_ref[at : at + size, cols])
                else:
                    turned = (at + half) % cells
                    found.append(other_ref[turned : turned + size, cols])
        return jnp.concatenate(found, axis=1).astype(F32)

    def attend(first_is_own):
        query = piece(first_is_own, 0, embed, 0, half)
        keys, values = [], []
        for at in (0, half):
            key = piece(first_is_own, embed, 2 * embed, at, half)
            value = piece(first_is_own, 2 * embed, 3 * embed, at, half)
            for t in range(half // sites):
                keys.append(key[t * sites : (t + 1) * sites, :])
                values.append(value[t * sites : (t + 1) * sites, :])
        column_attend(head, factor, query, keys, values, *refs)

    seq_index = lax.axis_index("seq")
    pl.when(seq_index == 0)(functools.partial(attend, True))
    pl.when(seq_index == 1)(functools.partial(attend, False))


def contact_kernel(heads, pair_ref, factor_ref, own_ref, slab_ref, out_ref, held):
    count, step, length = pair_ref.shape
    head_rows = round_up(heads, 8)
    sites = step - head_rows
    blocks = slab_ref.shape[1] // sites
    total = pair_ref[0, 0:head_rows, :]
    for n in range(1, count):
        total = total + pair_ref[n, 0:head_rows, :]
    held[0:head_rows, :] = total
    held[head_rows:step, :] = pair_ref[lax.axis_index("pos"), head_rows:step, :]
    first = lax.axis_index("seq") * blocks
    table = jnp.concatenate(
        [pair_ref[first + n, head_rows:step, :] for n in range(blocks)], axis=0
    )
    amount = jnp.sum(total, axis=1, keepdims=True)
    real = lax.broadcasted_iota(jnp.int32, (head_rows, 1), 0) < heads
    share = jnp.where(real, factor_ref[0:head_rows, 0:1] / jnp.where(real, amount, 1.0), 0.0)
    slab = dot_nn(held[...], slab_ref[...], HIGHEST)
    own = dot_nt(own_ref[...], total * share, HIGHEST)
    mirrored = dot_nt(own_ref[...], table, HIGHEST)
    adjuster = dot_nn(own, slab[0:head_rows, :], HIGHEST)
    out_ref[...] = jax.nn.sigmoid(
        slab[head_rows:step, :] + mirrored - adjuster + factor_ref[head_rows : head_rows + 1, 0:1]
    )


def call(kernel, out_shape, operands, smem=(), hbm=(), scratch=(), bytes_accessed=1000000):
    vmem = pl.BlockSpec(memory_space=pltpu.VMEM)
    held = sum(math.prod(a.shape) * a.dtype.itemsize for a in [*operands, *jax.tree.leaves(out_shape)])
    held += sum(
        math.prod(a.shape) * np.dtype(a.dtype).itemsize
        for a in scratch
        if a.memory_space == pltpu.VMEM
    )
    limit = 2 * held + 4 * 1024 * 1024
    specs = [
        pl.BlockSpec(memory_space=pltpu.SMEM if i in smem else pl.ANY if i in hbm else pltpu.VMEM)
        for i in range(len(operands))
    ]
    return pl.pallas_call(
        kernel,
        out_shape=out_shape,
        in_specs=specs,
        out_specs=jax.tree.map(lambda _: vmem, out_shape),
        scratch_shapes=list(scratch),
        compiler_params=pltpu.CompilerParams(vmem_limit_bytes=limit),
        cost_estimate=pl.CostEstimate(
            flops=1000000, bytes_accessed=bytes_accessed, transcendentals=0
        ),
    )(*operands)


def stages_of(count):
    stages, stride = [], 1
    while count > 1 and len(stages) < 2 and count % 2 == 0:
        stages.append((stride, 2))
        stride, count = stride * 2, count // 2
    if count > 1:
        stages.append((stride, count))
    return stages[::-1]


def send_pos(array, count, stride, size, delta):
    pairs = []
    for p in range(count):
        a = (p // stride) % size
        pairs.append((p, p + ((a + delta) % size - a) * stride))
    return lax.ppermute(array, "pos", pairs)


def send_all(parts, count, stage):
    stride, size = stage
    return [send_pos(part, count, stride, size, delta) for delta in range(1, size) for part in parts]


def after(array, *others):
    return lax.optimization_barrier((array, *others))[0]


def per_device(
    skip_stream_input,
    lateral_asking_vectors,
    lateral_matched_vectors,
    lateral_carried_vectors,
    lateral_closing_linear,
    upright_normalizer_multiplier,
    upright_threefold_linear,
    upright_closing_linear,
    regression_factors,
    regression_offset,
):
    rows, sites, embed = lateral_asking_vectors.shape
    heads = regression_factors.shape[0]
    head = embed // heads
    seq_count = lax.axis_size("seq")
    pos_count = lax.axis_size("pos")
    length = sites * pos_count
    slab_width = length // seq_count
    cells = rows * sites
    pos_index = lax.axis_index("pos").astype(jnp.int32)
    seq_index = lax.axis_index("seq").astype(jnp.int32)
    swap = [(s, 1 - s) for s in range(2)]
    columns = upright_threefold_linear.shape[1]
    swapped = seq_count == 2 and columns % 128 == 0

    stages = stages_of(pos_count)
    outer = stages[0]
    middle = stages[1] if len(stages) > 1 else None

    scalars = jnp.stack([seq_index, pos_index])
    head_rows = round_up(heads, 8)
    width = lane_block(embed, head)
    key_first = [lateral_matched_vectors] + send_all([lateral_matched_vectors], pos_count, outer)
    key_parts = [jnp.concatenate(key_first, axis=1)]
    later_value = after(lateral_carried_vectors, key_parts[0])
    value_first = [later_value]
    for delta in range(1, outer[1]):
        sent = lateral_carried_vectors if delta in (1, outer[1] - 1) else later_value
        value_first.append(send_pos(sent, pos_count, *outer, delta))
    masked = call(
        functools.partial(query_kernel, head),
        jax.ShapeDtypeStruct((rows, heads * sites, width), BF16),
        [after(lateral_asking_vectors, key_parts[0])],
        hbm=(0,),
        scratch=[pltpu.VMEM((rows, sites, embed), BF16), pltpu.SemaphoreType.DMA((1,))],
    )
    if middle:
        key_parts += send_all(key_parts, pos_count, middle)
    near = sum(part.shape[1] for part in key_parts)
    partial = call(
        functools.partial(logits_kernel, len(key_parts)),
        jax.ShapeDtypeStruct((heads * sites, near), F32),
        [masked, *key_parts],
    )
    value_first[1] = after(value_first[1], masked)
    value_parts = [jnp.concatenate(value_first, axis=1)]
    if middle:
        value_parts += send_all(value_parts, pos_count, middle)
    if len(stages) > 2:
        far_parts = send_all(key_parts, pos_count, stages[2])
        partial = call(
            functools.partial(logits_kernel, len(far_parts)),
            jax.ShapeDtypeStruct((heads * sites, length), F32),
            [masked, *far_parts, partial],
        )
    skip, gain, head_factors, order, own_select, slab_select = call(
        functools.partial(prepare_kernel, heads, stages),
        (
            jax.ShapeDtypeStruct((cells, embed), F32),
            jax.ShapeDtypeStruct((8, embed), F32),
            jax.ShapeDtypeStruct((head_rows + 8, 128), F32),
            jax.ShapeDtypeStruct((length, length), F32),
            jax.ShapeDtypeStruct((sites, length), F32),
            jax.ShapeDtypeStruct((length, slab_width), F32),
        ),
        [
            after(scalars, partial),
            skip_stream_input,
            upright_normalizer_multiplier,
            regression_factors,
            regression_offset,
        ],
        smem=(0, 3, 4),
        hbm=(1,),
        scratch=[pltpu.VMEM((rows, sites, embed), BF16), pltpu.SemaphoreType.DMA((1,))],
    )
    if seq_count == 2:
        partials = [partial, after(lax.ppermute(partial, "seq", swap), skip)]
    else:
        partials = [lax.psum(partial, "seq")]
    shares = call(
        functools.partial(
            softmax_kernel, 1.0 / (math.sqrt(head) * math.sqrt(rows * seq_count))
        ),
        jax.ShapeDtypeStruct((heads * sites, length), BF16),
        partials,
    )

    pair_local = call(
        functools.partial(pair_kernel, heads),
        jax.ShapeDtypeStruct((pos_count, head_rows + sites, length), F32),
        [shares, head_factors, order],
        scratch=[pltpu.VMEM((head_rows + sites, length), F32)],
    )
    if len(stages) > 2:
        value_parts = value_parts[:1] + [after(part, pair_local) for part in value_parts[1:]]
        value_parts += send_all(value_parts, pos_count, stages[2])
    hidden, normed = call(
        functools.partial(mix_kernel, head, len(value_parts)),
        (
            jax.ShapeDtypeStruct((cells, embed), F32),
            jax.ShapeDtypeStruct((cells, embed), BF16),
        ),
        [shares, *value_parts, lateral_closing_linear, skip, gain],
        scratch=[pltpu.VMEM((cells, embed), F32)],
    )
    pair_all = lax.all_to_all(pair_local, "pos", split_axis=0, concat_axis=0, tiled=True)
    pairing_chances = call(
        functools.partial(contact_kernel, heads),
        jax.ShapeDtypeStruct((sites, slab_width), F32),
        [pair_all, head_factors, own_select, slab_select],
        scratch=[pltpu.VMEM((head_rows + sites, length), F32)],
    )
    if swapped:
        normed_all = [normed, lax.ppermute(normed, "seq", swap)]
        weight = upright_threefold_linear
    else:
        normed_all = [normed]
        weight = lax.all_gather(upright_threefold_linear, "seq", axis=1, tiled=True)
    projected = call(
        functools.partial(project_kernel, len(normed_all)),
        jax.ShapeDtypeStruct((cells * len(normed_all), weight.shape[1]), BF16),
        [*normed_all, weight],
    )
    if swapped:
        column, column_inputs = swapped_column_kernel, [
            projected,
            lax.ppermute(projected, "seq", swap),
        ]
    else:
        key_value = lax.all_gather(projected[:, embed:], "seq", axis=0, tiled=True)
        column, column_inputs = column_kernel, [projected[:, :embed], key_value]
    alignment_output = call(
        functools.partial(column, head, 1.0 / math.sqrt(head)),
        jax.ShapeDtypeStruct((rows, sites, embed), BF16),
        [*column_inputs, after(hidden, pairing_chances), upright_closing_linear],
        scratch=[
            pltpu.VMEM((cells * rows * seq_count, embed), F32),
            pltpu.VMEM((cells, embed), F32),
        ],
    )
    return alignment_output, pairing_chances


def solution(mesh):
    cells = P("seq", "pos", None)
    return jax.shard_map(
        per_device,
        mesh=mesh,
        in_specs=(cells, cells, cells, cells, P(), P(), P(None, "seq"), P(), P(), P()),
        out_specs=(cells, P("pos", "seq")),
        check_vma=False,
    )
```

```python
import functools
import math

import jax
import jax.numpy as jnp
import numpy as np
from jax import lax
from jax.experimental import pallas as pl
from jax.experimental.pallas import tpu as pltpu
from jax.sharding import PartitionSpec as P

F32 = jnp.float32
BF16 = jnp.bfloat16
HIGHEST = lax.Precision.HIGHEST
LANE_BLOCK = 256


def dot_nn(a, b, precision=None):
    return lax.dot_general(
        a, b, (((1,), (0,)), ((), ())), precision=precision, preferred_element_type=F32
    )


def dot_nt(a, b, precision=None):
    return lax.dot_general(
        a, b, (((1,), (1,)), ((), ())), precision=precision, preferred_element_type=F32
    )


def round_up(n, m):
    return -(-n // m) * m


def lane_block(embed, head):
    return LANE_BLOCK if embed % LANE_BLOCK == 0 and LANE_BLOCK % head == 0 else head


def arrival_place(index, column, stages, sites):
    block, place, span = column // sites, column % sites, 1
    for stride, size in stages:
        digit = (block // span) % size
        place = place + ((index // stride) % size + size - digit) % size * (stride * sites)
        span *= size
    return place


def fetch(pairs, sems):
    copies = [pltpu.make_async_copy(src, dst, sems.at[i]) for i, (src, dst) in enumerate(pairs)]
    for copy in copies:
        copy.start()
    for copy in copies:
        copy.wait()


def query_kernel(head, q_hbm, masked_ref, q_ref, sems):
    rows, sites, embed = q_ref.shape
    width = masked_ref.shape[2]
    group = width // head
    span = group * sites
    fetch([(q_hbm, q_ref)], sems)
    lane_head = lax.broadcasted_iota(jnp.int32, (span, width), 1) // head
    row_head = lax.broadcasted_iota(jnp.int32, (span, width), 0) // sites
    own_head = lane_head == row_head
    for block in range(embed // width):
        for r in range(rows):
            q = q_ref[r, :, block * width : (block + 1) * width].astype(F32)
            q = jnp.where(own_head, jnp.concatenate([q] * group, axis=0), 0.0).astype(BF16)
            masked_ref[r, block * span : (block + 1) * span, :] = q


def prepare_kernel(heads, sites, stages, scalar_ref, factor_ref, offset_ref, *refs):
    head_ref, order_ref, own_ref, slab_ref = refs
    row = lax.broadcasted_iota(jnp.int32, head_ref.shape, 0)
    factors = jnp.zeros(head_ref.shape, F32)
    for h in range(heads):
        factors = jnp.where(row == h, factor_ref[h], factors)
    head_ref[...] = jnp.where(row == round_up(heads, 8), offset_ref[0], factors)
    seq_index, pos_index = scalar_ref[0], scalar_ref[1]
    length = order_ref.shape[0]
    row = lax.broadcasted_iota(jnp.int32, (length, length), 0)
    lane = lax.broadcasted_iota(jnp.int32, (length, length), 1)
    order_ref[...] = (arrival_place(pos_index, row, stages, sites) == lane).astype(F32)
    row = lax.broadcasted_iota(jnp.int32, own_ref.shape, 0)
    lane = lax.broadcasted_iota(jnp.int32, own_ref.shape, 1)
    own_ref[...] = (row + pos_index * sites == lane).astype(F32)
    row = lax.broadcasted_iota(jnp.int32, slab_ref.shape, 0)
    lane = lax.broadcasted_iota(jnp.int32, slab_ref.shape, 1)
    slab_ref[...] = (row == lane + seq_index * slab_ref.shape[1]).astype(F32)


def logits_kernel(part_count, *refs):
    q_ref, k_refs, done_refs, out_ref = refs[0], refs[1 : 1 + part_count], refs[1 + part_count : -1], refs[-1]
    rows, _, width = q_ref.shape
    blocks = k_refs[0].shape[2] // width
    span = q_ref.shape[1] // blocks
    for block in range(blocks):
        cols = slice(block * width, (block + 1) * width)
        lines = slice(block * span, (block + 1) * span)
        total = None
        for r in range(rows):
            keys = jnp.concatenate([k[r, :, cols] for k in k_refs], axis=0)
            term = dot_nt(q_ref[r, lines, :], keys)
            total = term if total is None else total + term
        out_ref[lines, :] = jnp.concatenate([done[lines, :] for done in done_refs] + [total], axis=1)


def softmax_kernel(factor, *refs):
    parts, w_ref = refs[:-1], refs[-1]
    logits = parts[0][...]
    for part in parts[1:]:
        logits = logits + part[...]
    logits = logits * factor
    exponent = jnp.exp(logits - jnp.max(logits, axis=1, keepdims=True))
    shares = (exponent / jnp.sum(exponent, axis=1, keepdims=True)).astype(BF16)
    w_ref[...] = shares


def pair_kernel(heads, w_ref, head_ref, order_ref, pair_ref, held):
    rows, length = w_ref.shape
    sites = rows // heads
    shares = w_ref[...].astype(F32)
    row_sum = jnp.sum(shares, axis=1, keepdims=True)
    lane = lax.broadcasted_iota(jnp.int32, (rows, length), 1)
    row = lax.broadcasted_iota(jnp.int32, (rows, length), 0) % sites
    both = (shares + jnp.where(lane == row, row_sum, 0.0)).reshape(heads, sites, length)
    head_rows = round_up(heads, 8)
    held[...] = jnp.zeros_like(held)
    held[0:heads, :] = jnp.sum(both, axis=1)
    merged = None
    for h in range(heads):
        term = shares[h * sites : (h + 1) * sites, :] * head_ref[h : h + 1, 0:1]
        merged = term if merged is None else merged + term
    held[head_rows : head_rows + sites, :] = merged
    pair_ref[...] = jnp.broadcast_to(
        dot_nn(held[...], order_ref[...], HIGHEST)[None], pair_ref.shape
    )


def mix_kernel(head, v_count, *refs):
    w_ref, v_refs = refs[0], refs[1 : 1 + v_count]
    closing_ref, skip_ref, gain_ref, hidden_ref, normed_ref, mixed = refs[1 + v_count :]
    rows, sites, embed = skip_ref.shape
    width = lane_block(embed, head)
    group = width // head
    lane_head = lax.broadcasted_iota(jnp.int32, (sites, width), 1) // head
    for block in range(embed // width):
        cols = slice(block * width, (block + 1) * width)
        shares = w_ref[block * group * sites : (block + 1) * group * sites, :]
        for r in range(rows):
            values = jnp.concatenate([v[r, :, cols] for v in v_refs], axis=0)
            product = dot_nn(shares, values)
            own = product[0:sites, :]
            for g in range(1, group):
                own = jnp.where(lane_head == g, product[g * sites : (g + 1) * sites, :], own)
            mixed[r * sites : (r + 1) * sites, cols] = own
    hidden = skip_ref[...].astype(F32).reshape(rows * sites, embed) + dot_nn(mixed[...].astype(BF16), closing_ref[...])
    hidden_ref[...] = hidden
    centered = hidden - jnp.mean(hidden, axis=1, keepdims=True)
    spread = jnp.mean(centered * centered, axis=1, keepdims=True)
    normed_ref[...] = (centered * lax.rsqrt(spread + 1e-05) * gain_ref[...].reshape(1, embed)).astype(BF16)


def project_kernel(part_count, *refs):
    parts, (weight_ref, out_ref) = refs[:part_count], refs[part_count:]
    normed = jnp.concatenate([part[...] for part in parts], axis=0)
    out_ref[...] = dot_nn(normed, weight_ref[...]).astype(BF16)


def column_attend(head, factor, query, keys, values, hidden_ref, closing_ref, out_ref, products, mixed):
    rows, sites, embed = out_ref.shape
    padded = round_up(embed // head, 128)
    pick = (
        lax.broadcasted_iota(jnp.int32, (embed, padded), 0) // head
        == lax.broadcasted_iota(jnp.int32, (embed, padded), 1)
    ).astype(BF16)
    spread = (
        lax.broadcasted_iota(jnp.int32, (padded, embed), 1) // head
        == lax.broadcasted_iota(jnp.int32, (padded, embed), 0)
    ).astype(BF16)
    seqs = len(keys)
    for s in range(rows):
        for t in range(seqs):
            at = (s * seqs + t) * sites
            products[at : at + sites, :] = query[s * sites : (s + 1) * sites, :] * keys[t]
    product = products[...]
    high = product.astype(BF16)
    low = (product - high.astype(F32)).astype(BF16)
    scores = (dot_nn(high, pick) + dot_nn(low, pick)) * factor
    exponent = jnp.exp(scores).reshape(rows, seqs, sites, padded)
    shares = (exponent / jnp.sum(exponent, axis=1, keepdims=True)).astype(BF16)
    wide = dot_nn(shares.reshape(rows * seqs * sites, padded), spread)
    for s in range(rows):
        total = None
        for t in range(seqs):
            at = (s * seqs + t) * sites
            term = wide[at : at + sites, :] * values[t]
            total = term if total is None else total + term
        mixed[s * sites : (s + 1) * sites, :] = total
    out = hidden_ref[...] + dot_nn(mixed[...].astype(BF16), closing_ref[...])
    out_ref[...] = out.reshape(rows, sites, embed).astype(BF16)


def column_kernel(head, factor, query_ref, kv_ref, *refs):
    rows, sites, embed = refs[2].shape
    kv = kv_ref[...].astype(F32)
    seqs = kv.shape[0] // sites
    keys = [kv[t * sites : (t + 1) * sites, 0:embed] for t in range(seqs)]
    values = [kv[t * sites : (t + 1) * sites, embed:] for t in range(seqs)]
    column_attend(head, factor, query_ref[...].astype(F32), keys, values, *refs)


def swapped_column_kernel(head, factor, own_ref, other_ref, *refs):
    rows, sites, embed = refs[2].shape
    cells, columns = own_ref.shape
    half = cells // 2

    def piece(first_is_own, start, stop, at, size):
        found = []
        for block in range(2):
            lo, hi = max(start, block * columns), min(stop, (block + 1) * columns)
            if lo < hi:
                cols = slice(lo - block * columns, hi - block * columns)
                if (block == 0) == first_is_own:
                    found.append(own_ref[at : at + size, cols])
                else:
                    turned = (at + half) % cells
                    found.append(other_ref[turned : turned + size, cols])
        return jnp.concatenate(found, axis=1).astype(F32)

    def attend(first_is_own):
        query = piece(first_is_own, 0, embed, 0, half)
        keys, values = [], []
        for at in (0, half):
            key = piece(first_is_own, embed, 2 * embed, at, half)
            value = piece(first_is_own, 2 * embed, 3 * embed, at, half)
            for t in range(half // sites):
                keys.append(key[t * sites : (t + 1) * sites, :])
                values.append(value[t * sites : (t + 1) * sites, :])
        column_attend(head, factor, query, keys, values, *refs)

    seq_index = lax.axis_index("seq")
    pl.when(seq_index == 0)(functools.partial(attend, True))
    pl.when(seq_index == 1)(functools.partial(attend, False))


def contact_kernel(heads, pair_ref, factor_ref, own_ref, slab_ref, out_ref, held):
    count, step, length = pair_ref.shape
    head_rows = round_up(heads, 8)
    sites = step - head_rows
    blocks = slab_ref.shape[1] // sites
    total = pair_ref[0, 0:head_rows, :]
    for n in range(1, count):
        total = total + pair_ref[n, 0:head_rows, :]
    held[0:head_rows, :] = total
    held[head_rows:step, :] = pair_ref[lax.axis_index("pos"), head_rows:step, :]
    first = lax.axis_index("seq") * blocks
    table = jnp.concatenate(
        [pair_ref[first + n, head_rows:step, :] for n in range(blocks)], axis=0
    )
    amount = jnp.sum(total, axis=1, keepdims=True)
    real = lax.broadcasted_iota(jnp.int32, (head_rows, 1), 0) < heads
    share = jnp.where(real, factor_ref[0:head_rows, 0:1] / jnp.where(real, amount, 1.0), 0.0)
    slab = dot_nn(held[...], slab_ref[...], HIGHEST)
    own = dot_nt(own_ref[...], total * share, HIGHEST)
    mirrored = dot_nt(own_ref[...], table, HIGHEST)
    adjuster = dot_nn(own, slab[0:head_rows, :], HIGHEST)
    out_ref[...] = jax.nn.sigmoid(
        slab[head_rows:step, :] + mirrored - adjuster + factor_ref[head_rows : head_rows + 1, 0:1]
    )


def call(kernel, out_shape, operands, smem=(), hbm=(), scratch=(), bytes_accessed=1000000):
    vmem = pl.BlockSpec(memory_space=pltpu.VMEM)
    held = sum(math.prod(a.shape) * a.dtype.itemsize for a in [*operands, *jax.tree.leaves(out_shape)])
    held += sum(
        math.prod(a.shape) * np.dtype(a.dtype).itemsize
        for a in scratch
        if a.memory_space == pltpu.VMEM
    )
    limit = 2 * held + 4 * 1024 * 1024
    specs = [
        pl.BlockSpec(memory_space=pltpu.SMEM if i in smem else pl.ANY if i in hbm else pltpu.VMEM)
        for i in range(len(operands))
    ]
    return pl.pallas_call(
        kernel,
        out_shape=out_shape,
        in_specs=specs,
        out_specs=jax.tree.map(lambda _: vmem, out_shape),
        scratch_shapes=list(scratch),
        compiler_params=pltpu.CompilerParams(vmem_limit_bytes=limit),
        cost_estimate=pl.CostEstimate(
            flops=1000000, bytes_accessed=bytes_accessed, transcendentals=0
        ),
    )(*operands)


def stages_of(count):
    stages, stride = [], 1
    while count > 1 and len(stages) < 2 and count % 2 == 0:
        stages.append((stride, 2))
        stride, count = stride * 2, count // 2
    if count > 1:
        stages.append((stride, count))
    return stages[::-1]


def send_pos(array, count, stride, size, delta):
    pairs = []
    for p in range(count):
        a = (p // stride) % size
        pairs.append((p, p + ((a + delta) % size - a) * stride))
    return lax.ppermute(array, "pos", pairs)


def send_all(parts, count, stage):
    stride, size = stage
    return [send_pos(part, count, stride, size, delta) for delta in range(1, size) for part in parts]


def after(array, *others):
    return lax.optimization_barrier((array, *others))[0]


def per_device(
    skip_stream_input,
    lateral_asking_vectors,
    lateral_matched_vectors,
    lateral_carried_vectors,
    lateral_closing_linear,
    upright_normalizer_multiplier,
    upright_threefold_linear,
    upright_closing_linear,
    regression_factors,
    regression_offset,
):
    rows, sites, embed = lateral_asking_vectors.shape
    heads = regression_factors.shape[0]
    head = embed // heads
    seq_count = lax.axis_size("seq")
    pos_count = lax.axis_size("pos")
    length = sites * pos_count
    slab_width = length // seq_count
    cells = rows * sites
    pos_index = lax.axis_index("pos").astype(jnp.int32)
    seq_index = lax.axis_index("seq").astype(jnp.int32)
    swap = [(s, 1 - s) for s in range(2)]
    columns = upright_threefold_linear.shape[1]
    swapped = seq_count == 2 and columns % 128 == 0

    stages = stages_of(pos_count)
    outer = stages[0]
    middle = stages[1] if len(stages) > 1 else None

    scalars = jnp.stack([seq_index, pos_index])
    head_rows = round_up(heads, 8)
    width = lane_block(embed, head)
    key_first = [lateral_matched_vectors] + send_all([lateral_matched_vectors], pos_count, outer)
    key_parts = [jnp.concatenate(key_first, axis=1)]
    value_first = [after(lateral_carried_vectors, key_parts[0])]
    value_first += send_all([lateral_carried_vectors], pos_count, outer)
    masked = call(
        functools.partial(query_kernel, head),
        jax.ShapeDtypeStruct((rows, heads * sites, width), BF16),
        [after(lateral_asking_vectors, key_parts[0])],
        hbm=(0,),
        scratch=[pltpu.VMEM((rows, sites, embed), BF16), pltpu.SemaphoreType.DMA((1,))],
    )
    if middle:
        key_parts += send_all(key_parts, pos_count, middle)
    near = sum(part.shape[1] for part in key_parts)
    partial = call(
        functools.partial(logits_kernel, len(key_parts)),
        jax.ShapeDtypeStruct((heads * sites, near), F32),
        [masked, *key_parts],
    )
    value_first[1] = after(value_first[1], masked)
    value_parts = [jnp.concatenate(value_first, axis=1)]
    if middle:
        value_parts += send_all(value_parts, pos_count, middle)
    if len(stages) > 2:
        far_parts = send_all(key_parts, pos_count, stages[2])
        partial = call(
            functools.partial(logits_kernel, len(far_parts)),
            jax.ShapeDtypeStruct((heads * sites, length), F32),
            [masked, *far_parts, partial],
        )
    head_factors, order, own_select, slab_select = call(
        functools.partial(prepare_kernel, heads, sites, stages),
        (
            jax.ShapeDtypeStruct((head_rows + 8, 128), F32),
            jax.ShapeDtypeStruct((length, length), F32),
            jax.ShapeDtypeStruct((sites, length), F32),
            jax.ShapeDtypeStruct((length, slab_width), F32),
        ),
        [after(scalars, partial), regression_factors, regression_offset],
        smem=(0, 1, 2),
    )
    if seq_count == 2:
        partials = [partial, after(lax.ppermute(partial, "seq", swap), order)]
    else:
        partials = [lax.psum(partial, "seq")]
    shares = call(
        functools.partial(
            softmax_kernel, 1.0 / (math.sqrt(head) * math.sqrt(rows * seq_count))
        ),
        jax.ShapeDtypeStruct((heads * sites, length), BF16),
        partials,
    )

    pair_local = call(
        functools.partial(pair_kernel, heads),
        jax.ShapeDtypeStruct((pos_count, head_rows + sites, length), F32),
        [shares, head_factors, order],
        scratch=[pltpu.VMEM((head_rows + sites, length), F32)],
    )
    if len(stages) > 2:
        value_parts = value_parts[:1] + [after(part, pair_local) for part in value_parts[1:]]
        value_parts += send_all(value_parts, pos_count, stages[2])
    hidden, normed = call(
        functools.partial(mix_kernel, head, len(value_parts)),
        (
            jax.ShapeDtypeStruct((cells, embed), F32),
            jax.ShapeDtypeStruct((cells, embed), BF16),
        ),
        [
            shares,
            *value_parts,
            lateral_closing_linear,
            skip_stream_input,
            upright_normalizer_multiplier,
        ],
        scratch=[pltpu.VMEM((cells, embed), F32)],
    )
    pair_all = lax.all_to_all(pair_local, "pos", split_axis=0, concat_axis=0, tiled=True)
    pairing_chances = call(
        functools.partial(contact_kernel, heads),
        jax.ShapeDtypeStruct((sites, slab_width), F32),
        [pair_all, head_factors, own_select, slab_select],
        scratch=[pltpu.VMEM((head_rows + sites, length), F32)],
    )
    if swapped:
        normed_all = [normed, lax.ppermute(normed, "seq", swap)]
        weight = after(upright_threefold_linear, normed)
    else:
        normed_all = [normed]
        weight = lax.all_gather(upright_threefold_linear, "seq", axis=1, tiled=True)
    projected = call(
        functools.partial(project_kernel, len(normed_all)),
        jax.ShapeDtypeStruct((cells * len(normed_all), weight.shape[1]), BF16),
        [*normed_all, weight],
    )
    if swapped:
        column, column_inputs = swapped_column_kernel, [
            projected,
            lax.ppermute(projected, "seq", swap),
        ]
    else:
        key_value = lax.all_gather(projected[:, embed:], "seq", axis=0, tiled=True)
        column, column_inputs = column_kernel, [projected[:, :embed], key_value]
    alignment_output = call(
        functools.partial(column, head, 1.0 / math.sqrt(head)),
        jax.ShapeDtypeStruct((rows, sites, embed), BF16),
        [
            *column_inputs,
            after(hidden, pairing_chances),
            after(upright_closing_linear, projected),
        ],
        scratch=[
            pltpu.VMEM((cells * rows * seq_count, embed), F32),
            pltpu.VMEM((cells, embed), F32),
        ],
    )
    return alignment_output, pairing_chances


def solution(mesh):
    cells = P("seq", "pos", None)
    return jax.shard_map(
        per_device,
        mesh=mesh,
        in_specs=(cells, cells, cells, cells, P(), P(), P(None, "seq"), P(), P(), P()),
        out_specs=(cells, P("pos", "seq")),
        check_vma=False,
    )
```

```python
import functools
import math

import jax
import jax.numpy as jnp
import numpy as np
from jax import lax
from jax.experimental import pallas as pl
from jax.experimental.pallas import tpu as pltpu
from jax.sharding import PartitionSpec as P

F32 = jnp.float32
BF16 = jnp.bfloat16
HIGHEST = lax.Precision.HIGHEST
LANE_BLOCK = 256


def dot_nn(a, b, precision=None):
    return lax.dot_general(
        a, b, (((1,), (0,)), ((), ())), precision=precision, preferred_element_type=F32
    )


def dot_nt(a, b, precision=None):
    return lax.dot_general(
        a, b, (((1,), (1,)), ((), ())), precision=precision, preferred_element_type=F32
    )


def round_up(n, m):
    return -(-n // m) * m


def lane_block(embed, head):
    return LANE_BLOCK if embed % LANE_BLOCK == 0 and LANE_BLOCK % head == 0 else head


def arrival_place(index, column, stages, sites):
    block, place, span = column // sites, column % sites, 1
    for stride, size in stages:
        digit = (block // span) % size
        place = place + ((index // stride) % size + size - digit) % size * (stride * sites)
        span *= size
    return place


def fetch(pairs, sems):
    copies = [pltpu.make_async_copy(src, dst, sems.at[i]) for i, (src, dst) in enumerate(pairs)]
    for copy in copies:
        copy.start()
    for copy in copies:
        copy.wait()


def query_kernel(head, q_hbm, masked_ref, q_ref, sems):
    rows, sites, embed = q_ref.shape
    width = masked_ref.shape[2]
    group = width // head
    span = group * sites
    fetch([(q_hbm, q_ref)], sems)
    lane_head = lax.broadcasted_iota(jnp.int32, (span, width), 1) // head
    row_head = lax.broadcasted_iota(jnp.int32, (span, width), 0) // sites
    own_head = lane_head == row_head
    for block in range(embed // width):
        for r in range(rows):
            q = q_ref[r, :, block * width : (block + 1) * width].astype(F32)
            q = jnp.where(own_head, jnp.concatenate([q] * group, axis=0), 0.0).astype(BF16)
            masked_ref[r, block * span : (block + 1) * span, :] = q


def prepare_kernel(heads, sites, stages, scalar_ref, factor_ref, offset_ref, *refs):
    head_ref, order_ref, own_ref, slab_ref = refs
    row = lax.broadcasted_iota(jnp.int32, head_ref.shape, 0)
    factors = jnp.zeros(head_ref.shape, F32)
    for h in range(heads):
        factors = jnp.where(row == h, factor_ref[h], factors)
    head_ref[...] = jnp.where(row == round_up(heads, 8), offset_ref[0], factors)
    seq_index, pos_index = scalar_ref[0], scalar_ref[1]
    length = order_ref.shape[0]
    row = lax.broadcasted_iota(jnp.int32, (length, length), 0)
    lane = lax.broadcasted_iota(jnp.int32, (length, length), 1)
    order_ref[...] = (arrival_place(pos_index, row, stages, sites) == lane).astype(F32)
    row = lax.broadcasted_iota(jnp.int32, own_ref.shape, 0)
    lane = lax.broadcasted_iota(jnp.int32, own_ref.shape, 1)
    own_ref[...] = (row + pos_index * sites == lane).astype(F32)
    row = lax.broadcasted_iota(jnp.int32, slab_ref.shape, 0)
    lane = lax.broadcasted_iota(jnp.int32, slab_ref.shape, 1)
    slab_ref[...] = (row == lane + seq_index * slab_ref.shape[1]).astype(F32)


def logits_kernel(part_count, *refs):
    q_ref, k_refs, done_refs, out_ref = refs[0], refs[1 : 1 + part_count], refs[1 + part_count : -1], refs[-1]
    rows, _, width = q_ref.shape
    blocks = k_refs[0].shape[2] // width
    span = q_ref.shape[1] // blocks
    for block in range(blocks):
        cols = slice(block * width, (block + 1) * width)
        lines = slice(block * span, (block + 1) * span)
        total = None
        for r in range(rows):
            keys = jnp.concatenate([k[r, :, cols] for k in k_refs], axis=0)
            term = dot_nt(q_ref[r, lines, :], keys)
            total = term if total is None else total + term
        out_ref[lines, :] = jnp.concatenate([done[lines, :] for done in done_refs] + [total], axis=1)


def softmax_kernel(factor, *refs):
    parts, w_ref = refs[:-1], refs[-1]
    logits = parts[0][...]
    for part in parts[1:]:
        logits = logits + part[...]
    logits = logits * factor
    exponent = jnp.exp(logits - jnp.max(logits, axis=1, keepdims=True))
    shares = (exponent / jnp.sum(exponent, axis=1, keepdims=True)).astype(BF16)
    w_ref[...] = shares


def pair_kernel(heads, w_ref, head_ref, order_ref, pair_ref, held):
    rows, length = w_ref.shape
    sites = rows // heads
    shares = w_ref[...].astype(F32)
    row_sum = jnp.sum(shares, axis=1, keepdims=True)
    lane = lax.broadcasted_iota(jnp.int32, (rows, length), 1)
    row = lax.broadcasted_iota(jnp.int32, (rows, length), 0) % sites
    both = (shares + jnp.where(lane == row, row_sum, 0.0)).reshape(heads, sites, length)
    head_rows = round_up(heads, 8)
    held[...] = jnp.zeros_like(held)
    held[0:heads, :] = jnp.sum(both, axis=1)
    merged = None
    for h in range(heads):
        term = shares[h * sites : (h + 1) * sites, :] * head_ref[h : h + 1, 0:1]
        merged = term if merged is None else merged + term
    held[head_rows : head_rows + sites, :] = merged
    pair_ref[...] = jnp.broadcast_to(
        dot_nn(held[...], order_ref[...], HIGHEST)[None], pair_ref.shape
    )


def mix_kernel(head, v_count, *refs):
    w_ref, v_refs = refs[0], refs[1 : 1 + v_count]
    closing_ref, skip_ref, gain_ref, hidden_ref, normed_ref, mixed = refs[1 + v_count :]
    rows, sites, embed = skip_ref.shape
    width = lane_block(embed, head)
    group = width // head
    lane_head = lax.broadcasted_iota(jnp.int32, (sites, width), 1) // head
    for block in range(embed // width):
        cols = slice(block * width, (block + 1) * width)
        shares = w_ref[block * group * sites : (block + 1) * group * sites, :]
        for r in range(rows):
            values = jnp.concatenate([v[r, :, cols] for v in v_refs], axis=0)
            product = dot_nn(shares, values)
            own = product[0:sites, :]
            for g in range(1, group):
                own = jnp.where(lane_head == g, product[g * sites : (g + 1) * sites, :], own)
            mixed[r * sites : (r + 1) * sites, cols] = own
    hidden = skip_ref[...].astype(F32).reshape(rows * sites, embed) + dot_nn(mixed[...].astype(BF16), closing_ref[...])
    hidden_ref[...] = hidden
    centered = hidden - jnp.mean(hidden, axis=1, keepdims=True)
    spread = jnp.mean(centered * centered, axis=1, keepdims=True)
    normed_ref[...] = (centered * lax.rsqrt(spread + 1e-05) * gain_ref[...].reshape(1, embed)).astype(BF16)


def project_kernel(part_count, *refs):
    parts, (weight_ref, out_ref) = refs[:part_count], refs[part_count:]
    normed = jnp.concatenate([part[...] for part in parts], axis=0)
    out_ref[...] = dot_nn(normed, weight_ref[...]).astype(BF16)


def column_attend(head, factor, query, keys, values, hidden_ref, closing_ref, out_ref, products, mixed):
    rows, sites, embed = out_ref.shape
    padded = round_up(embed // head, 128)
    pick = (
        lax.broadcasted_iota(jnp.int32, (embed, padded), 0) // head
        == lax.broadcasted_iota(jnp.int32, (embed, padded), 1)
    ).astype(BF16)
    spread = (
        lax.broadcasted_iota(jnp.int32, (padded, embed), 1) // head
        == lax.broadcasted_iota(jnp.int32, (padded, embed), 0)
    ).astype(BF16)
    seqs = len(keys)
    for s in range(rows):
        for t in range(seqs):
            at = (s * seqs + t) * sites
            products[at : at + sites, :] = query[s * sites : (s + 1) * sites, :] * keys[t]
    product = products[...]
    high = product.astype(BF16)
    low = (product - high.astype(F32)).astype(BF16)
    scores = (dot_nn(high, pick) + dot_nn(low, pick)) * factor
    exponent = jnp.exp(scores).reshape(rows, seqs, sites, padded)
    shares = (exponent / jnp.sum(exponent, axis=1, keepdims=True)).astype(BF16)
    wide = dot_nn(shares.reshape(rows * seqs * sites, padded), spread)
    for s in range(rows):
        total = None
        for t in range(seqs):
            at = (s * seqs + t) * sites
            term = wide[at : at + sites, :] * values[t]
            total = term if total is None else total + term
        mixed[s * sites : (s + 1) * sites, :] = total
    out = hidden_ref[...] + dot_nn(mixed[...].astype(BF16), closing_ref[...])
    out_ref[...] = out.reshape(rows, sites, embed).astype(BF16)


def column_kernel(head, factor, query_ref, kv_ref, *refs):
    rows, sites, embed = refs[2].shape
    kv = kv_ref[...].astype(F32)
    seqs = kv.shape[0] // sites
    keys = [kv[t * sites : (t + 1) * sites, 0:embed] for t in range(seqs)]
    values = [kv[t * sites : (t + 1) * sites, embed:] for t in range(seqs)]
    column_attend(head, factor, query_ref[...].astype(F32), keys, values, *refs)


def swapped_column_kernel(head, factor, own_ref, other_ref, *refs):
    rows, sites, embed = refs[2].shape
    cells, columns = own_ref.shape
    half = cells // 2

    def piece(first_is_own, start, stop, at, size):
        found = []
        for block in range(2):
            lo, hi = max(start, block * columns), min(stop, (block + 1) * columns)
            if lo < hi:
                cols = slice(lo - block * columns, hi - block * columns)
                if (block == 0) == first_is_own:
                    found.append(own_ref[at : at + size, cols])
                else:
                    turned = (at + half) % cells
                    found.append(other_ref[turned : turned + size, cols])
        return jnp.concatenate(found, axis=1).astype(F32)

    def attend(first_is_own):
        query = piece(first_is_own, 0, embed, 0, half)
        keys, values = [], []
        for at in (0, half):
            key = piece(first_is_own, embed, 2 * embed, at, half)
            value = piece(first_is_own, 2 * embed, 3 * embed, at, half)
            for t in range(half // sites):
                keys.append(key[t * sites : (t + 1) * sites, :])
                values.append(value[t * sites : (t + 1) * sites, :])
        column_attend(head, factor, query, keys, values, *refs)

    seq_index = lax.axis_index("seq")
    pl.when(seq_index == 0)(functools.partial(attend, True))
    pl.when(seq_index == 1)(functools.partial(attend, False))


def contact_kernel(heads, pair_ref, factor_ref, own_ref, slab_ref, out_ref, held):
    count, step, length = pair_ref.shape
    head_rows = round_up(heads, 8)
    sites = step - head_rows
    blocks = slab_ref.shape[1] // sites
    total = pair_ref[0, 0:head_rows, :]
    for n in range(1, count):
        total = total + pair_ref[n, 0:head_rows, :]
    held[0:head_rows, :] = total
    held[head_rows:step, :] = pair_ref[lax.axis_index("pos"), head_rows:step, :]
    first = lax.axis_index("seq") * blocks
    table = jnp.concatenate(
        [pair_ref[first + n, head_rows:step, :] for n in range(blocks)], axis=0
    )
    amount = jnp.sum(total, axis=1, keepdims=True)
    real = lax.broadcasted_iota(jnp.int32, (head_rows, 1), 0) < heads
    share = jnp.where(real, factor_ref[0:head_rows, 0:1] / jnp.where(real, amount, 1.0), 0.0)
    slab = dot_nn(held[...], slab_ref[...], HIGHEST)
    own = dot_nt(own_ref[...], total * share, HIGHEST)
    mirrored = dot_nt(own_ref[...], table, HIGHEST)
    adjuster = dot_nn(own, slab[0:head_rows, :], HIGHEST)
    out_ref[...] = jax.nn.sigmoid(
        slab[head_rows:step, :] + mirrored - adjuster + factor_ref[head_rows : head_rows + 1, 0:1]
    )


def call(kernel, out_shape, operands, smem=(), hbm=(), scratch=(), bytes_accessed=1000000):
    vmem = pl.BlockSpec(memory_space=pltpu.VMEM)
    held = sum(math.prod(a.shape) * a.dtype.itemsize for a in [*operands, *jax.tree.leaves(out_shape)])
    held += sum(
        math.prod(a.shape) * np.dtype(a.dtype).itemsize
        for a in scratch
        if a.memory_space == pltpu.VMEM
    )
    limit = 2 * held + 4 * 1024 * 1024
    specs = [
        pl.BlockSpec(memory_space=pltpu.SMEM if i in smem else pl.ANY if i in hbm else pltpu.VMEM)
        for i in range(len(operands))
    ]
    return pl.pallas_call(
        kernel,
        out_shape=out_shape,
        in_specs=specs,
        out_specs=jax.tree.map(lambda _: vmem, out_shape),
        scratch_shapes=list(scratch),
        compiler_params=pltpu.CompilerParams(vmem_limit_bytes=limit),
        cost_estimate=pl.CostEstimate(
            flops=1000000, bytes_accessed=bytes_accessed, transcendentals=0
        ),
    )(*operands)


def stages_of(count):
    stages, stride = [], 1
    while count > 1 and len(stages) < 2 and count % 2 == 0:
        stages.append((stride, 2))
        stride, count = stride * 2, count // 2
    if count > 1:
        stages.append((stride, count))
    return stages[::-1]


def send_pos(array, count, stride, size, delta):
    pairs = []
    for p in range(count):
        a = (p // stride) % size
        pairs.append((p, p + ((a + delta) % size - a) * stride))
    return lax.ppermute(array, "pos", pairs)


def send_all(parts, count, stage):
    stride, size = stage
    return [send_pos(part, count, stride, size, delta) for delta in range(1, size) for part in parts]


def after(array, *others):
    return lax.optimization_barrier((array, *others))[0]


def per_device(
    skip_stream_input,
    lateral_asking_vectors,
    lateral_matched_vectors,
    lateral_carried_vectors,
    lateral_closing_linear,
    upright_normalizer_multiplier,
    upright_threefold_linear,
    upright_closing_linear,
    regression_factors,
    regression_offset,
):
    rows, sites, embed = lateral_asking_vectors.shape
    heads = regression_factors.shape[0]
    head = embed // heads
    seq_count = lax.axis_size("seq")
    pos_count = lax.axis_size("pos")
    length = sites * pos_count
    slab_width = length // seq_count
    cells = rows * sites
    pos_index = lax.axis_index("pos").astype(jnp.int32)
    seq_index = lax.axis_index("seq").astype(jnp.int32)
    swap = [(s, 1 - s) for s in range(2)]
    columns = upright_threefold_linear.shape[1]
    swapped = seq_count == 2 and columns % 128 == 0

    stages = stages_of(pos_count)
    outer = stages[0]
    middle = stages[1] if len(stages) > 1 else None

    scalars = jnp.stack([seq_index, pos_index])
    head_rows = round_up(heads, 8)
    width = lane_block(embed, head)
    key_first = [lateral_matched_vectors] + send_all([lateral_matched_vectors], pos_count, outer)
    key_parts = [jnp.concatenate(key_first, axis=1)]
    value_first = [after(lateral_carried_vectors, key_parts[0])]
    value_first += send_all([lateral_carried_vectors], pos_count, outer)
    masked = call(
        functools.partial(query_kernel, head),
        jax.ShapeDtypeStruct((rows, heads * sites, width), BF16),
        [after(lateral_asking_vectors, key_parts[0])],
        hbm=(0,),
        scratch=[pltpu.VMEM((rows, sites, embed), BF16), pltpu.SemaphoreType.DMA((1,))],
    )
    if middle:
        key_parts += send_all(key_parts, pos_count, middle)
    near = sum(part.shape[1] for part in key_parts)
    partial = call(
        functools.partial(logits_kernel, len(key_parts)),
        jax.ShapeDtypeStruct((heads * sites, near), F32),
        [masked, *key_parts],
    )
    value_first[1] = after(value_first[1], masked)
    value_parts = [jnp.concatenate(value_first, axis=1)]
    if middle:
        value_parts += send_all(value_parts, pos_count, middle)
    if len(stages) > 2:
        far_parts = send_all(key_parts, pos_count, stages[2])
        partial = call(
            functools.partial(logits_kernel, len(far_parts)),
            jax.ShapeDtypeStruct((heads * sites, length), F32),
            [masked, *far_parts, partial],
        )
    head_factors, order, own_select, slab_select = call(
        functools.partial(prepare_kernel, heads, sites, stages),
        (
            jax.ShapeDtypeStruct((head_rows + 8, 128), F32),
            jax.ShapeDtypeStruct((length, length), F32),
            jax.ShapeDtypeStruct((sites, length), F32),
            jax.ShapeDtypeStruct((length, slab_width), F32),
        ),
        [after(scalars, partial), regression_factors, regression_offset],
        smem=(0, 1, 2),
    )
    if seq_count == 2:
        partials = [partial, after(lax.ppermute(partial, "seq", swap), order)]
    else:
        partials = [lax.psum(partial, "seq")]
    shares = call(
        functools.partial(
            softmax_kernel, 1.0 / (math.sqrt(head) * math.sqrt(rows * seq_count))
        ),
        jax.ShapeDtypeStruct((heads * sites, length), BF16),
        partials,
    )

    pair_local = call(
        functools.partial(pair_kernel, heads),
        jax.ShapeDtypeStruct((pos_count, head_rows + sites, length), F32),
        [shares, head_factors, order],
        scratch=[pltpu.VMEM((head_rows + sites, length), F32)],
    )
    if len(stages) > 2:
        value_parts = value_parts[:1] + [after(part, pair_local) for part in value_parts[1:]]
        value_parts += send_all(value_parts, pos_count, stages[2])
    hidden, normed = call(
        functools.partial(mix_kernel, head, len(value_parts)),
        (
            jax.ShapeDtypeStruct((cells, embed), F32),
            jax.ShapeDtypeStruct((cells, embed), BF16),
        ),
        [
            shares,
            *value_parts,
            lateral_closing_linear,
            skip_stream_input,
            upright_normalizer_multiplier,
        ],
        scratch=[pltpu.VMEM((cells, embed), F32)],
    )
    pair_all = lax.all_to_all(pair_local, "pos", split_axis=0, concat_axis=0, tiled=True)
    pairing_chances = call(
        functools.partial(contact_kernel, heads),
        jax.ShapeDtypeStruct((sites, slab_width), F32),
        [pair_all, head_factors, own_select, slab_select],
        scratch=[pltpu.VMEM((head_rows + sites, length), F32)],
    )
    if swapped:
        normed_all = [normed, lax.ppermute(normed, "seq", swap)]
        weight = after(upright_threefold_linear, normed)
    else:
        normed_all = [normed]
        weight = lax.all_gather(upright_threefold_linear, "seq", axis=1, tiled=True)
    projected = call(
        functools.partial(project_kernel, len(normed_all)),
        jax.ShapeDtypeStruct((cells * len(normed_all), weight.shape[1]), BF16),
        [*normed_all, weight],
    )
    if swapped:
        column, column_inputs = swapped_column_kernel, [
            projected,
            lax.ppermute(projected, "seq", swap),
        ]
    else:
        key_value = lax.all_gather(projected[:, embed:], "seq", axis=0, tiled=True)
        column, column_inputs = column_kernel, [projected[:, :embed], key_value]
    alignment_output = call(
        functools.partial(column, head, 1.0 / math.sqrt(head)),
        jax.ShapeDtypeStruct((rows, sites, embed), BF16),
        [
            *column_inputs,
            hidden,
            after(upright_closing_linear, projected),
        ],
        scratch=[
            pltpu.VMEM((cells * rows * seq_count, embed), F32),
            pltpu.VMEM((cells, embed), F32),
        ],
    )
    return alignment_output, pairing_chances


def solution(mesh):
    cells = P("seq", "pos", None)
    return jax.shard_map(
        per_device,
        mesh=mesh,
        in_specs=(cells, cells, cells, cells, P(), P(), P(None, "seq"), P(), P(), P()),
        out_specs=(cells, P("pos", "seq")),
        check_vma=False,
    )
```

```python
import functools
import math

import jax
import jax.numpy as jnp
import numpy as np
from jax import lax
from jax.experimental import pallas as pl
from jax.experimental.pallas import tpu as pltpu
from jax.sharding import PartitionSpec as P

F32 = jnp.float32
BF16 = jnp.bfloat16
HIGHEST = lax.Precision.HIGHEST
LANE_BLOCK = 256


def dot_nn(a, b, precision=None):
    return lax.dot_general(
        a, b, (((1,), (0,)), ((), ())), precision=precision, preferred_element_type=F32
    )


def dot_nt(a, b, precision=None):
    return lax.dot_general(
        a, b, (((1,), (1,)), ((), ())), precision=precision, preferred_element_type=F32
    )


def round_up(n, m):
    return -(-n // m) * m


def lane_block(embed, head):
    return LANE_BLOCK if embed % LANE_BLOCK == 0 and LANE_BLOCK % head == 0 else head


def arrival_place(index, column, stages, sites):
    block, place, span = column // sites, column % sites, 1
    for stride, size in stages:
        digit = (block // span) % size
        place = place + ((index // stride) % size + size - digit) % size * (stride * sites)
        span *= size
    return place


def fetch(pairs, sems):
    copies = [pltpu.make_async_copy(src, dst, sems.at[i]) for i, (src, dst) in enumerate(pairs)]
    for copy in copies:
        copy.start()
    for copy in copies:
        copy.wait()


def query_kernel(head, q_hbm, masked_ref, q_ref, sems):
    rows, sites, embed = q_ref.shape
    width = masked_ref.shape[2]
    group = width // head
    span = group * sites
    fetch([(q_hbm, q_ref)], sems)
    lane_head = lax.broadcasted_iota(jnp.int32, (span, width), 1) // head
    row_head = lax.broadcasted_iota(jnp.int32, (span, width), 0) // sites
    own_head = lane_head == row_head
    for block in range(embed // width):
        for r in range(rows):
            q = q_ref[r, :, block * width : (block + 1) * width].astype(F32)
            q = jnp.where(own_head, jnp.concatenate([q] * group, axis=0), 0.0).astype(BF16)
            masked_ref[r, block * span : (block + 1) * span, :] = q


def prepare_kernel(heads, sites, stages, scalar_ref, factor_ref, offset_ref, *refs):
    head_ref, order_ref, own_ref, slab_ref = refs
    row = lax.broadcasted_iota(jnp.int32, head_ref.shape, 0)
    factors = jnp.zeros(head_ref.shape, F32)
    for h in range(heads):
        factors = jnp.where(row == h, factor_ref[h], factors)
    head_ref[...] = jnp.where(row == round_up(heads, 8), offset_ref[0], factors)
    seq_index, pos_index = scalar_ref[0], scalar_ref[1]
    length = order_ref.shape[0]
    row = lax.broadcasted_iota(jnp.int32, (length, length), 0)
    lane = lax.broadcasted_iota(jnp.int32, (length, length), 1)
    order_ref[...] = (arrival_place(pos_index, row, stages, sites) == lane).astype(F32)
    row = lax.broadcasted_iota(jnp.int32, own_ref.shape, 0)
    lane = lax.broadcasted_iota(jnp.int32, own_ref.shape, 1)
    own_ref[...] = (row + pos_index * sites == lane).astype(F32)
    row = lax.broadcasted_iota(jnp.int32, slab_ref.shape, 0)
    lane = lax.broadcasted_iota(jnp.int32, slab_ref.shape, 1)
    slab_ref[...] = (row == lane + seq_index * slab_ref.shape[1]).astype(F32)


def logits_kernel(part_count, *refs):
    q_ref, k_refs, done_refs, out_ref = refs[0], refs[1 : 1 + part_count], refs[1 + part_count : -1], refs[-1]
    rows, _, width = q_ref.shape
    blocks = k_refs[0].shape[2] // width
    span = q_ref.shape[1] // blocks
    for block in range(blocks):
        cols = slice(block * width, (block + 1) * width)
        lines = slice(block * span, (block + 1) * span)
        total = None
        for r in range(rows):
            keys = jnp.concatenate([k[r, :, cols] for k in k_refs], axis=0)
            term = dot_nt(q_ref[r, lines, :], keys)
            total = term if total is None else total + term
        out_ref[lines, :] = jnp.concatenate([done[lines, :] for done in done_refs] + [total], axis=1)


def softmax_kernel(factor, *refs):
    parts, w_ref = refs[:-1], refs[-1]
    logits = parts[0][...]
    for part in parts[1:]:
        logits = logits + part[...]
    logits = logits * factor
    exponent = jnp.exp(logits - jnp.max(logits, axis=1, keepdims=True))
    shares = (exponent / jnp.sum(exponent, axis=1, keepdims=True)).astype(BF16)
    w_ref[...] = shares


def pair_kernel(heads, w_ref, head_ref, order_ref, pair_ref, held):
    rows, length = w_ref.shape
    sites = rows // heads
    shares = w_ref[...].astype(F32)
    row_sum = jnp.sum(shares, axis=1, keepdims=True)
    lane = lax.broadcasted_iota(jnp.int32, (rows, length), 1)
    row = lax.broadcasted_iota(jnp.int32, (rows, length), 0) % sites
    both = (shares + jnp.where(lane == row, row_sum, 0.0)).reshape(heads, sites, length)
    head_rows = round_up(heads, 8)
    held[...] = jnp.zeros_like(held)
    held[0:heads, :] = jnp.sum(both, axis=1)
    merged = None
    for h in range(heads):
        term = shares[h * sites : (h + 1) * sites, :] * head_ref[h : h + 1, 0:1]
        merged = term if merged is None else merged + term
    held[head_rows : head_rows + sites, :] = merged
    pair_ref[...] = jnp.broadcast_to(
        dot_nn(held[...], order_ref[...], HIGHEST)[None], pair_ref.shape
    )


def mix_kernel(head, v_count, *refs):
    w_ref, v_refs = refs[0], refs[1 : 1 + v_count]
    closing_ref, skip_ref, gain_ref, hidden_ref, normed_ref, mixed = refs[1 + v_count :]
    rows, sites, embed = skip_ref.shape
    width = lane_block(embed, head)
    group = width // head
    lane_head = lax.broadcasted_iota(jnp.int32, (sites, width), 1) // head
    for block in range(embed // width):
        cols = slice(block * width, (block + 1) * width)
        shares = w_ref[block * group * sites : (block + 1) * group * sites, :]
        for r in range(rows):
            values = jnp.concatenate([v[r, :, cols] for v in v_refs], axis=0)
            product = dot_nn(shares, values)
            own = product[0:sites, :]
            for g in range(1, group):
                own = jnp.where(lane_head == g, product[g * sites : (g + 1) * sites, :], own)
            mixed[r * sites : (r + 1) * sites, cols] = own
    hidden = skip_ref[...].astype(F32).reshape(rows * sites, embed) + dot_nn(mixed[...].astype(BF16), closing_ref[...])
    hidden_ref[...] = hidden
    centered = hidden - jnp.mean(hidden, axis=1, keepdims=True)
    spread = jnp.mean(centered * centered, axis=1, keepdims=True)
    normed_ref[...] = (centered * lax.rsqrt(spread + 1e-05) * gain_ref[...].reshape(1, embed)).astype(BF16)


def project_kernel(part_count, *refs):
    parts, (weight_ref, out_ref) = refs[:part_count], refs[part_count:]
    normed = jnp.concatenate([part[...] for part in parts], axis=0)
    out_ref[...] = dot_nn(normed, weight_ref[...]).astype(BF16)


def column_attend(head, factor, query, keys, values, hidden_ref, closing_ref, out_ref, products, mixed):
    rows, sites, embed = out_ref.shape
    padded = round_up(embed // head, 128)
    pick = (
        lax.broadcasted_iota(jnp.int32, (embed, padded), 0) // head
        == lax.broadcasted_iota(jnp.int32, (embed, padded), 1)
    ).astype(BF16)
    spread = (
        lax.broadcasted_iota(jnp.int32, (padded, embed), 1) // head
        == lax.broadcasted_iota(jnp.int32, (padded, embed), 0)
    ).astype(BF16)
    seqs = len(keys)
    for s in range(rows):
        for t in range(seqs):
            at = (s * seqs + t) * sites
            products[at : at + sites, :] = query[s * sites : (s + 1) * sites, :] * keys[t]
    product = products[...]
    high = product.astype(BF16)
    low = (product - high.astype(F32)).astype(BF16)
    scores = (dot_nn(high, pick) + dot_nn(low, pick)) * factor
    exponent = jnp.exp(scores).reshape(rows, seqs, sites, padded)
    shares = (exponent / jnp.sum(exponent, axis=1, keepdims=True)).astype(BF16)
    wide = dot_nn(shares.reshape(rows * seqs * sites, padded), spread)
    for s in range(rows):
        total = None
        for t in range(seqs):
            at = (s * seqs + t) * sites
            term = wide[at : at + sites, :] * values[t]
            total = term if total is None else total + term
        mixed[s * sites : (s + 1) * sites, :] = total
    out = hidden_ref[...] + dot_nn(mixed[...].astype(BF16), closing_ref[...])
    out_ref[...] = out.reshape(rows, sites, embed).astype(BF16)


def column_kernel(head, factor, query_ref, kv_ref, *refs):
    rows, sites, embed = refs[2].shape
    kv = kv_ref[...].astype(F32)
    seqs = kv.shape[0] // sites
    keys = [kv[t * sites : (t + 1) * sites, 0:embed] for t in range(seqs)]
    values = [kv[t * sites : (t + 1) * sites, embed:] for t in range(seqs)]
    column_attend(head, factor, query_ref[...].astype(F32), keys, values, *refs)


def swapped_column_kernel(head, factor, own_ref, other_ref, *refs):
    rows, sites, embed = refs[2].shape
    cells, columns = own_ref.shape
    half = cells // 2

    def piece(first_is_own, start, stop, at, size):
        found = []
        for block in range(2):
            lo, hi = max(start, block * columns), min(stop, (block + 1) * columns)
            if lo < hi:
                cols = slice(lo - block * columns, hi - block * columns)
                if (block == 0) == first_is_own:
                    found.append(own_ref[at : at + size, cols])
                else:
                    turned = (at + half) % cells
                    found.append(other_ref[turned : turned + size, cols])
        return jnp.concatenate(found, axis=1).astype(F32)

    def attend(first_is_own):
        query = piece(first_is_own, 0, embed, 0, half)
        keys, values = [], []
        for at in (0, half):
            key = piece(first_is_own, embed, 2 * embed, at, half)
            value = piece(first_is_own, 2 * embed, 3 * embed, at, half)
            for t in range(half // sites):
                keys.append(key[t * sites : (t + 1) * sites, :])
                values.append(value[t * sites : (t + 1) * sites, :])
        column_attend(head, factor, query, keys, values, *refs)

    seq_index = lax.axis_index("seq")
    pl.when(seq_index == 0)(functools.partial(attend, True))
    pl.when(seq_index == 1)(functools.partial(attend, False))


def contact_kernel(heads, pair_ref, factor_ref, own_ref, slab_ref, out_ref, held):
    count, step, length = pair_ref.shape
    head_rows = round_up(heads, 8)
    sites = step - head_rows
    blocks = slab_ref.shape[1] // sites
    total = pair_ref[0, 0:head_rows, :]
    for n in range(1, count):
        total = total + pair_ref[n, 0:head_rows, :]
    held[0:head_rows, :] = total
    held[head_rows:step, :] = pair_ref[lax.axis_index("pos"), head_rows:step, :]
    first = lax.axis_index("seq") * blocks
    table = jnp.concatenate(
        [pair_ref[first + n, head_rows:step, :] for n in range(blocks)], axis=0
    )
    amount = jnp.sum(total, axis=1, keepdims=True)
    real = lax.broadcasted_iota(jnp.int32, (head_rows, 1), 0) < heads
    share = jnp.where(real, factor_ref[0:head_rows, 0:1] / jnp.where(real, amount, 1.0), 0.0)
    slab = dot_nn(held[...], slab_ref[...], HIGHEST)
    own = dot_nt(own_ref[...], total * share, HIGHEST)
    mirrored = dot_nt(own_ref[...], table, HIGHEST)
    adjuster = dot_nn(own, slab[0:head_rows, :], HIGHEST)
    out_ref[...] = jax.nn.sigmoid(
        slab[head_rows:step, :] + mirrored - adjuster + factor_ref[head_rows : head_rows + 1, 0:1]
    )


def call(kernel, out_shape, operands, smem=(), hbm=(), scratch=(), bytes_accessed=1000000):
    vmem = pl.BlockSpec(memory_space=pltpu.VMEM)
    held = sum(math.prod(a.shape) * a.dtype.itemsize for a in [*operands, *jax.tree.leaves(out_shape)])
    held += sum(
        math.prod(a.shape) * np.dtype(a.dtype).itemsize
        for a in scratch
        if a.memory_space == pltpu.VMEM
    )
    limit = 2 * held + 4 * 1024 * 1024
    specs = [
        pl.BlockSpec(memory_space=pltpu.SMEM if i in smem else pl.ANY if i in hbm else pltpu.VMEM)
        for i in range(len(operands))
    ]
    return pl.pallas_call(
        kernel,
        out_shape=out_shape,
        in_specs=specs,
        out_specs=jax.tree.map(lambda _: vmem, out_shape),
        scratch_shapes=list(scratch),
        compiler_params=pltpu.CompilerParams(vmem_limit_bytes=limit),
        cost_estimate=pl.CostEstimate(
            flops=1000000, bytes_accessed=bytes_accessed, transcendentals=0
        ),
    )(*operands)


def stages_of(count):
    stages, stride = [], 1
    while count > 1 and len(stages) < 2 and count % 2 == 0:
        stages.append((stride, 2))
        stride, count = stride * 2, count // 2
    if count > 1:
        stages.append((stride, count))
    return stages[::-1]


def send_pos(array, count, stride, size, delta):
    pairs = []
    for p in range(count):
        a = (p // stride) % size
        pairs.append((p, p + ((a + delta) % size - a) * stride))
    return lax.ppermute(array, "pos", pairs)


def send_all(parts, count, stage):
    stride, size = stage
    return [send_pos(part, count, stride, size, delta) for delta in range(1, size) for part in parts]


def after(array, *others):
    return lax.optimization_barrier((array, *others))[0]


def per_device(
    skip_stream_input,
    lateral_asking_vectors,
    lateral_matched_vectors,
    lateral_carried_vectors,
    lateral_closing_linear,
    upright_normalizer_multiplier,
    upright_threefold_linear,
    upright_closing_linear,
    regression_factors,
    regression_offset,
):
    rows, sites, embed = lateral_asking_vectors.shape
    heads = regression_factors.shape[0]
    head = embed // heads
    seq_count = lax.axis_size("seq")
    pos_count = lax.axis_size("pos")
    length = sites * pos_count
    slab_width = length // seq_count
    cells = rows * sites
    pos_index = lax.axis_index("pos").astype(jnp.int32)
    seq_index = lax.axis_index("seq").astype(jnp.int32)
    swap = [(s, 1 - s) for s in range(2)]
    columns = upright_threefold_linear.shape[1]
    swapped = seq_count == 2 and columns % 128 == 0

    stages = stages_of(pos_count)
    outer = stages[0]
    middle = stages[1] if len(stages) > 1 else None

    scalars = jnp.stack([seq_index, pos_index])
    head_rows = round_up(heads, 8)
    width = lane_block(embed, head)
    key_first = [lateral_matched_vectors] + send_all([lateral_matched_vectors], pos_count, outer)
    key_parts = [jnp.concatenate(key_first, axis=1)]
    value_first = [after(lateral_carried_vectors, key_parts[0])]
    value_first += send_all([lateral_carried_vectors], pos_count, outer)
    masked = call(
        functools.partial(query_kernel, head),
        jax.ShapeDtypeStruct((rows, heads * sites, width), BF16),
        [after(lateral_asking_vectors, key_parts[0])],
        hbm=(0,),
        scratch=[pltpu.VMEM((rows, sites, embed), BF16), pltpu.SemaphoreType.DMA((1,))],
    )
    if middle:
        key_parts += send_all(key_parts, pos_count, middle)
    near = sum(part.shape[1] for part in key_parts)
    partial = call(
        functools.partial(logits_kernel, len(key_parts)),
        jax.ShapeDtypeStruct((heads * sites, near), F32),
        [masked, *key_parts],
    )
    value_first[1] = after(value_first[1], masked)
    value_parts = [jnp.concatenate(value_first, axis=1)]
    if middle:
        value_parts += send_all(value_parts, pos_count, middle)
    if len(stages) > 2:
        far_parts = send_all(key_parts, pos_count, stages[2])
        partial = call(
            functools.partial(logits_kernel, len(far_parts)),
            jax.ShapeDtypeStruct((heads * sites, length), F32),
            [masked, *far_parts, partial],
        )
    head_factors, order, own_select, slab_select = call(
        functools.partial(prepare_kernel, heads, sites, stages),
        (
            jax.ShapeDtypeStruct((head_rows + 8, 128), F32),
            jax.ShapeDtypeStruct((length, length), F32),
            jax.ShapeDtypeStruct((sites, length), F32),
            jax.ShapeDtypeStruct((length, slab_width), F32),
        ),
        [after(scalars, partial), regression_factors, regression_offset],
        smem=(0, 1, 2),
    )
    if seq_count == 2:
        partials = [partial, after(lax.ppermute(partial, "seq", swap), order)]
    else:
        partials = [lax.psum(partial, "seq")]
    shares = call(
        functools.partial(
            softmax_kernel, 1.0 / (math.sqrt(head) * math.sqrt(rows * seq_count))
        ),
        jax.ShapeDtypeStruct((heads * sites, length), BF16),
        partials,
    )

    pair_local = call(
        functools.partial(pair_kernel, heads),
        jax.ShapeDtypeStruct((pos_count, head_rows + sites, length), F32),
        [shares, head_factors, order],
        scratch=[pltpu.VMEM((head_rows + sites, length), F32)],
    )
    if len(stages) > 2:
        value_parts = value_parts[:1] + [after(part, pair_local) for part in value_parts[1:]]
        value_parts += send_all(value_parts, pos_count, stages[2])
    hidden, normed = call(
        functools.partial(mix_kernel, head, len(value_parts)),
        (
            jax.ShapeDtypeStruct((cells, embed), F32),
            jax.ShapeDtypeStruct((cells, embed), BF16),
        ),
        [
            shares,
            *value_parts,
            lateral_closing_linear,
            skip_stream_input,
            upright_normalizer_multiplier,
        ],
        scratch=[pltpu.VMEM((cells, embed), F32)],
    )
    pair_all = lax.all_to_all(pair_local, "pos", split_axis=0, concat_axis=0, tiled=True)
    if swapped:
        normed_all = [normed, lax.ppermute(normed, "seq", swap)]
        weight = after(upright_threefold_linear, normed)
    else:
        normed_all = [normed]
        weight = lax.all_gather(upright_threefold_linear, "seq", axis=1, tiled=True)
    projected = call(
        functools.partial(project_kernel, len(normed_all)),
        jax.ShapeDtypeStruct((cells * len(normed_all), weight.shape[1]), BF16),
        [*normed_all, weight],
    )
    if swapped:
        column, column_inputs = swapped_column_kernel, [
            projected,
            lax.ppermute(projected, "seq", swap),
        ]
    else:
        key_value = lax.all_gather(projected[:, embed:], "seq", axis=0, tiled=True)
        column, column_inputs = column_kernel, [projected[:, :embed], key_value]
    alignment_output = call(
        functools.partial(column, head, 1.0 / math.sqrt(head)),
        jax.ShapeDtypeStruct((rows, sites, embed), BF16),
        [
            *column_inputs,
            hidden,
            after(upright_closing_linear, projected),
        ],
        scratch=[
            pltpu.VMEM((cells * rows * seq_count, embed), F32),
            pltpu.VMEM((cells, embed), F32),
        ],
    )
    pairing_chances = call(
        functools.partial(contact_kernel, heads),
        jax.ShapeDtypeStruct((sites, slab_width), F32),
        [pair_all, after(head_factors, alignment_output), own_select, slab_select],
        scratch=[pltpu.VMEM((head_rows + sites, length), F32)],
    )
    return alignment_output, pairing_chances


def solution(mesh):
    cells = P("seq", "pos", None)
    return jax.shard_map(
        per_device,
        mesh=mesh,
        in_specs=(cells, cells, cells, cells, P(), P(), P(None, "seq"), P(), P(), P()),
        out_specs=(cells, P("pos", "seq")),
        check_vma=False,
    )
```

```python
import functools
import math

import jax
import jax.numpy as jnp
import numpy as np
from jax import lax
from jax.experimental import pallas as pl
from jax.experimental.pallas import tpu as pltpu
from jax.sharding import PartitionSpec as P

F32 = jnp.float32
BF16 = jnp.bfloat16
HIGHEST = lax.Precision.HIGHEST
LANE_BLOCK = 256


def dot_nn(a, b, precision=None):
    return lax.dot_general(
        a, b, (((1,), (0,)), ((), ())), precision=precision, preferred_element_type=F32
    )


def dot_nt(a, b, precision=None):
    return lax.dot_general(
        a, b, (((1,), (1,)), ((), ())), precision=precision, preferred_element_type=F32
    )


def round_up(n, m):
    return -(-n // m) * m


def lane_block(embed, head):
    return LANE_BLOCK if embed % LANE_BLOCK == 0 and LANE_BLOCK % head == 0 else head


def arrival_place(index, column, stages, sites):
    block, place, span = column // sites, column % sites, 1
    for stride, size in stages:
        digit = (block // span) % size
        place = place + ((index // stride) % size + size - digit) % size * (stride * sites)
        span *= size
    return place


def fetch(pairs, sems):
    copies = [pltpu.make_async_copy(src, dst, sems.at[i]) for i, (src, dst) in enumerate(pairs)]
    for copy in copies:
        copy.start()
    for copy in copies:
        copy.wait()


def query_kernel(head, q_hbm, masked_ref, q_ref, sems):
    rows, sites, embed = q_ref.shape
    width = masked_ref.shape[2]
    group = width // head
    span = group * sites
    fetch([(q_hbm, q_ref)], sems)
    lane_head = lax.broadcasted_iota(jnp.int32, (span, width), 1) // head
    row_head = lax.broadcasted_iota(jnp.int32, (span, width), 0) // sites
    own_head = lane_head == row_head
    for block in range(embed // width):
        for r in range(rows):
            q = q_ref[r, :, block * width : (block + 1) * width].astype(F32)
            q = jnp.where(own_head, jnp.concatenate([q] * group, axis=0), 0.0).astype(BF16)
            masked_ref[r, block * span : (block + 1) * span, :] = q


def prepare_kernel(heads, sites, stages, scalar_ref, factor_ref, offset_ref, *refs):
    head_ref, order_ref, own_ref, slab_ref, pick_ref, spread_ref = refs
    head = pick_ref.shape[0] // heads
    row = lax.broadcasted_iota(jnp.int32, pick_ref.shape, 0)
    lane = lax.broadcasted_iota(jnp.int32, pick_ref.shape, 1)
    pick_ref[...] = (row // head == lane).astype(BF16)
    row = lax.broadcasted_iota(jnp.int32, spread_ref.shape, 0)
    lane = lax.broadcasted_iota(jnp.int32, spread_ref.shape, 1)
    spread_ref[...] = (lane // head == row).astype(BF16)
    row = lax.broadcasted_iota(jnp.int32, head_ref.shape, 0)
    factors = jnp.zeros(head_ref.shape, F32)
    for h in range(heads):
        factors = jnp.where(row == h, factor_ref[h], factors)
    head_ref[...] = jnp.where(row == round_up(heads, 8), offset_ref[0], factors)
    seq_index, pos_index = scalar_ref[0], scalar_ref[1]
    length = order_ref.shape[0]
    row = lax.broadcasted_iota(jnp.int32, (length, length), 0)
    lane = lax.broadcasted_iota(jnp.int32, (length, length), 1)
    order_ref[...] = (arrival_place(pos_index, row, stages, sites) == lane).astype(F32)
    row = lax.broadcasted_iota(jnp.int32, own_ref.shape, 0)
    lane = lax.broadcasted_iota(jnp.int32, own_ref.shape, 1)
    own_ref[...] = (row + pos_index * sites == lane).astype(F32)
    row = lax.broadcasted_iota(jnp.int32, slab_ref.shape, 0)
    lane = lax.broadcasted_iota(jnp.int32, slab_ref.shape, 1)
    slab_ref[...] = (row == lane + seq_index * slab_ref.shape[1]).astype(F32)


def logits_kernel(part_count, *refs):
    q_ref, k_refs, done_refs, out_ref = refs[0], refs[1 : 1 + part_count], refs[1 + part_count : -1], refs[-1]
    rows, _, width = q_ref.shape
    blocks = k_refs[0].shape[2] // width
    span = q_ref.shape[1] // blocks
    for block in range(blocks):
        cols = slice(block * width, (block + 1) * width)
        lines = slice(block * span, (block + 1) * span)
        total = None
        for r in range(rows):
            keys = jnp.concatenate([k[r, :, cols] for k in k_refs], axis=0)
            term = dot_nt(q_ref[r, lines, :], keys)
            total = term if total is None else total + term
        out_ref[lines, :] = jnp.concatenate([done[lines, :] for done in done_refs] + [total], axis=1)


def softmax_kernel(factor, heads, *refs):
    parts, (head_ref, order_ref, w_ref, pair_ref, held) = refs[:-5], refs[-5:]
    rows, length = w_ref.shape
    sites = rows // heads
    logits = parts[0][...]
    for part in parts[1:]:
        logits = logits + part[...]
    logits = logits * factor
    exponent = jnp.exp(logits - jnp.max(logits, axis=1, keepdims=True))
    shares = (exponent / jnp.sum(exponent, axis=1, keepdims=True)).astype(BF16)
    w_ref[...] = shares
    shares = shares.astype(F32)
    row_sum = jnp.sum(shares, axis=1, keepdims=True)
    lane = lax.broadcasted_iota(jnp.int32, (rows, length), 1)
    row = lax.broadcasted_iota(jnp.int32, (rows, length), 0) % sites
    both = (shares + jnp.where(lane == row, row_sum, 0.0)).reshape(heads, sites, length)
    head_rows = round_up(heads, 8)
    held[...] = jnp.zeros_like(held)
    held[0:heads, :] = jnp.sum(both, axis=1)
    merged = None
    for h in range(heads):
        term = shares[h * sites : (h + 1) * sites, :] * head_ref[h : h + 1, 0:1]
        merged = term if merged is None else merged + term
    held[head_rows : head_rows + sites, :] = merged
    pair_ref[...] = jnp.broadcast_to(
        dot_nn(held[...], order_ref[...], HIGHEST)[None], pair_ref.shape
    )


def mix_kernel(head, v_count, *refs):
    w_ref, v_refs = refs[0], refs[1 : 1 + v_count]
    closing_ref, skip_ref, gain_ref, hidden_ref, normed_ref, mixed = refs[1 + v_count :]
    rows, sites, embed = skip_ref.shape
    width = lane_block(embed, head)
    group = width // head
    lane_head = lax.broadcasted_iota(jnp.int32, (sites, width), 1) // head
    for block in range(embed // width):
        cols = slice(block * width, (block + 1) * width)
        shares = w_ref[block * group * sites : (block + 1) * group * sites, :]
        for r in range(rows):
            values = jnp.concatenate([v[r, :, cols] for v in v_refs], axis=0)
            product = dot_nn(shares, values)
            own = product[0:sites, :]
            for g in range(1, group):
                own = jnp.where(lane_head == g, product[g * sites : (g + 1) * sites, :], own)
            mixed[r * sites : (r + 1) * sites, cols] = own
    hidden = skip_ref[...].astype(F32).reshape(rows * sites, embed) + dot_nn(mixed[...].astype(BF16), closing_ref[...])
    hidden_ref[...] = hidden
    centered = hidden - jnp.mean(hidden, axis=1, keepdims=True)
    spread = jnp.mean(centered * centered, axis=1, keepdims=True)
    normed_ref[...] = (centered * lax.rsqrt(spread + 1e-05) * gain_ref[...].reshape(1, embed)).astype(BF16)


def project_kernel(part_count, *refs):
    parts, (weight_ref, out_ref) = refs[:part_count], refs[part_count:]
    normed = jnp.concatenate([part[...] for part in parts], axis=0)
    out_ref[...] = dot_nn(normed, weight_ref[...]).astype(BF16)


def column_attend(
    factor, query, keys, values, hidden_ref, closing_ref, pick_ref, spread_ref, out_ref, products, mixed
):
    rows, sites, embed = out_ref.shape
    pick = pick_ref[...]
    padded = pick.shape[1]
    seqs = len(keys)
    for s in range(rows):
        for t in range(seqs):
            at = (s * seqs + t) * sites
            products[at : at + sites, :] = query[s * sites : (s + 1) * sites, :] * keys[t]
    product = products[...]
    high = product.astype(BF16)
    low = (product - high.astype(F32)).astype(BF16)
    scores = (dot_nn(high, pick) + dot_nn(low, pick)) * factor
    exponent = jnp.exp(scores).reshape(rows, seqs, sites, padded)
    shares = (exponent / jnp.sum(exponent, axis=1, keepdims=True)).astype(BF16)
    wide = dot_nn(shares.reshape(rows * seqs * sites, padded), spread_ref[...])
    for s in range(rows):
        total = None
        for t in range(seqs):
            at = (s * seqs + t) * sites
            term = wide[at : at + sites, :] * values[t]
            total = term if total is None else total + term
        mixed[s * sites : (s + 1) * sites, :] = total
    out = hidden_ref[...] + dot_nn(mixed[...].astype(BF16), closing_ref[...])
    out_ref[...] = out.reshape(rows, sites, embed).astype(BF16)


def column_kernel(factor, query_ref, kv_ref, *refs):
    rows, sites, embed = refs[4].shape
    kv = kv_ref[...].astype(F32)
    seqs = kv.shape[0] // sites
    keys = [kv[t * sites : (t + 1) * sites, 0:embed] for t in range(seqs)]
    values = [kv[t * sites : (t + 1) * sites, embed:] for t in range(seqs)]
    column_attend(factor, query_ref[...].astype(F32), keys, values, *refs)


def swapped_column_kernel(factor, own_ref, other_ref, *refs):
    rows, sites, embed = refs[4].shape
    cells, columns = own_ref.shape
    half = cells // 2

    def piece(first_is_own, start, stop, at, size):
        found = []
        for block in range(2):
            lo, hi = max(start, block * columns), min(stop, (block + 1) * columns)
            if lo < hi:
                cols = slice(lo - block * columns, hi - block * columns)
                if (block == 0) == first_is_own:
                    found.append(own_ref[at : at + size, cols])
                else:
                    turned = (at + half) % cells
                    found.append(other_ref[turned : turned + size, cols])
        return jnp.concatenate(found, axis=1).astype(F32)

    def attend(first_is_own):
        query = piece(first_is_own, 0, embed, 0, half)
        keys, values = [], []
        for at in (0, half):
            key = piece(first_is_own, embed, 2 * embed, at, half)
            value = piece(first_is_own, 2 * embed, 3 * embed, at, half)
            for t in range(half // sites):
                keys.append(key[t * sites : (t + 1) * sites, :])
                values.append(value[t * sites : (t + 1) * sites, :])
        column_attend(factor, query, keys, values, *refs)

    seq_index = lax.axis_index("seq")
    pl.when(seq_index == 0)(functools.partial(attend, True))
    pl.when(seq_index == 1)(functools.partial(attend, False))


def contact_kernel(heads, pair_ref, factor_ref, own_ref, slab_ref, out_ref, held):
    count, step, length = pair_ref.shape
    head_rows = round_up(heads, 8)
    sites = step - head_rows
    blocks = slab_ref.shape[1] // sites
    total = pair_ref[0, 0:head_rows, :]
    for n in range(1, count):
        total = total + pair_ref[n, 0:head_rows, :]
    held[0:head_rows, :] = total
    held[head_rows:step, :] = pair_ref[lax.axis_index("pos"), head_rows:step, :]
    first = lax.axis_index("seq") * blocks
    table = jnp.concatenate(
        [pair_ref[first + n, head_rows:step, :] for n in range(blocks)], axis=0
    )
    amount = jnp.sum(total, axis=1, keepdims=True)
    real = lax.broadcasted_iota(jnp.int32, (head_rows, 1), 0) < heads
    share = jnp.where(real, factor_ref[0:head_rows, 0:1] / jnp.where(real, amount, 1.0), 0.0)
    slab = dot_nn(held[...], slab_ref[...], HIGHEST)
    own = dot_nt(own_ref[...], total * share, HIGHEST)
    mirrored = dot_nt(own_ref[...], table, HIGHEST)
    adjuster = dot_nn(own, slab[0:head_rows, :], HIGHEST)
    out_ref[...] = jax.nn.sigmoid(
        slab[head_rows:step, :] + mirrored - adjuster + factor_ref[head_rows : head_rows + 1, 0:1]
    )


def call(kernel, out_shape, operands, smem=(), hbm=(), scratch=(), bytes_accessed=1000000):
    vmem = pl.BlockSpec(memory_space=pltpu.VMEM)
    held = sum(math.prod(a.shape) * a.dtype.itemsize for a in [*operands, *jax.tree.leaves(out_shape)])
    held += sum(
        math.prod(a.shape) * np.dtype(a.dtype).itemsize
        for a in scratch
        if a.memory_space == pltpu.VMEM
    )
    limit = 2 * held + 4 * 1024 * 1024
    specs = [
        pl.BlockSpec(memory_space=pltpu.SMEM if i in smem else pl.ANY if i in hbm else pltpu.VMEM)
        for i in range(len(operands))
    ]
    return pl.pallas_call(
        kernel,
        out_shape=out_shape,
        in_specs=specs,
        out_specs=jax.tree.map(lambda _: vmem, out_shape),
        scratch_shapes=list(scratch),
        compiler_params=pltpu.CompilerParams(vmem_limit_bytes=limit),
        cost_estimate=pl.CostEstimate(
            flops=1000000, bytes_accessed=bytes_accessed, transcendentals=0
        ),
    )(*operands)


def stages_of(count):
    stages, stride = [], 1
    while count > 1 and len(stages) < 2 and count % 2 == 0:
        stages.append((stride, 2))
        stride, count = stride * 2, count // 2
    if count > 1:
        stages.append((stride, count))
    return stages[::-1]


def send_pos(array, count, stride, size, delta):
    pairs = []
    for p in range(count):
        a = (p // stride) % size
        pairs.append((p, p + ((a + delta) % size - a) * stride))
    return lax.ppermute(array, "pos", pairs)


def send_all(parts, count, stage):
    stride, size = stage
    return [send_pos(part, count, stride, size, delta) for delta in range(1, size) for part in parts]


def after(array, *others):
    return lax.optimization_barrier((array, *others))[0]


def per_device(
    skip_stream_input,
    lateral_asking_vectors,
    lateral_matched_vectors,
    lateral_carried_vectors,
    lateral_closing_linear,
    upright_normalizer_multiplier,
    upright_threefold_linear,
    upright_closing_linear,
    regression_factors,
    regression_offset,
):
    rows, sites, embed = lateral_asking_vectors.shape
    heads = regression_factors.shape[0]
    head = embed // heads
    seq_count = lax.axis_size("seq")
    pos_count = lax.axis_size("pos")
    length = sites * pos_count
    slab_width = length // seq_count
    cells = rows * sites
    pos_index = lax.axis_index("pos").astype(jnp.int32)
    seq_index = lax.axis_index("seq").astype(jnp.int32)
    swap = [(s, 1 - s) for s in range(2)]
    columns = upright_threefold_linear.shape[1]
    swapped = seq_count == 2 and columns % 128 == 0

    stages = stages_of(pos_count)
    outer = stages[0]
    middle = stages[1] if len(stages) > 1 else None

    scalars = jnp.stack([seq_index, pos_index])
    head_rows = round_up(heads, 8)
    width = lane_block(embed, head)
    key_first = [lateral_matched_vectors] + send_all([lateral_matched_vectors], pos_count, outer)
    key_parts = [jnp.concatenate(key_first, axis=1)]
    value_first = [after(lateral_carried_vectors, key_parts[0])]
    value_first += send_all([lateral_carried_vectors], pos_count, outer)
    masked = call(
        functools.partial(query_kernel, head),
        jax.ShapeDtypeStruct((rows, heads * sites, width), BF16),
        [after(lateral_asking_vectors, key_parts[0])],
        hbm=(0,),
        scratch=[pltpu.VMEM((rows, sites, embed), BF16), pltpu.SemaphoreType.DMA((1,))],
    )
    if middle:
        key_parts += send_all(key_parts, pos_count, middle)
    near = sum(part.shape[1] for part in key_parts)
    partial = call(
        functools.partial(logits_kernel, len(key_parts)),
        jax.ShapeDtypeStruct((heads * sites, near), F32),
        [masked, *key_parts],
    )
    value_first[1] = after(value_first[1], masked)
    value_parts = [jnp.concatenate(value_first, axis=1)]
    if middle:
        value_parts += send_all(value_parts, pos_count, middle)
    if len(stages) > 2:
        far_parts = send_all(key_parts, pos_count, stages[2])
        partial = call(
            functools.partial(logits_kernel, len(far_parts)),
            jax.ShapeDtypeStruct((heads * sites, length), F32),
            [masked, *far_parts, partial],
        )
    padded = round_up(heads, 128)
    head_factors, order, own_select, slab_select, pick, spread = call(
        functools.partial(prepare_kernel, heads, sites, stages),
        (
            jax.ShapeDtypeStruct((head_rows + 8, 128), F32),
            jax.ShapeDtypeStruct((length, length), F32),
            jax.ShapeDtypeStruct((sites, length), F32),
            jax.ShapeDtypeStruct((length, slab_width), F32),
            jax.ShapeDtypeStruct((embed, padded), BF16),
            jax.ShapeDtypeStruct((padded, embed), BF16),
        ),
        [after(scalars, partial), regression_factors, regression_offset],
        smem=(0, 1, 2),
    )
    if seq_count == 2:
        partials = [partial, after(lax.ppermute(partial, "seq", swap), order)]
    else:
        partials = [lax.psum(partial, "seq")]
    shares, pair_local = call(
        functools.partial(
            softmax_kernel, 1.0 / (math.sqrt(head) * math.sqrt(rows * seq_count)), heads
        ),
        (
            jax.ShapeDtypeStruct((heads * sites, length), BF16),
            jax.ShapeDtypeStruct((pos_count, head_rows + sites, length), F32),
        ),
        [*partials, head_factors, order],
        scratch=[pltpu.VMEM((head_rows + sites, length), F32)],
    )
    if len(stages) > 2:
        value_parts = value_parts[:1] + [after(part, pair_local) for part in value_parts[1:]]
        value_parts += send_all(value_parts, pos_count, stages[2])
    hidden, normed = call(
        functools.partial(mix_kernel, head, len(value_parts)),
        (
            jax.ShapeDtypeStruct((cells, embed), F32),
            jax.ShapeDtypeStruct((cells, embed), BF16),
        ),
        [
            shares,
            *value_parts,
            lateral_closing_linear,
            skip_stream_input,
            upright_normalizer_multiplier,
        ],
        scratch=[pltpu.VMEM((cells, embed), F32)],
    )
    pair_all = lax.all_to_all(pair_local, "pos", split_axis=0, concat_axis=0, tiled=True)
    pairing_chances = call(
        functools.partial(contact_kernel, heads),
        jax.ShapeDtypeStruct((sites, slab_width), F32),
        [pair_all, head_factors, own_select, slab_select],
        scratch=[pltpu.VMEM((head_rows + sites, length), F32)],
    )
    if swapped:
        normed_all = [normed, lax.ppermute(normed, "seq", swap)]
        one = jnp.minimum(jnp.abs(normed[0, 0]) + 1, 1)
        weight = upright_threefold_linear * one
    else:
        normed_all = [normed]
        weight = lax.all_gather(upright_threefold_linear, "seq", axis=1, tiled=True)
    projected = call(
        functools.partial(project_kernel, len(normed_all)),
        jax.ShapeDtypeStruct((cells * len(normed_all), weight.shape[1]), BF16),
        [*normed_all, weight],
    )
    if swapped:
        column, column_inputs = swapped_column_kernel, [
            projected,
            lax.ppermute(projected, "seq", swap),
        ]
    else:
        key_value = lax.all_gather(projected[:, embed:], "seq", axis=0, tiled=True)
        column, column_inputs = column_kernel, [projected[:, :embed], key_value]
    alignment_output = call(
        functools.partial(column, 1.0 / math.sqrt(head)),
        jax.ShapeDtypeStruct((rows, sites, embed), BF16),
        [
            *column_inputs,
            hidden,
            after(upright_closing_linear, projected),
            pick,
            spread,
        ],
        scratch=[
            pltpu.VMEM((cells * rows * seq_count, embed), F32),
            pltpu.VMEM((cells, embed), F32),
        ],
    )
    return alignment_output, pairing_chances


def solution(mesh):
    cells = P("seq", "pos", None)
    return jax.shard_map(
        per_device,
        mesh=mesh,
        in_specs=(cells, cells, cells, cells, P(), P(), P(None, "seq"), P(), P(), P()),
        out_specs=(cells, P("pos", "seq")),
        check_vma=False,
    )
```

```python
import functools
import math

import jax
import jax.numpy as jnp
import numpy as np
from jax import lax
from jax.experimental import pallas as pl
from jax.experimental.pallas import tpu as pltpu
from jax.sharding import PartitionSpec as P

F32 = jnp.float32
BF16 = jnp.bfloat16
HIGHEST = lax.Precision.HIGHEST
LANE_BLOCK = 256


def dot_nn(a, b, precision=None):
    return lax.dot_general(
        a, b, (((1,), (0,)), ((), ())), precision=precision, preferred_element_type=F32
    )


def dot_nt(a, b, precision=None):
    return lax.dot_general(
        a, b, (((1,), (1,)), ((), ())), precision=precision, preferred_element_type=F32
    )


def round_up(n, m):
    return -(-n // m) * m


def lane_block(embed, head):
    return LANE_BLOCK if embed % LANE_BLOCK == 0 and LANE_BLOCK % head == 0 else head


def arrival_place(index, column, stages, sites):
    block, place, span = column // sites, column % sites, 1
    for stride, size in stages:
        digit = (block // span) % size
        place = place + ((index // stride) % size + size - digit) % size * (stride * sites)
        span *= size
    return place


def fetch(pairs, sems):
    copies = [pltpu.make_async_copy(src, dst, sems.at[i]) for i, (src, dst) in enumerate(pairs)]
    for copy in copies:
        copy.start()
    for copy in copies:
        copy.wait()


def query_kernel(head, q_hbm, masked_ref, q_ref, sems):
    rows, sites, embed = q_ref.shape
    width = masked_ref.shape[2]
    group = width // head
    span = group * sites
    fetch([(q_hbm, q_ref)], sems)
    lane_head = lax.broadcasted_iota(jnp.int32, (span, width), 1) // head
    row_head = lax.broadcasted_iota(jnp.int32, (span, width), 0) // sites
    own_head = lane_head == row_head
    for block in range(embed // width):
        for r in range(rows):
            q = q_ref[r, :, block * width : (block + 1) * width].astype(F32)
            q = jnp.where(own_head, jnp.concatenate([q] * group, axis=0), 0.0).astype(BF16)
            masked_ref[r, block * span : (block + 1) * span, :] = q


def prepare_kernel(heads, sites, stages, scalar_ref, factor_ref, offset_ref, *refs):
    head_ref, order_ref, own_ref, slab_ref, pick_ref, spread_ref = refs
    head = pick_ref.shape[0] // heads
    row = lax.broadcasted_iota(jnp.int32, pick_ref.shape, 0)
    lane = lax.broadcasted_iota(jnp.int32, pick_ref.shape, 1)
    pick_ref[...] = (row // head == lane).astype(BF16)
    row = lax.broadcasted_iota(jnp.int32, spread_ref.shape, 0)
    lane = lax.broadcasted_iota(jnp.int32, spread_ref.shape, 1)
    spread_ref[...] = (lane // head == row).astype(BF16)
    row = lax.broadcasted_iota(jnp.int32, head_ref.shape, 0)
    factors = jnp.zeros(head_ref.shape, F32)
    for h in range(heads):
        factors = jnp.where(row == h, factor_ref[h], factors)
    head_ref[...] = jnp.where(row == round_up(heads, 8), offset_ref[0], factors)
    seq_index, pos_index = scalar_ref[0], scalar_ref[1]
    length = order_ref.shape[0]
    row = lax.broadcasted_iota(jnp.int32, (length, length), 0)
    lane = lax.broadcasted_iota(jnp.int32, (length, length), 1)
    order_ref[...] = (arrival_place(pos_index, row, stages, sites) == lane).astype(F32)
    row = lax.broadcasted_iota(jnp.int32, own_ref.shape, 0)
    lane = lax.broadcasted_iota(jnp.int32, own_ref.shape, 1)
    own_ref[...] = (row + pos_index * sites == lane).astype(F32)
    row = lax.broadcasted_iota(jnp.int32, slab_ref.shape, 0)
    lane = lax.broadcasted_iota(jnp.int32, slab_ref.shape, 1)
    slab_ref[...] = (row == lane + seq_index * slab_ref.shape[1]).astype(F32)


def logits_kernel(part_count, *refs):
    q_ref, k_refs, done_refs, out_ref = refs[0], refs[1 : 1 + part_count], refs[1 + part_count : -1], refs[-1]
    rows, _, width = q_ref.shape
    blocks = k_refs[0].shape[2] // width
    span = q_ref.shape[1] // blocks
    for block in range(blocks):
        cols = slice(block * width, (block + 1) * width)
        lines = slice(block * span, (block + 1) * span)
        total = None
        for r in range(rows):
            keys = jnp.concatenate([k[r, :, cols] for k in k_refs], axis=0)
            term = dot_nt(q_ref[r, lines, :], keys)
            total = term if total is None else total + term
        out_ref[lines, :] = jnp.concatenate([done[lines, :] for done in done_refs] + [total], axis=1)


def softmax_kernel(factor, heads, *refs):
    parts, (head_ref, order_ref, w_ref, pair_ref, held) = refs[:-5], refs[-5:]
    rows, length = w_ref.shape
    sites = rows // heads
    logits = parts[0][...]
    for part in parts[1:]:
        logits = logits + part[...]
    logits = logits * factor
    exponent = jnp.exp(logits - jnp.max(logits, axis=1, keepdims=True))
    shares = (exponent / jnp.sum(exponent, axis=1, keepdims=True)).astype(BF16)
    w_ref[...] = shares
    shares = shares.astype(F32)
    row_sum = jnp.sum(shares, axis=1, keepdims=True)
    lane = lax.broadcasted_iota(jnp.int32, (rows, length), 1)
    row = lax.broadcasted_iota(jnp.int32, (rows, length), 0) % sites
    both = (shares + jnp.where(lane == row, row_sum, 0.0)).reshape(heads, sites, length)
    head_rows = round_up(heads, 8)
    held[...] = jnp.zeros_like(held)
    held[0:heads, :] = jnp.sum(both, axis=1)
    merged = None
    for h in range(heads):
        term = shares[h * sites : (h + 1) * sites, :] * head_ref[h : h + 1, 0:1]
        merged = term if merged is None else merged + term
    held[head_rows : head_rows + sites, :] = merged
    pair_ref[...] = jnp.broadcast_to(
        dot_nn(held[...], order_ref[...], HIGHEST)[None], pair_ref.shape
    )


def mix_kernel(head, v_count, *refs):
    w_ref, v_refs = refs[0], refs[1 : 1 + v_count]
    closing_ref, skip_ref, gain_ref, hidden_ref, normed_ref, one_ref, mixed = refs[1 + v_count :]
    one_ref[...] = jnp.ones_like(one_ref)
    rows, sites, embed = skip_ref.shape
    width = lane_block(embed, head)
    group = width // head
    lane_head = lax.broadcasted_iota(jnp.int32, (sites, width), 1) // head
    for block in range(embed // width):
        cols = slice(block * width, (block + 1) * width)
        shares = w_ref[block * group * sites : (block + 1) * group * sites, :]
        for r in range(rows):
            values = jnp.concatenate([v[r, :, cols] for v in v_refs], axis=0)
            product = dot_nn(shares, values)
            own = product[0:sites, :]
            for g in range(1, group):
                own = jnp.where(lane_head == g, product[g * sites : (g + 1) * sites, :], own)
            mixed[r * sites : (r + 1) * sites, cols] = own
    hidden = skip_ref[...].astype(F32).reshape(rows * sites, embed) + dot_nn(mixed[...].astype(BF16), closing_ref[...])
    hidden_ref[...] = hidden
    centered = hidden - jnp.mean(hidden, axis=1, keepdims=True)
    spread = jnp.mean(centered * centered, axis=1, keepdims=True)
    normed_ref[...] = (centered * lax.rsqrt(spread + 1e-05) * gain_ref[...].reshape(1, embed)).astype(BF16)


def project_kernel(part_count, *refs):
    parts, (weight_ref, out_ref) = refs[:part_count], refs[part_count:]
    normed = jnp.concatenate([part[...] for part in parts], axis=0)
    out_ref[...] = dot_nn(normed, weight_ref[...]).astype(BF16)


def column_attend(
    factor, query, keys, values, hidden_ref, closing_ref, pick_ref, spread_ref, out_ref, products, mixed
):
    rows, sites, embed = out_ref.shape
    pick = pick_ref[...]
    padded = pick.shape[1]
    seqs = len(keys)
    for s in range(rows):
        for t in range(seqs):
            at = (s * seqs + t) * sites
            products[at : at + sites, :] = query[s * sites : (s + 1) * sites, :] * keys[t]
    product = products[...]
    high = product.astype(BF16)
    low = (product - high.astype(F32)).astype(BF16)
    scores = (dot_nn(high, pick) + dot_nn(low, pick)) * factor
    exponent = jnp.exp(scores).reshape(rows, seqs, sites, padded)
    shares = (exponent / jnp.sum(exponent, axis=1, keepdims=True)).astype(BF16)
    wide = dot_nn(shares.reshape(rows * seqs * sites, padded), spread_ref[...])
    for s in range(rows):
        total = None
        for t in range(seqs):
            at = (s * seqs + t) * sites
            term = wide[at : at + sites, :] * values[t]
            total = term if total is None else total + term
        mixed[s * sites : (s + 1) * sites, :] = total
    out = hidden_ref[...] + dot_nn(mixed[...].astype(BF16), closing_ref[...])
    out_ref[...] = out.reshape(rows, sites, embed).astype(BF16)


def column_kernel(factor, query_ref, kv_ref, *refs):
    rows, sites, embed = refs[4].shape
    kv = kv_ref[...].astype(F32)
    seqs = kv.shape[0] // sites
    keys = [kv[t * sites : (t + 1) * sites, 0:embed] for t in range(seqs)]
    values = [kv[t * sites : (t + 1) * sites, embed:] for t in range(seqs)]
    column_attend(factor, query_ref[...].astype(F32), keys, values, *refs)


def swapped_column_kernel(factor, own_ref, other_ref, *refs):
    rows, sites, embed = refs[4].shape
    cells, columns = own_ref.shape
    half = cells // 2

    def piece(first_is_own, start, stop, at, size):
        found = []
        for block in range(2):
            lo, hi = max(start, block * columns), min(stop, (block + 1) * columns)
            if lo < hi:
                cols = slice(lo - block * columns, hi - block * columns)
                if (block == 0) == first_is_own:
                    found.append(own_ref[at : at + size, cols])
                else:
                    turned = (at + half) % cells
                    found.append(other_ref[turned : turned + size, cols])
        return jnp.concatenate(found, axis=1).astype(F32)

    def attend(first_is_own):
        query = piece(first_is_own, 0, embed, 0, half)
        keys, values = [], []
        for at in (0, half):
            key = piece(first_is_own, embed, 2 * embed, at, half)
            value = piece(first_is_own, 2 * embed, 3 * embed, at, half)
            for t in range(half // sites):
                keys.append(key[t * sites : (t + 1) * sites, :])
                values.append(value[t * sites : (t + 1) * sites, :])
        column_attend(factor, query, keys, values, *refs)

    seq_index = lax.axis_index("seq")
    pl.when(seq_index == 0)(functools.partial(attend, True))
    pl.when(seq_index == 1)(functools.partial(attend, False))


def contact_kernel(heads, pair_ref, factor_ref, own_ref, slab_ref, out_ref, held):
    count, step, length = pair_ref.shape
    head_rows = round_up(heads, 8)
    sites = step - head_rows
    blocks = slab_ref.shape[1] // sites
    total = pair_ref[0, 0:head_rows, :]
    for n in range(1, count):
        total = total + pair_ref[n, 0:head_rows, :]
    held[0:head_rows, :] = total
    held[head_rows:step, :] = pair_ref[lax.axis_index("pos"), head_rows:step, :]
    first = lax.axis_index("seq") * blocks
    table = jnp.concatenate(
        [pair_ref[first + n, head_rows:step, :] for n in range(blocks)], axis=0
    )
    amount = jnp.sum(total, axis=1, keepdims=True)
    real = lax.broadcasted_iota(jnp.int32, (head_rows, 1), 0) < heads
    share = jnp.where(real, factor_ref[0:head_rows, 0:1] / jnp.where(real, amount, 1.0), 0.0)
    slab = dot_nn(held[...], slab_ref[...], HIGHEST)
    own = dot_nt(own_ref[...], total * share, HIGHEST)
    mirrored = dot_nt(own_ref[...], table, HIGHEST)
    adjuster = dot_nn(own, slab[0:head_rows, :], HIGHEST)
    out_ref[...] = jax.nn.sigmoid(
        slab[head_rows:step, :] + mirrored - adjuster + factor_ref[head_rows : head_rows + 1, 0:1]
    )


def call(kernel, out_shape, operands, smem=(), hbm=(), scratch=(), bytes_accessed=1000000):
    vmem = pl.BlockSpec(memory_space=pltpu.VMEM)
    held = sum(math.prod(a.shape) * a.dtype.itemsize for a in [*operands, *jax.tree.leaves(out_shape)])
    held += sum(
        math.prod(a.shape) * np.dtype(a.dtype).itemsize
        for a in scratch
        if a.memory_space == pltpu.VMEM
    )
    limit = 2 * held + 4 * 1024 * 1024
    specs = [
        pl.BlockSpec(memory_space=pltpu.SMEM if i in smem else pl.ANY if i in hbm else pltpu.VMEM)
        for i in range(len(operands))
    ]
    return pl.pallas_call(
        kernel,
        out_shape=out_shape,
        in_specs=specs,
        out_specs=jax.tree.map(lambda _: vmem, out_shape),
        scratch_shapes=list(scratch),
        compiler_params=pltpu.CompilerParams(vmem_limit_bytes=limit),
        cost_estimate=pl.CostEstimate(
            flops=1000000, bytes_accessed=bytes_accessed, transcendentals=0
        ),
    )(*operands)


def stages_of(count):
    stages, stride = [], 1
    while count > 1 and len(stages) < 2 and count % 2 == 0:
        stages.append((stride, 2))
        stride, count = stride * 2, count // 2
    if count > 1:
        stages.append((stride, count))
    return stages[::-1]


def send_pos(array, count, stride, size, delta):
    pairs = []
    for p in range(count):
        a = (p // stride) % size
        pairs.append((p, p + ((a + delta) % size - a) * stride))
    return lax.ppermute(array, "pos", pairs)


def send_all(parts, count, stage):
    stride, size = stage
    return [send_pos(part, count, stride, size, delta) for delta in range(1, size) for part in parts]


def after(array, *others):
    return lax.optimization_barrier((array, *others))[0]


def per_device(
    skip_stream_input,
    lateral_asking_vectors,
    lateral_matched_vectors,
    lateral_carried_vectors,
    lateral_closing_linear,
    upright_normalizer_multiplier,
    upright_threefold_linear,
    upright_closing_linear,
    regression_factors,
    regression_offset,
):
    rows, sites, embed = lateral_asking_vectors.shape
    heads = regression_factors.shape[0]
    head = embed // heads
    seq_count = lax.axis_size("seq")
    pos_count = lax.axis_size("pos")
    length = sites * pos_count
    slab_width = length // seq_count
    cells = rows * sites
    pos_index = lax.axis_index("pos").astype(jnp.int32)
    seq_index = lax.axis_index("seq").astype(jnp.int32)
    swap = [(s, 1 - s) for s in range(2)]
    columns = upright_threefold_linear.shape[1]
    swapped = seq_count == 2 and columns % 128 == 0

    stages = stages_of(pos_count)
    outer = stages[0]
    middle = stages[1] if len(stages) > 1 else None

    scalars = jnp.stack([seq_index, pos_index])
    head_rows = round_up(heads, 8)
    width = lane_block(embed, head)
    key_first = [lateral_matched_vectors] + send_all([lateral_matched_vectors], pos_count, outer)
    key_parts = [jnp.concatenate(key_first, axis=1)]
    value_first = [after(lateral_carried_vectors, key_parts[0])]
    value_first += [
        send_pos(lateral_carried_vectors, pos_count, *outer, delta) for delta in range(outer[1] - 1, 0, -1)
    ][::-1]
    masked = call(
        functools.partial(query_kernel, head),
        jax.ShapeDtypeStruct((rows, heads * sites, width), BF16),
        [after(lateral_asking_vectors, key_parts[0])],
        hbm=(0,),
        scratch=[pltpu.VMEM((rows, sites, embed), BF16), pltpu.SemaphoreType.DMA((1,))],
    )
    if middle:
        key_parts += send_all(key_parts, pos_count, middle)
    near = sum(part.shape[1] for part in key_parts)
    partial = call(
        functools.partial(logits_kernel, len(key_parts)),
        jax.ShapeDtypeStruct((heads * sites, near), F32),
        [masked, *key_parts],
    )
    value_first[-1] = after(value_first[-1], masked)
    value_own = jnp.zeros((rows, sites * outer[1], embed), BF16)
    for delta in [0, *range(outer[1] - 1, 0, -1)]:
        value_own = lax.dynamic_update_slice(value_own, value_first[delta], (0, delta * sites, 0))
    value_parts = [value_own]
    if middle:
        value_parts += send_all(value_parts, pos_count, middle)
    if len(stages) > 2:
        far_parts = send_all(key_parts, pos_count, stages[2])
        partial = call(
            functools.partial(logits_kernel, len(far_parts)),
            jax.ShapeDtypeStruct((heads * sites, length), F32),
            [masked, *far_parts, partial],
        )
    padded = round_up(heads, 128)
    head_factors, order, own_select, slab_select, pick, spread = call(
        functools.partial(prepare_kernel, heads, sites, stages),
        (
            jax.ShapeDtypeStruct((head_rows + 8, 128), F32),
            jax.ShapeDtypeStruct((length, length), F32),
            jax.ShapeDtypeStruct((sites, length), F32),
            jax.ShapeDtypeStruct((length, slab_width), F32),
            jax.ShapeDtypeStruct((embed, padded), BF16),
            jax.ShapeDtypeStruct((padded, embed), BF16),
        ),
        [after(scalars, partial), regression_factors, regression_offset],
        smem=(0, 1, 2),
    )
    if seq_count == 2:
        partials = [partial, after(lax.ppermute(partial, "seq", swap), order)]
    else:
        partials = [lax.psum(partial, "seq")]
    shares, pair_local = call(
        functools.partial(
            softmax_kernel, 1.0 / (math.sqrt(head) * math.sqrt(rows * seq_count)), heads
        ),
        (
            jax.ShapeDtypeStruct((heads * sites, length), BF16),
            jax.ShapeDtypeStruct((pos_count, head_rows + sites, length), F32),
        ),
        [*partials, head_factors, order],
        scratch=[pltpu.VMEM((head_rows + sites, length), F32)],
    )
    if len(stages) > 2:
        value_parts = value_parts[:1] + [after(part, pair_local) for part in value_parts[1:]]
        value_parts += send_all(value_parts, pos_count, stages[2])
    hidden, normed, one = call(
        functools.partial(mix_kernel, head, len(value_parts)),
        (
            jax.ShapeDtypeStruct((cells, embed), F32),
            jax.ShapeDtypeStruct((cells, embed), BF16),
            jax.ShapeDtypeStruct((1, columns), BF16),
        ),
        [
            shares,
            *value_parts,
            lateral_closing_linear,
            skip_stream_input,
            upright_normalizer_multiplier,
        ],
        scratch=[pltpu.VMEM((cells, embed), F32)],
    )
    pair_all = lax.all_to_all(pair_local, "pos", split_axis=0, concat_axis=0, tiled=True)
    pairing_chances = call(
        functools.partial(contact_kernel, heads),
        jax.ShapeDtypeStruct((sites, slab_width), F32),
        [pair_all, head_factors, own_select, slab_select],
        scratch=[pltpu.VMEM((head_rows + sites, length), F32)],
    )
    if swapped:
        normed_all = [normed, lax.ppermute(normed, "seq", swap)]
        weight = upright_threefold_linear * one
    else:
        normed_all = [normed]
        weight = lax.all_gather(upright_threefold_linear, "seq", axis=1, tiled=True)
    projected = call(
        functools.partial(project_kernel, len(normed_all)),
        jax.ShapeDtypeStruct((cells * len(normed_all), weight.shape[1]), BF16),
        [*normed_all, weight],
    )
    if swapped:
        column, column_inputs = swapped_column_kernel, [
            projected,
            lax.ppermute(projected, "seq", swap),
        ]
    else:
        key_value = lax.all_gather(projected[:, embed:], "seq", axis=0, tiled=True)
        column, column_inputs = column_kernel, [projected[:, :embed], key_value]
    alignment_output = call(
        functools.partial(column, 1.0 / math.sqrt(head)),
        jax.ShapeDtypeStruct((rows, sites, embed), BF16),
        [
            *column_inputs,
            hidden,
            after(upright_closing_linear, projected),
            pick,
            spread,
        ],
        scratch=[
            pltpu.VMEM((cells * rows * seq_count, embed), F32),
            pltpu.VMEM((cells, embed), F32),
        ],
    )
    return alignment_output, pairing_chances


def solution(mesh):
    cells = P("seq", "pos", None)
    return jax.shard_map(
        per_device,
        mesh=mesh,
        in_specs=(cells, cells, cells, cells, P(), P(), P(None, "seq"), P(), P(), P()),
        out_specs=(cells, P("pos", "seq")),
        check_vma=False,
    )
```

```python
import functools
import math

import jax
import jax.numpy as jnp
import numpy as np
from jax import lax
from jax.experimental import pallas as pl
from jax.experimental.pallas import tpu as pltpu
from jax.sharding import PartitionSpec as P

F32 = jnp.float32
BF16 = jnp.bfloat16
HIGHEST = lax.Precision.HIGHEST
LANE_BLOCK = 256


def dot_nn(a, b, precision=None):
    return lax.dot_general(
        a, b, (((1,), (0,)), ((), ())), precision=precision, preferred_element_type=F32
    )


def dot_nt(a, b, precision=None):
    return lax.dot_general(
        a, b, (((1,), (1,)), ((), ())), precision=precision, preferred_element_type=F32
    )


def round_up(n, m):
    return -(-n // m) * m


def lane_block(embed, head):
    return LANE_BLOCK if embed % LANE_BLOCK == 0 and LANE_BLOCK % head == 0 else head


def arrival_place(index, column, stages, sites):
    block, place, span = column // sites, column % sites, 1
    for stride, size in stages:
        digit = (block // span) % size
        place = place + ((index // stride) % size + size - digit) % size * (stride * sites)
        span *= size
    return place


def fetch(pairs, sems):
    copies = [pltpu.make_async_copy(src, dst, sems.at[i]) for i, (src, dst) in enumerate(pairs)]
    for copy in copies:
        copy.start()
    for copy in copies:
        copy.wait()


def query_kernel(head, q_hbm, masked_ref, q_ref, sems):
    rows, sites, embed = q_ref.shape
    width = masked_ref.shape[2]
    group = width // head
    span = group * sites
    fetch([(q_hbm, q_ref)], sems)
    lane_head = lax.broadcasted_iota(jnp.int32, (span, width), 1) // head
    row_head = lax.broadcasted_iota(jnp.int32, (span, width), 0) // sites
    own_head = lane_head == row_head
    for block in range(embed // width):
        for r in range(rows):
            q = q_ref[r, :, block * width : (block + 1) * width].astype(F32)
            q = jnp.where(own_head, jnp.concatenate([q] * group, axis=0), 0.0).astype(BF16)
            masked_ref[r, block * span : (block + 1) * span, :] = q


def prepare_kernel(heads, sites, stages, scalar_ref, factor_ref, offset_ref, *refs):
    head_ref, order_ref, own_ref, slab_ref, pick_ref, spread_ref = refs
    head = pick_ref.shape[0] // heads
    row = lax.broadcasted_iota(jnp.int32, pick_ref.shape, 0)
    lane = lax.broadcasted_iota(jnp.int32, pick_ref.shape, 1)
    pick_ref[...] = (row // head == lane).astype(BF16)
    row = lax.broadcasted_iota(jnp.int32, spread_ref.shape, 0)
    lane = lax.broadcasted_iota(jnp.int32, spread_ref.shape, 1)
    spread_ref[...] = (lane // head == row).astype(BF16)
    row = lax.broadcasted_iota(jnp.int32, head_ref.shape, 0)
    factors = jnp.zeros(head_ref.shape, F32)
    for h in range(heads):
        factors = jnp.where(row == h, factor_ref[h], factors)
    head_ref[...] = jnp.where(row == round_up(heads, 8), offset_ref[0], factors)
    seq_index, pos_index = scalar_ref[0], scalar_ref[1]
    length = order_ref.shape[0]
    row = lax.broadcasted_iota(jnp.int32, (length, length), 0)
    lane = lax.broadcasted_iota(jnp.int32, (length, length), 1)
    order_ref[...] = (arrival_place(pos_index, row, stages, sites) == lane).astype(BF16)
    row = lax.broadcasted_iota(jnp.int32, own_ref.shape, 0)
    lane = lax.broadcasted_iota(jnp.int32, own_ref.shape, 1)
    own_ref[...] = (row + pos_index * sites == lane).astype(F32)
    row = lax.broadcasted_iota(jnp.int32, slab_ref.shape, 0)
    lane = lax.broadcasted_iota(jnp.int32, slab_ref.shape, 1)
    slab_ref[...] = (row == lane + seq_index * slab_ref.shape[1]).astype(F32)


def logits_kernel(part_count, *refs):
    q_ref, k_refs, done_refs, out_ref = refs[0], refs[1 : 1 + part_count], refs[1 + part_count : -1], refs[-1]
    rows, _, width = q_ref.shape
    blocks = k_refs[0].shape[2] // width
    span = q_ref.shape[1] // blocks
    for block in range(blocks):
        cols = slice(block * width, (block + 1) * width)
        lines = slice(block * span, (block + 1) * span)
        total = None
        for r in range(rows):
            keys = jnp.concatenate([k[r, :, cols] for k in k_refs], axis=0)
            term = dot_nt(q_ref[r, lines, :], keys)
            total = term if total is None else total + term
        out_ref[lines, :] = jnp.concatenate([done[lines, :] for done in done_refs] + [total], axis=1)


def softmax_kernel(factor, heads, *refs):
    parts, (head_ref, order_ref, w_ref, pair_ref, held) = refs[:-5], refs[-5:]
    rows, length = w_ref.shape
    sites = rows // heads
    logits = parts[0][...]
    for part in parts[1:]:
        logits = logits + part[...]
    logits = logits * factor
    exponent = jnp.exp(logits - jnp.max(logits, axis=1, keepdims=True))
    shares = (exponent / jnp.sum(exponent, axis=1, keepdims=True)).astype(BF16)
    w_ref[...] = shares
    shares = shares.astype(F32)
    row_sum = jnp.sum(shares, axis=1, keepdims=True)
    lane = lax.broadcasted_iota(jnp.int32, (rows, length), 1)
    row = lax.broadcasted_iota(jnp.int32, (rows, length), 0) % sites
    both = (shares + jnp.where(lane == row, row_sum, 0.0)).reshape(heads, sites, length)
    head_rows = round_up(heads, 8)
    held[...] = jnp.zeros_like(held)
    held[0:heads, :] = jnp.sum(both, axis=1)
    merged = None
    for h in range(heads):
        term = shares[h * sites : (h + 1) * sites, :] * head_ref[h : h + 1, 0:1]
        merged = term if merged is None else merged + term
    held[head_rows : head_rows + sites, :] = merged
    rest, ordered = held[...], None
    for _ in range(3):
        part = rest.astype(BF16)
        rest = rest - part.astype(F32)
        term = dot_nn(part, order_ref[...])
        ordered = term if ordered is None else ordered + term
    pair_ref[...] = jnp.broadcast_to(ordered[None], pair_ref.shape)


def mix_kernel(head, v_count, *refs):
    w_ref, v_refs = refs[0], refs[1 : 1 + v_count]
    closing_ref, skip_ref, gain_ref, hidden_ref, normed_ref, one_ref, mixed = refs[1 + v_count :]
    one_ref[...] = jnp.ones_like(one_ref)
    rows, sites, embed = skip_ref.shape
    width = lane_block(embed, head)
    group = width // head
    lane_head = lax.broadcasted_iota(jnp.int32, (sites, width), 1) // head
    for block in range(embed // width):
        cols = slice(block * width, (block + 1) * width)
        shares = w_ref[block * group * sites : (block + 1) * group * sites, :]
        for r in range(rows):
            values = jnp.concatenate([v[r, :, cols] for v in v_refs], axis=0)
            product = dot_nn(shares, values)
            own = product[0:sites, :]
            for g in range(1, group):
                own = jnp.where(lane_head == g, product[g * sites : (g + 1) * sites, :], own)
            mixed[r * sites : (r + 1) * sites, cols] = own
    hidden = skip_ref[...].astype(F32).reshape(rows * sites, embed) + dot_nn(mixed[...].astype(BF16), closing_ref[...])
    hidden_ref[...] = hidden
    centered = hidden - jnp.mean(hidden, axis=1, keepdims=True)
    spread = jnp.mean(centered * centered, axis=1, keepdims=True)
    normed_ref[...] = (centered * lax.rsqrt(spread + 1e-05) * gain_ref[...].reshape(1, embed)).astype(BF16)


def project_kernel(part_count, *refs):
    parts, (weight_ref, out_ref) = refs[:part_count], refs[part_count:]
    normed = jnp.concatenate([part[...] for part in parts], axis=0)
    out_ref[...] = dot_nn(normed, weight_ref[...]).astype(BF16)


def column_attend(
    factor, query, keys, values, hidden_ref, closing_ref, pick_ref, spread_ref, out_ref, products, mixed
):
    rows, sites, embed = out_ref.shape
    pick = pick_ref[...]
    padded = pick.shape[1]
    seqs = len(keys)
    for s in range(rows):
        for t in range(seqs):
            at = (s * seqs + t) * sites
            products[at : at + sites, :] = query[s * sites : (s + 1) * sites, :] * keys[t]
    product = products[...]
    high = product.astype(BF16)
    low = (product - high.astype(F32)).astype(BF16)
    scores = (dot_nn(high, pick) + dot_nn(low, pick)) * factor
    exponent = jnp.exp(scores).reshape(rows, seqs, sites, padded)
    shares = (exponent / jnp.sum(exponent, axis=1, keepdims=True)).astype(BF16)
    wide = dot_nn(shares.reshape(rows * seqs * sites, padded), spread_ref[...])
    for s in range(rows):
        total = None
        for t in range(seqs):
            at = (s * seqs + t) * sites
            term = wide[at : at + sites, :] * values[t]
            total = term if total is None else total + term
        mixed[s * sites : (s + 1) * sites, :] = total
    out = hidden_ref[...] + dot_nn(mixed[...].astype(BF16), closing_ref[...])
    out_ref[...] = out.reshape(rows, sites, embed).astype(BF16)


def column_kernel(factor, query_ref, kv_ref, *refs):
    rows, sites, embed = refs[4].shape
    kv = kv_ref[...].astype(F32)
    seqs = kv.shape[0] // sites
    keys = [kv[t * sites : (t + 1) * sites, 0:embed] for t in range(seqs)]
    values = [kv[t * sites : (t + 1) * sites, embed:] for t in range(seqs)]
    column_attend(factor, query_ref[...].astype(F32), keys, values, *refs)


def swapped_column_kernel(factor, own_ref, other_ref, *refs):
    rows, sites, embed = refs[4].shape
    cells, columns = own_ref.shape
    half = cells // 2

    def piece(first_is_own, start, stop, at, size):
        found = []
        for block in range(2):
            lo, hi = max(start, block * columns), min(stop, (block + 1) * columns)
            if lo < hi:
                cols = slice(lo - block * columns, hi - block * columns)
                if (block == 0) == first_is_own:
                    found.append(own_ref[at : at + size, cols])
                else:
                    turned = (at + half) % cells
                    found.append(other_ref[turned : turned + size, cols])
        return jnp.concatenate(found, axis=1).astype(F32)

    def attend(first_is_own):
        query = piece(first_is_own, 0, embed, 0, half)
        keys, values = [], []
        for at in (0, half):
            key = piece(first_is_own, embed, 2 * embed, at, half)
            value = piece(first_is_own, 2 * embed, 3 * embed, at, half)
            for t in range(half // sites):
                keys.append(key[t * sites : (t + 1) * sites, :])
                values.append(value[t * sites : (t + 1) * sites, :])
        column_attend(factor, query, keys, values, *refs)

    seq_index = lax.axis_index("seq")
    pl.when(seq_index == 0)(functools.partial(attend, True))
    pl.when(seq_index == 1)(functools.partial(attend, False))


def contact_kernel(heads, pair_ref, factor_ref, own_ref, slab_ref, out_ref, held):
    count, step, length = pair_ref.shape
    head_rows = round_up(heads, 8)
    sites = step - head_rows
    blocks = slab_ref.shape[1] // sites
    total = pair_ref[0, 0:head_rows, :]
    for n in range(1, count):
        total = total + pair_ref[n, 0:head_rows, :]
    held[0:head_rows, :] = total
    held[head_rows:step, :] = pair_ref[lax.axis_index("pos"), head_rows:step, :]
    first = lax.axis_index("seq") * blocks
    table = jnp.concatenate(
        [pair_ref[first + n, head_rows:step, :] for n in range(blocks)], axis=0
    )
    amount = jnp.sum(total, axis=1, keepdims=True)
    real = lax.broadcasted_iota(jnp.int32, (head_rows, 1), 0) < heads
    share = jnp.where(real, factor_ref[0:head_rows, 0:1] / jnp.where(real, amount, 1.0), 0.0)
    slab = dot_nn(held[...], slab_ref[...], HIGHEST)
    own = dot_nt(own_ref[...], total * share, HIGHEST)
    mirrored = dot_nt(own_ref[...], table, HIGHEST)
    adjuster = dot_nn(own, slab[0:head_rows, :], HIGHEST)
    out_ref[...] = jax.nn.sigmoid(
        slab[head_rows:step, :] + mirrored - adjuster + factor_ref[head_rows : head_rows + 1, 0:1]
    )


def call(kernel, out_shape, operands, smem=(), hbm=(), scratch=(), bytes_accessed=1000000):
    vmem = pl.BlockSpec(memory_space=pltpu.VMEM)
    held = sum(math.prod(a.shape) * a.dtype.itemsize for a in [*operands, *jax.tree.leaves(out_shape)])
    held += sum(
        math.prod(a.shape) * np.dtype(a.dtype).itemsize
        for a in scratch
        if a.memory_space == pltpu.VMEM
    )
    limit = 2 * held + 4 * 1024 * 1024
    specs = [
        pl.BlockSpec(memory_space=pltpu.SMEM if i in smem else pl.ANY if i in hbm else pltpu.VMEM)
        for i in range(len(operands))
    ]
    return pl.pallas_call(
        kernel,
        out_shape=out_shape,
        in_specs=specs,
        out_specs=jax.tree.map(lambda _: vmem, out_shape),
        scratch_shapes=list(scratch),
        compiler_params=pltpu.CompilerParams(vmem_limit_bytes=limit),
        cost_estimate=pl.CostEstimate(
            flops=1000000, bytes_accessed=bytes_accessed, transcendentals=0
        ),
    )(*operands)


def stages_of(count):
    stages, stride = [], 1
    while count > 1 and len(stages) < 2 and count % 2 == 0:
        stages.append((stride, 2))
        stride, count = stride * 2, count // 2
    if count > 1:
        stages.append((stride, count))
    return stages[::-1]


def send_pos(array, count, stride, size, delta):
    pairs = []
    for p in range(count):
        a = (p // stride) % size
        pairs.append((p, p + ((a + delta) % size - a) * stride))
    return lax.ppermute(array, "pos", pairs)


def send_all(parts, count, stage):
    stride, size = stage
    return [send_pos(part, count, stride, size, delta) for delta in range(1, size) for part in parts]


def lay_together(parts, order):
    size = parts[0].shape[1]
    whole = jnp.zeros((parts[0].shape[0], size * len(parts), parts[0].shape[2]), parts[0].dtype)
    for at in order:
        whole = lax.dynamic_update_slice(whole, parts[at], (0, at * size, 0))
    return whole


def after(array, *others):
    return lax.optimization_barrier((array, *others))[0]


def per_device(
    skip_stream_input,
    lateral_asking_vectors,
    lateral_matched_vectors,
    lateral_carried_vectors,
    lateral_closing_linear,
    upright_normalizer_multiplier,
    upright_threefold_linear,
    upright_closing_linear,
    regression_factors,
    regression_offset,
):
    rows, sites, embed = lateral_asking_vectors.shape
    heads = regression_factors.shape[0]
    head = embed // heads
    seq_count = lax.axis_size("seq")
    pos_count = lax.axis_size("pos")
    length = sites * pos_count
    slab_width = length // seq_count
    cells = rows * sites
    pos_index = lax.axis_index("pos").astype(jnp.int32)
    seq_index = lax.axis_index("seq").astype(jnp.int32)
    swap = [(s, 1 - s) for s in range(2)]
    columns = upright_threefold_linear.shape[1]
    swapped = seq_count == 2 and columns % 128 == 0

    stages = stages_of(pos_count)
    outer = stages[0]
    size = outer[1]
    middle = stages[1] if len(stages) > 1 else None

    scalars = jnp.stack([seq_index, pos_index])
    head_rows = round_up(heads, 8)
    width = lane_block(embed, head)
    key_first = [lateral_matched_vectors] + send_all([lateral_matched_vectors], pos_count, outer)
    key_parts = [lay_together(key_first, [0, 1, *range(3, size), *range(2, min(size, 3))])]
    value_first = [after(lateral_carried_vectors, key_parts[0])]
    value_first += [
        send_pos(lateral_carried_vectors, pos_count, *outer, delta) for delta in range(outer[1] - 1, 0, -1)
    ][::-1]
    masked = call(
        functools.partial(query_kernel, head),
        jax.ShapeDtypeStruct((rows, heads * sites, width), BF16),
        [after(lateral_asking_vectors, key_parts[0])],
        hbm=(0,),
        scratch=[pltpu.VMEM((rows, sites, embed), BF16), pltpu.SemaphoreType.DMA((1,))],
    )
    if middle:
        key_parts += send_all(key_parts, pos_count, middle)
    near = sum(part.shape[1] for part in key_parts)
    partial = call(
        functools.partial(logits_kernel, len(key_parts)),
        jax.ShapeDtypeStruct((heads * sites, near), F32),
        [masked, *key_parts],
    )
    value_first[-1] = after(value_first[-1], masked)
    value_own = lay_together(
        value_first, [0, *range(size - 1, size - 2, -1), *range(1, size - 2), *range(max(size - 2, 1), size - 1)]
    )
    value_parts = [value_own]
    if middle:
        value_parts += send_all(value_parts, pos_count, middle)
    if len(stages) > 2:
        far_parts = send_all(key_parts, pos_count, stages[2])
        partial = call(
            functools.partial(logits_kernel, len(far_parts)),
            jax.ShapeDtypeStruct((heads * sites, length), F32),
            [masked, *far_parts, partial],
        )
    padded = round_up(heads, 128)
    head_factors, order, own_select, slab_select, pick, spread = call(
        functools.partial(prepare_kernel, heads, sites, stages),
        (
            jax.ShapeDtypeStruct((head_rows + 8, 128), F32),
            jax.ShapeDtypeStruct((length, length), BF16),
            jax.ShapeDtypeStruct((sites, length), F32),
            jax.ShapeDtypeStruct((length, slab_width), F32),
            jax.ShapeDtypeStruct((embed, padded), BF16),
            jax.ShapeDtypeStruct((padded, embed), BF16),
        ),
        [after(scalars, partial), regression_factors, regression_offset],
        smem=(0, 1, 2),
    )
    if seq_count == 2:
        partials = [partial, after(lax.ppermute(partial, "seq", swap), order)]
    else:
        partials = [lax.psum(partial, "seq")]
    shares, pair_local = call(
        functools.partial(
            softmax_kernel, 1.0 / (math.sqrt(head) * math.sqrt(rows * seq_count)), heads
        ),
        (
            jax.ShapeDtypeStruct((heads * sites, length), BF16),
            jax.ShapeDtypeStruct((pos_count, head_rows + sites, length), F32),
        ),
        [*partials, head_factors, order],
        scratch=[pltpu.VMEM((head_rows + sites, length), F32)],
    )
    if len(stages) > 2:
        value_parts = value_parts[:1] + [after(part, pair_local) for part in value_parts[1:]]
        value_parts += send_all(value_parts, pos_count, stages[2])
    hidden, normed, one = call(
        functools.partial(mix_kernel, head, len(value_parts)),
        (
            jax.ShapeDtypeStruct((cells, embed), F32),
            jax.ShapeDtypeStruct((cells, embed), BF16),
            jax.ShapeDtypeStruct((1, columns), BF16),
        ),
        [
            shares,
            *value_parts,
            lateral_closing_linear,
            skip_stream_input,
            upright_normalizer_multiplier,
        ],
        scratch=[pltpu.VMEM((cells, embed), F32)],
    )
    pair_all = lax.all_to_all(pair_local, "pos", split_axis=0, concat_axis=0, tiled=True)
    pairing_chances = call(
        functools.partial(contact_kernel, heads),
        jax.ShapeDtypeStruct((sites, slab_width), F32),
        [pair_all, head_factors, own_select, slab_select],
        scratch=[pltpu.VMEM((head_rows + sites, length), F32)],
    )
    if swapped:
        normed_all = [normed, lax.ppermute(normed, "seq", swap)]
        weight = upright_threefold_linear * one
    else:
        normed_all = [normed]
        weight = lax.all_gather(upright_threefold_linear, "seq", axis=1, tiled=True)
    projected = call(
        functools.partial(project_kernel, len(normed_all)),
        jax.ShapeDtypeStruct((cells * len(normed_all), weight.shape[1]), BF16),
        [*normed_all, weight],
    )
    if swapped:
        column, column_inputs = swapped_column_kernel, [
            projected,
            lax.ppermute(projected, "seq", swap),
        ]
    else:
        key_value = lax.all_gather(projected[:, embed:], "seq", axis=0, tiled=True)
        column, column_inputs = column_kernel, [projected[:, :embed], key_value]
    alignment_output = call(
        functools.partial(column, 1.0 / math.sqrt(head)),
        jax.ShapeDtypeStruct((rows, sites, embed), BF16),
        [
            *column_inputs,
            hidden,
            after(upright_closing_linear, projected),
            pick,
            spread,
        ],
        scratch=[
            pltpu.VMEM((cells * rows * seq_count, embed), F32),
            pltpu.VMEM((cells, embed), F32),
        ],
    )
    return alignment_output, pairing_chances


def solution(mesh):
    cells = P("seq", "pos", None)
    return jax.shard_map(
        per_device,
        mesh=mesh,
        in_specs=(cells, cells, cells, cells, P(), P(), P(None, "seq"), P(), P(), P()),
        out_specs=(cells, P("pos", "seq")),
        check_vma=False,
    )
```

```python
import functools
import math

import jax
import jax.numpy as jnp
import numpy as np
from jax import lax
from jax.experimental import pallas as pl
from jax.experimental.pallas import tpu as pltpu
from jax.sharding import PartitionSpec as P

F32 = jnp.float32
BF16 = jnp.bfloat16
HIGHEST = lax.Precision.HIGHEST
LANE_BLOCK = 256


def dot_nn(a, b, precision=None):
    return lax.dot_general(
        a, b, (((1,), (0,)), ((), ())), precision=precision, preferred_element_type=F32
    )


def dot_nt(a, b, precision=None):
    return lax.dot_general(
        a, b, (((1,), (1,)), ((), ())), precision=precision, preferred_element_type=F32
    )


def round_up(n, m):
    return -(-n // m) * m


def lane_block(embed, head):
    return LANE_BLOCK if embed % LANE_BLOCK == 0 and LANE_BLOCK % head == 0 else head


def arrival_place(index, column, stages, sites):
    block, place, span = column // sites, column % sites, 1
    for stride, size in stages:
        digit = (block // span) % size
        place = place + ((index // stride) % size + size - digit) % size * (stride * sites)
        span *= size
    return place


def fetch(pairs, sems):
    copies = [pltpu.make_async_copy(src, dst, sems.at[i]) for i, (src, dst) in enumerate(pairs)]
    for copy in copies:
        copy.start()
    for copy in copies:
        copy.wait()


def query_kernel(head, q_hbm, masked_ref, q_ref, sems):
    rows, sites, embed = q_ref.shape
    width = masked_ref.shape[2]
    group = width // head
    span = group * sites
    fetch([(q_hbm, q_ref)], sems)
    lane_head = lax.broadcasted_iota(jnp.int32, (span, width), 1) // head
    row_head = lax.broadcasted_iota(jnp.int32, (span, width), 0) // sites
    own_head = lane_head == row_head
    for block in range(embed // width):
        for r in range(rows):
            q = q_ref[r, :, block * width : (block + 1) * width].astype(F32)
            q = jnp.where(own_head, jnp.concatenate([q] * group, axis=0), 0.0).astype(BF16)
            masked_ref[r, block * span : (block + 1) * span, :] = q


def prepare_kernel(heads, sites, stages, scalar_ref, factor_ref, offset_ref, *refs):
    head_ref, order_ref, own_ref, slab_ref, pick_ref, spread_ref = refs
    head = pick_ref.shape[0] // heads
    row = lax.broadcasted_iota(jnp.int32, pick_ref.shape, 0)
    lane = lax.broadcasted_iota(jnp.int32, pick_ref.shape, 1)
    pick_ref[...] = (row // head == lane).astype(BF16)
    row = lax.broadcasted_iota(jnp.int32, spread_ref.shape, 0)
    lane = lax.broadcasted_iota(jnp.int32, spread_ref.shape, 1)
    spread_ref[...] = (lane // head == row).astype(BF16)
    row = lax.broadcasted_iota(jnp.int32, head_ref.shape, 0)
    factors = jnp.zeros(head_ref.shape, F32)
    for h in range(heads):
        factors = jnp.where(row == h, factor_ref[h], factors)
    head_ref[...] = jnp.where(row == round_up(heads, 8), offset_ref[0], factors)
    seq_index, pos_index = scalar_ref[0], scalar_ref[1]
    length = order_ref.shape[0]
    row = lax.broadcasted_iota(jnp.int32, (length, length), 0)
    lane = lax.broadcasted_iota(jnp.int32, (length, length), 1)
    order_ref[...] = (arrival_place(pos_index, row, stages, sites) == lane).astype(BF16)
    row = lax.broadcasted_iota(jnp.int32, own_ref.shape, 0)
    lane = lax.broadcasted_iota(jnp.int32, own_ref.shape, 1)
    own_ref[...] = (row + pos_index * sites == lane).astype(F32)
    row = lax.broadcasted_iota(jnp.int32, slab_ref.shape, 0)
    lane = lax.broadcasted_iota(jnp.int32, slab_ref.shape, 1)
    slab_ref[...] = (row == lane + seq_index * slab_ref.shape[1]).astype(F32)


def logits_kernel(part_count, *refs):
    q_ref, k_refs, done_refs, out_ref = refs[0], refs[1 : 1 + part_count], refs[1 + part_count : -1], refs[-1]
    rows, _, width = q_ref.shape
    blocks = k_refs[0].shape[2] // width
    span = q_ref.shape[1] // blocks
    for block in range(blocks):
        cols = slice(block * width, (block + 1) * width)
        lines = slice(block * span, (block + 1) * span)
        total = None
        for r in range(rows):
            keys = jnp.concatenate([k[r, :, cols] for k in k_refs], axis=0)
            term = dot_nt(q_ref[r, lines, :], keys)
            total = term if total is None else total + term
        out_ref[lines, :] = jnp.concatenate([done[lines, :] for done in done_refs] + [total], axis=1)


def softmax_kernel(factor, heads, *refs):
    parts, (head_ref, order_ref, w_ref, pair_ref, held) = refs[:-5], refs[-5:]
    rows, length = w_ref.shape
    sites = rows // heads
    logits = parts[0][...]
    for part in parts[1:]:
        logits = logits + part[...]
    logits = logits * factor
    exponent = jnp.exp(logits - jnp.max(logits, axis=1, keepdims=True))
    shares = (exponent / jnp.sum(exponent, axis=1, keepdims=True)).astype(BF16)
    w_ref[...] = shares
    shares = shares.astype(F32)
    row_sum = jnp.sum(shares, axis=1, keepdims=True)
    lane = lax.broadcasted_iota(jnp.int32, (rows, length), 1)
    row = lax.broadcasted_iota(jnp.int32, (rows, length), 0) % sites
    both = (shares + jnp.where(lane == row, row_sum, 0.0)).reshape(heads, sites, length)
    head_rows = round_up(heads, 8)
    held[...] = jnp.zeros_like(held)
    held[0:heads, :] = jnp.sum(both, axis=1)
    merged = None
    for h in range(heads):
        term = shares[h * sites : (h + 1) * sites, :] * head_ref[h : h + 1, 0:1]
        merged = term if merged is None else merged + term
    held[head_rows : head_rows + sites, :] = merged
    rest, ordered = held[...], None
    for _ in range(3):
        part = rest.astype(BF16)
        rest = rest - part.astype(F32)
        term = dot_nn(part, order_ref[...])
        ordered = term if ordered is None else ordered + term
    pair_ref[...] = jnp.broadcast_to(ordered[None], pair_ref.shape)


def mix_kernel(head, v_count, *refs):
    w_ref, v_refs = refs[0], refs[1 : 1 + v_count]
    closing_ref, skip_ref, gain_ref, hidden_ref, normed_ref, one_ref, mixed = refs[1 + v_count :]
    one_ref[...] = jnp.ones_like(one_ref)
    rows, sites, embed = skip_ref.shape
    width = lane_block(embed, head)
    group = width // head
    lane_head = lax.broadcasted_iota(jnp.int32, (sites, width), 1) // head
    for block in range(embed // width):
        cols = slice(block * width, (block + 1) * width)
        shares = w_ref[block * group * sites : (block + 1) * group * sites, :]
        for r in range(rows):
            values = jnp.concatenate([v[r, :, cols] for v in v_refs], axis=0)
            product = dot_nn(shares, values)
            own = product[0:sites, :]
            for g in range(1, group):
                own = jnp.where(lane_head == g, product[g * sites : (g + 1) * sites, :], own)
            mixed[r * sites : (r + 1) * sites, cols] = own
    hidden = skip_ref[...].astype(F32).reshape(rows * sites, embed) + dot_nn(mixed[...].astype(BF16), closing_ref[...])
    hidden_ref[...] = hidden
    centered = hidden - jnp.mean(hidden, axis=1, keepdims=True)
    spread = jnp.mean(centered * centered, axis=1, keepdims=True)
    normed_ref[...] = (centered * lax.rsqrt(spread + 1e-05) * gain_ref[...].reshape(1, embed)).astype(BF16)


def project_kernel(part_count, *refs):
    parts, (weight_ref, out_ref) = refs[:part_count], refs[part_count:]
    normed = jnp.concatenate([part[...] for part in parts], axis=0)
    out_ref[...] = dot_nn(normed, weight_ref[...]).astype(BF16)


def column_attend(
    factor, query, keys, values, hidden_ref, closing_ref, pick_ref, spread_ref, out_ref, products, mixed
):
    rows, sites, embed = out_ref.shape
    pick = pick_ref[...]
    padded = pick.shape[1]
    seqs = len(keys)
    for s in range(rows):
        for t in range(seqs):
            at = (s * seqs + t) * sites
            products[at : at + sites, :] = query[s * sites : (s + 1) * sites, :] * keys[t]
    product = products[...]
    high = product.astype(BF16)
    low = (product - high.astype(F32)).astype(BF16)
    scores = (dot_nn(high, pick) + dot_nn(low, pick)) * factor
    exponent = jnp.exp(scores).reshape(rows, seqs, sites, padded)
    shares = (exponent / jnp.sum(exponent, axis=1, keepdims=True)).astype(BF16)
    wide = dot_nn(shares.reshape(rows * seqs * sites, padded), spread_ref[...])
    for s in range(rows):
        total = None
        for t in range(seqs):
            at = (s * seqs + t) * sites
            term = wide[at : at + sites, :] * values[t]
            total = term if total is None else total + term
        mixed[s * sites : (s + 1) * sites, :] = total
    out = hidden_ref[...] + dot_nn(mixed[...].astype(BF16), closing_ref[...])
    out_ref[...] = out.reshape(rows, sites, embed).astype(BF16)


def column_kernel(factor, query_ref, kv_ref, *refs):
    rows, sites, embed = refs[4].shape
    kv = kv_ref[...].astype(F32)
    seqs = kv.shape[0] // sites
    keys = [kv[t * sites : (t + 1) * sites, 0:embed] for t in range(seqs)]
    values = [kv[t * sites : (t + 1) * sites, embed:] for t in range(seqs)]
    column_attend(factor, query_ref[...].astype(F32), keys, values, *refs)


def swapped_column_kernel(factor, own_ref, other_ref, *refs):
    rows, sites, embed = refs[4].shape
    cells, columns = own_ref.shape
    half = cells // 2

    def piece(first_is_own, start, stop, at, size):
        found = []
        for block in range(2):
            lo, hi = max(start, block * columns), min(stop, (block + 1) * columns)
            if lo < hi:
                cols = slice(lo - block * columns, hi - block * columns)
                if (block == 0) == first_is_own:
                    found.append(own_ref[at : at + size, cols])
                else:
                    turned = (at + half) % cells
                    found.append(other_ref[turned : turned + size, cols])
        return jnp.concatenate(found, axis=1).astype(F32)

    def attend(first_is_own):
        query = piece(first_is_own, 0, embed, 0, half)
        keys, values = [], []
        for at in (0, half):
            key = piece(first_is_own, embed, 2 * embed, at, half)
            value = piece(first_is_own, 2 * embed, 3 * embed, at, half)
            for t in range(half // sites):
                keys.append(key[t * sites : (t + 1) * sites, :])
                values.append(value[t * sites : (t + 1) * sites, :])
        column_attend(factor, query, keys, values, *refs)

    seq_index = lax.axis_index("seq")
    pl.when(seq_index == 0)(functools.partial(attend, True))
    pl.when(seq_index == 1)(functools.partial(attend, False))


def contact_kernel(heads, pair_ref, factor_ref, own_ref, slab_ref, out_ref, held):
    count, step, length = pair_ref.shape
    head_rows = round_up(heads, 8)
    sites = step - head_rows
    blocks = slab_ref.shape[1] // sites
    total = pair_ref[0, 0:head_rows, :]
    for n in range(1, count):
        total = total + pair_ref[n, 0:head_rows, :]
    held[0:head_rows, :] = total
    held[head_rows:step, :] = pair_ref[lax.axis_index("pos"), head_rows:step, :]
    first = lax.axis_index("seq") * blocks
    table = jnp.concatenate(
        [pair_ref[first + n, head_rows:step, :] for n in range(blocks)], axis=0
    )
    amount = jnp.sum(total, axis=1, keepdims=True)
    real = lax.broadcasted_iota(jnp.int32, (head_rows, 1), 0) < heads
    share = jnp.where(real, factor_ref[0:head_rows, 0:1] / jnp.where(real, amount, 1.0), 0.0)
    slab = dot_nn(held[...], slab_ref[...], HIGHEST)
    own = dot_nt(own_ref[...], total * share, HIGHEST)
    mirrored = dot_nt(own_ref[...], table, HIGHEST)
    adjuster = dot_nn(own, slab[0:head_rows, :], HIGHEST)
    out_ref[...] = jax.nn.sigmoid(
        slab[head_rows:step, :] + mirrored - adjuster + factor_ref[head_rows : head_rows + 1, 0:1]
    )


def call(kernel, out_shape, operands, smem=(), hbm=(), scratch=(), bytes_accessed=1000000):
    vmem = pl.BlockSpec(memory_space=pltpu.VMEM)
    held = sum(math.prod(a.shape) * a.dtype.itemsize for a in [*operands, *jax.tree.leaves(out_shape)])
    held += sum(
        math.prod(a.shape) * np.dtype(a.dtype).itemsize
        for a in scratch
        if a.memory_space == pltpu.VMEM
    )
    limit = 2 * held + 4 * 1024 * 1024
    specs = [
        pl.BlockSpec(memory_space=pltpu.SMEM if i in smem else pl.ANY if i in hbm else pltpu.VMEM)
        for i in range(len(operands))
    ]
    return pl.pallas_call(
        kernel,
        out_shape=out_shape,
        in_specs=specs,
        out_specs=jax.tree.map(lambda _: vmem, out_shape),
        scratch_shapes=list(scratch),
        compiler_params=pltpu.CompilerParams(vmem_limit_bytes=limit),
        cost_estimate=pl.CostEstimate(
            flops=1000000, bytes_accessed=bytes_accessed, transcendentals=0
        ),
    )(*operands)


def stages_of(count):
    stages, stride = [], 1
    while count > 1 and len(stages) < 2 and count % 2 == 0:
        stages.append((stride, 2))
        stride, count = stride * 2, count // 2
    if count > 1:
        stages.append((stride, count))
    return stages[::-1]


def send_pos(array, count, stride, size, delta):
    pairs = []
    for p in range(count):
        a = (p // stride) % size
        pairs.append((p, p + ((a + delta) % size - a) * stride))
    return lax.ppermute(array, "pos", pairs)


def send_all(parts, count, stage):
    stride, size = stage
    return [send_pos(part, count, stride, size, delta) for delta in range(1, size) for part in parts]


def lay_together(parts, order):
    size = parts[0].shape[1]
    whole = jnp.zeros((parts[0].shape[0], size * len(parts), parts[0].shape[2]), parts[0].dtype)
    for at in order:
        whole = lax.dynamic_update_slice(whole, parts[at], (0, at * size, 0))
    return whole


def after(array, *others):
    return lax.optimization_barrier((array, *others))[0]


def per_device(
    skip_stream_input,
    lateral_asking_vectors,
    lateral_matched_vectors,
    lateral_carried_vectors,
    lateral_closing_linear,
    upright_normalizer_multiplier,
    upright_threefold_linear,
    upright_closing_linear,
    regression_factors,
    regression_offset,
):
    rows, sites, embed = lateral_asking_vectors.shape
    heads = regression_factors.shape[0]
    head = embed // heads
    seq_count = lax.axis_size("seq")
    pos_count = lax.axis_size("pos")
    length = sites * pos_count
    slab_width = length // seq_count
    cells = rows * sites
    pos_index = lax.axis_index("pos").astype(jnp.int32)
    seq_index = lax.axis_index("seq").astype(jnp.int32)
    swap = [(s, 1 - s) for s in range(2)]
    columns = upright_threefold_linear.shape[1]
    swapped = seq_count == 2 and columns % 128 == 0

    stages = stages_of(pos_count)
    outer = stages[0]
    size = outer[1]
    middle = stages[1] if len(stages) > 1 else None

    scalars = jnp.stack([seq_index, pos_index])
    head_rows = round_up(heads, 8)
    width = lane_block(embed, head)
    key_first = [lateral_matched_vectors] + send_all([lateral_matched_vectors], pos_count, outer)
    key_parts = [lay_together(key_first, [0, 1, *range(3, size), *range(2, min(size, 3))])]
    value_first = [after(lateral_carried_vectors, key_parts[0])]
    value_first += [
        send_pos(lateral_carried_vectors, pos_count, *outer, delta) for delta in range(outer[1] - 1, 0, -1)
    ][::-1]
    masked = call(
        functools.partial(query_kernel, head),
        jax.ShapeDtypeStruct((rows, heads * sites, width), BF16),
        [after(lateral_asking_vectors, key_parts[0])],
        hbm=(0,),
        scratch=[pltpu.VMEM((rows, sites, embed), BF16), pltpu.SemaphoreType.DMA((1,))],
    )
    if middle:
        key_parts += send_all(key_parts, pos_count, middle)
    near = sum(part.shape[1] for part in key_parts)
    partial = call(
        functools.partial(logits_kernel, len(key_parts)),
        jax.ShapeDtypeStruct((heads * sites, near), F32),
        [masked, *key_parts],
    )
    value_first[-1] = after(value_first[-1], masked)
    value_own = lay_together(
        value_first, [0, *range(size - 1, size - 2, -1), *range(1, size - 2), *range(max(size - 2, 1), size - 1)]
    )
    value_parts = [value_own]
    if middle:
        value_parts += send_all(value_parts, pos_count, middle)
    if len(stages) > 2:
        late_parts = [after(key_parts[0], *key_parts[1:])] + key_parts[1:]
        far_parts = send_all(late_parts, pos_count, stages[2])
        partial = call(
            functools.partial(logits_kernel, len(far_parts)),
            jax.ShapeDtypeStruct((heads * sites, length), F32),
            [masked, *far_parts, partial],
        )
    padded = round_up(heads, 128)
    head_factors, order, own_select, slab_select, pick, spread = call(
        functools.partial(prepare_kernel, heads, sites, stages),
        (
            jax.ShapeDtypeStruct((head_rows + 8, 128), F32),
            jax.ShapeDtypeStruct((length, length), BF16),
            jax.ShapeDtypeStruct((sites, length), F32),
            jax.ShapeDtypeStruct((length, slab_width), F32),
            jax.ShapeDtypeStruct((embed, padded), BF16),
            jax.ShapeDtypeStruct((padded, embed), BF16),
        ),
        [after(scalars, partial), regression_factors, regression_offset],
        smem=(0, 1, 2),
    )
    if seq_count == 2:
        partials = [partial, after(lax.ppermute(partial, "seq", swap), order)]
    else:
        partials = [lax.psum(partial, "seq")]
    shares, pair_local = call(
        functools.partial(
            softmax_kernel, 1.0 / (math.sqrt(head) * math.sqrt(rows * seq_count)), heads
        ),
        (
            jax.ShapeDtypeStruct((heads * sites, length), BF16),
            jax.ShapeDtypeStruct((pos_count, head_rows + sites, length), F32),
        ),
        [*partials, head_factors, order],
        scratch=[pltpu.VMEM((head_rows + sites, length), F32)],
    )
    if len(stages) > 2:
        late_parts = [after(part, pair_local, *value_parts[1:]) for part in value_parts]
        value_parts = value_parts + send_all(late_parts, pos_count, stages[2])
    hidden, normed, one = call(
        functools.partial(mix_kernel, head, len(value_parts)),
        (
            jax.ShapeDtypeStruct((cells, embed), F32),
            jax.ShapeDtypeStruct((cells, embed), BF16),
            jax.ShapeDtypeStruct((1, columns), BF16),
        ),
        [
            shares,
            *value_parts,
            lateral_closing_linear,
            skip_stream_input,
            upright_normalizer_multiplier,
        ],
        scratch=[pltpu.VMEM((cells, embed), F32)],
    )
    pair_all = lax.all_to_all(pair_local, "pos", split_axis=0, concat_axis=0, tiled=True)
    pairing_chances = call(
        functools.partial(contact_kernel, heads),
        jax.ShapeDtypeStruct((sites, slab_width), F32),
        [pair_all, head_factors, own_select, slab_select],
        scratch=[pltpu.VMEM((head_rows + sites, length), F32)],
    )
    if swapped:
        normed_all = [normed, lax.ppermute(normed, "seq", swap)]
        weight = upright_threefold_linear * one
    else:
        normed_all = [normed]
        weight = lax.all_gather(upright_threefold_linear, "seq", axis=1, tiled=True)
    projected = call(
        functools.partial(project_kernel, len(normed_all)),
        jax.ShapeDtypeStruct((cells * len(normed_all), weight.shape[1]), BF16),
        [*normed_all, weight],
    )
    if swapped:
        column, column_inputs = swapped_column_kernel, [
            projected,
            lax.ppermute(projected, "seq", swap),
        ]
    else:
        key_value = lax.all_gather(projected[:, embed:], "seq", axis=0, tiled=True)
        column, column_inputs = column_kernel, [projected[:, :embed], key_value]
    alignment_output = call(
        functools.partial(column, 1.0 / math.sqrt(head)),
        jax.ShapeDtypeStruct((rows, sites, embed), BF16),
        [
            *column_inputs,
            hidden,
            after(upright_closing_linear, projected),
            pick,
            spread,
        ],
        scratch=[
            pltpu.VMEM((cells * rows * seq_count, embed), F32),
            pltpu.VMEM((cells, embed), F32),
        ],
    )
    return alignment_output, pairing_chances


def solution(mesh):
    cells = P("seq", "pos", None)
    return jax.shard_map(
        per_device,
        mesh=mesh,
        in_specs=(cells, cells, cells, cells, P(), P(), P(None, "seq"), P(), P(), P()),
        out_specs=(cells, P("pos", "seq")),
        check_vma=False,
    )
```

```python
import functools
import math

import jax
import jax.numpy as jnp
import numpy as np
from jax import lax
from jax.experimental import pallas as pl
from jax.experimental.pallas import tpu as pltpu
from jax.sharding import PartitionSpec as P

F32 = jnp.float32
BF16 = jnp.bfloat16
HIGHEST = lax.Precision.HIGHEST
LANE_BLOCK = 256


def dot_nn(a, b, precision=None):
    return lax.dot_general(
        a, b, (((1,), (0,)), ((), ())), precision=precision, preferred_element_type=F32
    )


def dot_nt(a, b, precision=None):
    return lax.dot_general(
        a, b, (((1,), (1,)), ((), ())), precision=precision, preferred_element_type=F32
    )


def round_up(n, m):
    return -(-n // m) * m


def lane_block(embed, head):
    return LANE_BLOCK if embed % LANE_BLOCK == 0 and LANE_BLOCK % head == 0 else head


def arrival_place(index, column, stages, sites):
    block, place, span = column // sites, column % sites, 1
    for stride, size in stages:
        digit = (block // span) % size
        place = place + ((index // stride) % size + size - digit) % size * (stride * sites)
        span *= size
    return place


def fetch(pairs, sems):
    copies = [pltpu.make_async_copy(src, dst, sems.at[i]) for i, (src, dst) in enumerate(pairs)]
    for copy in copies:
        copy.start()
    for copy in copies:
        copy.wait()


def query_kernel(head, q_hbm, masked_ref, q_ref, sems):
    rows, sites, embed = q_ref.shape
    width = masked_ref.shape[2]
    group = width // head
    span = group * sites
    fetch([(q_hbm, q_ref)], sems)
    lane_head = lax.broadcasted_iota(jnp.int32, (span, width), 1) // head
    row_head = lax.broadcasted_iota(jnp.int32, (span, width), 0) // sites
    own_head = lane_head == row_head
    for block in range(embed // width):
        for r in range(rows):
            q = q_ref[r, :, block * width : (block + 1) * width].astype(F32)
            q = jnp.where(own_head, jnp.concatenate([q] * group, axis=0), 0.0).astype(BF16)
            masked_ref[r, block * span : (block + 1) * span, :] = q


def prepare_kernel(heads, sites, stages, scalar_ref, factor_ref, offset_ref, *refs):
    head_ref, order_ref, own_ref, slab_ref, pick_ref, spread_ref = refs
    head = pick_ref.shape[0] // heads
    row = lax.broadcasted_iota(jnp.int32, pick_ref.shape, 0)
    lane = lax.broadcasted_iota(jnp.int32, pick_ref.shape, 1)
    pick_ref[...] = (row // head == lane).astype(BF16)
    row = lax.broadcasted_iota(jnp.int32, spread_ref.shape, 0)
    lane = lax.broadcasted_iota(jnp.int32, spread_ref.shape, 1)
    spread_ref[...] = (lane // head == row).astype(BF16)
    row = lax.broadcasted_iota(jnp.int32, head_ref.shape, 0)
    factors = jnp.zeros(head_ref.shape, F32)
    for h in range(heads):
        factors = jnp.where(row == h, factor_ref[h], factors)
    head_ref[...] = jnp.where(row == round_up(heads, 8), offset_ref[0], factors)
    seq_index, pos_index = scalar_ref[0], scalar_ref[1]
    length = order_ref.shape[0]
    row = lax.broadcasted_iota(jnp.int32, (length, length), 0)
    lane = lax.broadcasted_iota(jnp.int32, (length, length), 1)
    order_ref[...] = (arrival_place(pos_index, row, stages, sites) == lane).astype(BF16)
    row = lax.broadcasted_iota(jnp.int32, own_ref.shape, 0)
    lane = lax.broadcasted_iota(jnp.int32, own_ref.shape, 1)
    own_ref[...] = (row + pos_index * sites == lane).astype(F32)
    row = lax.broadcasted_iota(jnp.int32, slab_ref.shape, 0)
    lane = lax.broadcasted_iota(jnp.int32, slab_ref.shape, 1)
    slab_ref[...] = (row == lane + seq_index * slab_ref.shape[1]).astype(F32)


def logits_kernel(part_count, *refs):
    q_ref, k_refs, done_refs, out_ref = refs[0], refs[1 : 1 + part_count], refs[1 + part_count : -1], refs[-1]
    rows, _, width = q_ref.shape
    blocks = k_refs[0].shape[2] // width
    span = q_ref.shape[1] // blocks
    for block in range(blocks):
        cols = slice(block * width, (block + 1) * width)
        lines = slice(block * span, (block + 1) * span)
        total = None
        for r in range(rows):
            keys = jnp.concatenate([k[r, :, cols] for k in k_refs], axis=0)
            term = dot_nt(q_ref[r, lines, :], keys)
            total = term if total is None else total + term
        out_ref[lines, :] = jnp.concatenate([done[lines, :] for done in done_refs] + [total], axis=1)


def softmax_kernel(factor, heads, *refs):
    parts, (head_ref, order_ref, w_ref, pair_ref, held) = refs[:-5], refs[-5:]
    rows, length = w_ref.shape
    sites = rows // heads
    logits = parts[0][...]
    for part in parts[1:]:
        logits = logits + part[...]
    logits = logits * factor
    exponent = jnp.exp(logits - jnp.max(logits, axis=1, keepdims=True))
    shares = (exponent / jnp.sum(exponent, axis=1, keepdims=True)).astype(BF16)
    w_ref[...] = shares
    shares = shares.astype(F32)
    row_sum = jnp.sum(shares, axis=1, keepdims=True)
    lane = lax.broadcasted_iota(jnp.int32, (rows, length), 1)
    row = lax.broadcasted_iota(jnp.int32, (rows, length), 0) % sites
    both = (shares + jnp.where(lane == row, row_sum, 0.0)).reshape(heads, sites, length)
    head_rows = round_up(heads, 8)
    held[...] = jnp.zeros_like(held)
    held[0:heads, :] = jnp.sum(both, axis=1)
    merged = None
    for h in range(heads):
        term = shares[h * sites : (h + 1) * sites, :] * head_ref[h : h + 1, 0:1]
        merged = term if merged is None else merged + term
    held[head_rows : head_rows + sites, :] = merged
    rest, ordered = held[...], None
    for _ in range(3):
        part = rest.astype(BF16)
        rest = rest - part.astype(F32)
        term = dot_nn(part, order_ref[...])
        ordered = term if ordered is None else ordered + term
    pair_ref[...] = jnp.broadcast_to(ordered[None], pair_ref.shape)


def mix_kernel(head, v_count, *refs):
    w_ref, v_refs = refs[0], refs[1 : 1 + v_count]
    closing_ref, skip_ref, gain_ref, hidden_ref, normed_ref, one_ref, mixed = refs[1 + v_count :]
    one_ref[...] = jnp.ones_like(one_ref)
    rows, sites, embed = skip_ref.shape
    width = lane_block(embed, head)
    group = width // head
    lane_head = lax.broadcasted_iota(jnp.int32, (sites, width), 1) // head
    for block in range(embed // width):
        cols = slice(block * width, (block + 1) * width)
        shares = w_ref[block * group * sites : (block + 1) * group * sites, :]
        for r in range(rows):
            values = jnp.concatenate([v[r, :, cols] for v in v_refs], axis=0)
            product = dot_nn(shares, values)
            own = product[0:sites, :]
            for g in range(1, group):
                own = jnp.where(lane_head == g, product[g * sites : (g + 1) * sites, :], own)
            mixed[r * sites : (r + 1) * sites, cols] = own
    hidden = skip_ref[...].astype(F32).reshape(rows * sites, embed) + dot_nn(mixed[...].astype(BF16), closing_ref[...])
    hidden_ref[...] = hidden
    centered = hidden - jnp.mean(hidden, axis=1, keepdims=True)
    spread = jnp.mean(centered * centered, axis=1, keepdims=True)
    normed_ref[...] = (centered * lax.rsqrt(spread + 1e-05) * gain_ref[...].reshape(1, embed)).astype(BF16)


def project_kernel(part_count, *refs):
    parts, (weight_ref, out_ref) = refs[:part_count], refs[part_count:]
    normed = jnp.concatenate([part[...] for part in parts], axis=0)
    out_ref[...] = dot_nn(normed, weight_ref[...]).astype(BF16)


def column_attend(
    factor, query, keys, values, hidden_ref, closing_ref, pick_ref, spread_ref, out_ref, products, mixed
):
    rows, sites, embed = out_ref.shape
    pick = pick_ref[...]
    padded = pick.shape[1]
    seqs = len(keys)
    for s in range(rows):
        for t in range(seqs):
            at = (s * seqs + t) * sites
            products[at : at + sites, :] = query[s * sites : (s + 1) * sites, :] * keys[t]
    product = products[...]
    high = product.astype(BF16)
    low = (product - high.astype(F32)).astype(BF16)
    scores = (dot_nn(high, pick) + dot_nn(low, pick)) * factor
    exponent = jnp.exp(scores).reshape(rows, seqs, sites, padded)
    shares = (exponent / jnp.sum(exponent, axis=1, keepdims=True)).astype(BF16)
    wide = dot_nn(shares.reshape(rows * seqs * sites, padded), spread_ref[...])
    for s in range(rows):
        total = None
        for t in range(seqs):
            at = (s * seqs + t) * sites
            term = wide[at : at + sites, :] * values[t]
            total = term if total is None else total + term
        mixed[s * sites : (s + 1) * sites, :] = total
    out = hidden_ref[...] + dot_nn(mixed[...].astype(BF16), closing_ref[...])
    out_ref[...] = out.reshape(rows, sites, embed).astype(BF16)


def column_kernel(factor, query_ref, kv_ref, *refs):
    rows, sites, embed = refs[4].shape
    kv = kv_ref[...].astype(F32)
    seqs = kv.shape[0] // sites
    keys = [kv[t * sites : (t + 1) * sites, 0:embed] for t in range(seqs)]
    values = [kv[t * sites : (t + 1) * sites, embed:] for t in range(seqs)]
    column_attend(factor, query_ref[...].astype(F32), keys, values, *refs)


def swapped_column_kernel(factor, own_ref, other_ref, *refs):
    rows, sites, embed = refs[4].shape
    cells, columns = own_ref.shape
    half = cells // 2

    def piece(first_is_own, start, stop, at, size):
        found = []
        for block in range(2):
            lo, hi = max(start, block * columns), min(stop, (block + 1) * columns)
            if lo < hi:
                cols = slice(lo - block * columns, hi - block * columns)
                if (block == 0) == first_is_own:
                    found.append(own_ref[at : at + size, cols])
                else:
                    turned = (at + half) % cells
                    found.append(other_ref[turned : turned + size, cols])
        return jnp.concatenate(found, axis=1).astype(F32)

    def attend(first_is_own):
        query = piece(first_is_own, 0, embed, 0, half)
        keys, values = [], []
        for at in (0, half):
            key = piece(first_is_own, embed, 2 * embed, at, half)
            value = piece(first_is_own, 2 * embed, 3 * embed, at, half)
            for t in range(half // sites):
                keys.append(key[t * sites : (t + 1) * sites, :])
                values.append(value[t * sites : (t + 1) * sites, :])
        column_attend(factor, query, keys, values, *refs)

    seq_index = lax.axis_index("seq")
    pl.when(seq_index == 0)(functools.partial(attend, True))
    pl.when(seq_index == 1)(functools.partial(attend, False))


def contact_kernel(heads, pair_ref, factor_ref, own_ref, slab_ref, out_ref, held):
    count, step, length = pair_ref.shape
    head_rows = round_up(heads, 8)
    sites = step - head_rows
    blocks = slab_ref.shape[1] // sites
    total = pair_ref[0, 0:head_rows, :]
    for n in range(1, count):
        total = total + pair_ref[n, 0:head_rows, :]
    held[0:head_rows, :] = total
    held[head_rows:step, :] = pair_ref[lax.axis_index("pos"), head_rows:step, :]
    first = lax.axis_index("seq") * blocks
    table = jnp.concatenate(
        [pair_ref[first + n, head_rows:step, :] for n in range(blocks)], axis=0
    )
    amount = jnp.sum(total, axis=1, keepdims=True)
    real = lax.broadcasted_iota(jnp.int32, (head_rows, 1), 0) < heads
    share = jnp.where(real, factor_ref[0:head_rows, 0:1] / jnp.where(real, amount, 1.0), 0.0)
    slab = dot_nn(held[...], slab_ref[...], HIGHEST)
    own = dot_nt(own_ref[...], total * share, HIGHEST)
    mirrored = dot_nt(own_ref[...], table, HIGHEST)
    adjuster = dot_nn(own, slab[0:head_rows, :], HIGHEST)
    out_ref[...] = jax.nn.sigmoid(
        slab[head_rows:step, :] + mirrored - adjuster + factor_ref[head_rows : head_rows + 1, 0:1]
    )


def call(kernel, out_shape, operands, smem=(), hbm=(), scratch=(), bytes_accessed=1000000):
    vmem = pl.BlockSpec(memory_space=pltpu.VMEM)
    held = sum(math.prod(a.shape) * a.dtype.itemsize for a in [*operands, *jax.tree.leaves(out_shape)])
    held += sum(
        math.prod(a.shape) * np.dtype(a.dtype).itemsize
        for a in scratch
        if a.memory_space == pltpu.VMEM
    )
    limit = 2 * held + 4 * 1024 * 1024
    specs = [
        pl.BlockSpec(memory_space=pltpu.SMEM if i in smem else pl.ANY if i in hbm else pltpu.VMEM)
        for i in range(len(operands))
    ]
    return pl.pallas_call(
        kernel,
        out_shape=out_shape,
        in_specs=specs,
        out_specs=jax.tree.map(lambda _: vmem, out_shape),
        scratch_shapes=list(scratch),
        compiler_params=pltpu.CompilerParams(vmem_limit_bytes=limit),
        cost_estimate=pl.CostEstimate(
            flops=1000000, bytes_accessed=bytes_accessed, transcendentals=0
        ),
    )(*operands)


def stages_of(count):
    stages, stride = [], 1
    while count > 1 and len(stages) < 2 and count % 2 == 0:
        stages.append((stride, 2))
        stride, count = stride * 2, count // 2
    if count > 1:
        stages.append((stride, count))
    return stages[::-1]


def send_pos(array, count, stride, size, delta):
    pairs = []
    for p in range(count):
        a = (p // stride) % size
        pairs.append((p, p + ((a + delta) % size - a) * stride))
    return lax.ppermute(array, "pos", pairs)


def send_all(parts, count, stage):
    stride, size = stage
    return [send_pos(part, count, stride, size, delta) for delta in range(1, size) for part in parts]


def lay_together(parts, order):
    size = parts[0].shape[1]
    whole = jnp.zeros((parts[0].shape[0], size * len(parts), parts[0].shape[2]), parts[0].dtype)
    for at in order:
        whole = lax.dynamic_update_slice(whole, parts[at], (0, at * size, 0))
    return whole


def after(array, *others):
    return lax.optimization_barrier((array, *others))[0]


def per_device(
    skip_stream_input,
    lateral_asking_vectors,
    lateral_matched_vectors,
    lateral_carried_vectors,
    lateral_closing_linear,
    upright_normalizer_multiplier,
    upright_threefold_linear,
    upright_closing_linear,
    regression_factors,
    regression_offset,
):
    rows, sites, embed = lateral_asking_vectors.shape
    heads = regression_factors.shape[0]
    head = embed // heads
    seq_count = lax.axis_size("seq")
    pos_count = lax.axis_size("pos")
    length = sites * pos_count
    slab_width = length // seq_count
    cells = rows * sites
    pos_index = lax.axis_index("pos").astype(jnp.int32)
    seq_index = lax.axis_index("seq").astype(jnp.int32)
    swap = [(s, 1 - s) for s in range(2)]
    columns = upright_threefold_linear.shape[1]
    swapped = seq_count == 2 and columns % 128 == 0

    stages = stages_of(pos_count)
    outer = stages[0]
    size = outer[1]
    middle = stages[1] if len(stages) > 1 else None

    scalars = jnp.stack([seq_index, pos_index])
    head_rows = round_up(heads, 8)
    width = lane_block(embed, head)
    key_first = [lateral_matched_vectors] + send_all([lateral_matched_vectors], pos_count, outer)
    key_parts = [lay_together(key_first, [0, 1, *range(3, size), *range(2, min(size, 3))])]
    value_first = [after(lateral_carried_vectors, key_parts[0])]
    value_first += [
        send_pos(lateral_carried_vectors, pos_count, *outer, delta) for delta in range(outer[1] - 1, 0, -1)
    ][::-1]
    masked = call(
        functools.partial(query_kernel, head),
        jax.ShapeDtypeStruct((rows, heads * sites, width), BF16),
        [after(lateral_asking_vectors, key_parts[0])],
        hbm=(0,),
        scratch=[pltpu.VMEM((rows, sites, embed), BF16), pltpu.SemaphoreType.DMA((1,))],
    )
    if middle:
        key_parts += send_all(key_parts, pos_count, middle)
    value_first[-1] = after(value_first[-1], masked)
    value_own = lay_together(
        value_first, [0, *range(size - 1, size - 2, -1), *range(1, size - 2), *range(max(size - 2, 1), size - 1)]
    )
    value_parts = [value_own]
    if middle:
        value_parts += send_all(value_parts, pos_count, middle)
    if len(stages) > 2:
        key_parts += send_all(key_parts, pos_count, stages[2])
    partial = call(
        functools.partial(logits_kernel, len(key_parts)),
        jax.ShapeDtypeStruct((heads * sites, length), F32),
        [masked, *key_parts],
    )
    padded = round_up(heads, 128)
    head_factors, order, own_select, slab_select, pick, spread = call(
        functools.partial(prepare_kernel, heads, sites, stages),
        (
            jax.ShapeDtypeStruct((head_rows + 8, 128), F32),
            jax.ShapeDtypeStruct((length, length), BF16),
            jax.ShapeDtypeStruct((sites, length), F32),
            jax.ShapeDtypeStruct((length, slab_width), F32),
            jax.ShapeDtypeStruct((embed, padded), BF16),
            jax.ShapeDtypeStruct((padded, embed), BF16),
        ),
        [after(scalars, partial), regression_factors, regression_offset],
        smem=(0, 1, 2),
    )
    if seq_count == 2:
        partials = [partial, after(lax.ppermute(partial, "seq", swap), order)]
    else:
        partials = [lax.psum(partial, "seq")]
    shares, pair_local = call(
        functools.partial(
            softmax_kernel, 1.0 / (math.sqrt(head) * math.sqrt(rows * seq_count)), heads
        ),
        (
            jax.ShapeDtypeStruct((heads * sites, length), BF16),
            jax.ShapeDtypeStruct((pos_count, head_rows + sites, length), F32),
        ),
        [*partials, head_factors, order],
        scratch=[pltpu.VMEM((head_rows + sites, length), F32)],
    )
    if len(stages) > 2:
        value_parts = value_parts[:1] + [after(part, pair_local) for part in value_parts[1:]]
        value_parts += send_all(value_parts, pos_count, stages[2])
    hidden, normed, one = call(
        functools.partial(mix_kernel, head, len(value_parts)),
        (
            jax.ShapeDtypeStruct((cells, embed), F32),
            jax.ShapeDtypeStruct((cells, embed), BF16),
            jax.ShapeDtypeStruct((1, columns), BF16),
        ),
        [
            shares,
            *value_parts,
            lateral_closing_linear,
            skip_stream_input,
            upright_normalizer_multiplier,
        ],
        scratch=[pltpu.VMEM((cells, embed), F32)],
    )
    pair_all = lax.all_to_all(pair_local, "pos", split_axis=0, concat_axis=0, tiled=True)
    pairing_chances = call(
        functools.partial(contact_kernel, heads),
        jax.ShapeDtypeStruct((sites, slab_width), F32),
        [pair_all, head_factors, own_select, slab_select],
        scratch=[pltpu.VMEM((head_rows + sites, length), F32)],
    )
    if swapped:
        normed_all = [normed, lax.ppermute(normed, "seq", swap)]
        weight = upright_threefold_linear * one
    else:
        normed_all = [normed]
        weight = lax.all_gather(upright_threefold_linear, "seq", axis=1, tiled=True)
    projected = call(
        functools.partial(project_kernel, len(normed_all)),
        jax.ShapeDtypeStruct((cells * len(normed_all), weight.shape[1]), BF16),
        [*normed_all, weight],
    )
    if swapped:
        column, column_inputs = swapped_column_kernel, [
            projected,
            lax.ppermute(projected, "seq", swap),
        ]
    else:
        key_value = lax.all_gather(projected[:, embed:], "seq", axis=0, tiled=True)
        column, column_inputs = column_kernel, [projected[:, :embed], key_value]
    alignment_output = call(
        functools.partial(column, 1.0 / math.sqrt(head)),
        jax.ShapeDtypeStruct((rows, sites, embed), BF16),
        [
            *column_inputs,
            hidden,
            after(upright_closing_linear, projected),
            pick,
            spread,
        ],
        scratch=[
            pltpu.VMEM((cells * rows * seq_count, embed), F32),
            pltpu.VMEM((cells, embed), F32),
        ],
    )
    return alignment_output, pairing_chances


def solution(mesh):
    cells = P("seq", "pos", None)
    return jax.shard_map(
        per_device,
        mesh=mesh,
        in_specs=(cells, cells, cells, cells, P(), P(), P(None, "seq"), P(), P(), P()),
        out_specs=(cells, P("pos", "seq")),
        check_vma=False,
    )
```

```python
import functools
import math

import jax
import jax.numpy as jnp
import numpy as np
from jax import lax
from jax.experimental import pallas as pl
from jax.experimental.pallas import tpu as pltpu
from jax.sharding import PartitionSpec as P

F32 = jnp.float32
BF16 = jnp.bfloat16
HIGHEST = lax.Precision.HIGHEST
LANE_BLOCK = 256


def dot_nn(a, b, precision=None):
    return lax.dot_general(
        a, b, (((1,), (0,)), ((), ())), precision=precision, preferred_element_type=F32
    )


def dot_nt(a, b, precision=None):
    return lax.dot_general(
        a, b, (((1,), (1,)), ((), ())), precision=precision, preferred_element_type=F32
    )


def round_up(n, m):
    return -(-n // m) * m


def lane_block(embed, head):
    return LANE_BLOCK if embed % LANE_BLOCK == 0 and LANE_BLOCK % head == 0 else head


def arrival_place(index, column, stages, sites):
    block, place, span = column // sites, column % sites, 1
    for stride, size in stages:
        digit = (block // span) % size
        place = place + ((index // stride) % size + size - digit) % size * (stride * sites)
        span *= size
    return place


def fetch(pairs, sems):
    copies = [pltpu.make_async_copy(src, dst, sems.at[i]) for i, (src, dst) in enumerate(pairs)]
    for copy in copies:
        copy.start()
    for copy in copies:
        copy.wait()


def query_kernel(head, q_hbm, masked_ref, q_ref, sems):
    rows, sites, embed = q_ref.shape
    width = masked_ref.shape[2]
    group = width // head
    span = group * sites
    fetch([(q_hbm, q_ref)], sems)
    lane_head = lax.broadcasted_iota(jnp.int32, (span, width), 1) // head
    row_head = lax.broadcasted_iota(jnp.int32, (span, width), 0) // sites
    own_head = lane_head == row_head
    for block in range(embed // width):
        for r in range(rows):
            q = q_ref[r, :, block * width : (block + 1) * width].astype(F32)
            q = jnp.where(own_head, jnp.concatenate([q] * group, axis=0), 0.0).astype(BF16)
            masked_ref[r, block * span : (block + 1) * span, :] = q


def prepare_kernel(heads, sites, stages, scalar_ref, factor_ref, offset_ref, *refs):
    head_ref, order_ref, own_ref, slab_ref, pick_ref, spread_ref = refs
    head = pick_ref.shape[0] // heads
    row = lax.broadcasted_iota(jnp.int32, pick_ref.shape, 0)
    lane = lax.broadcasted_iota(jnp.int32, pick_ref.shape, 1)
    pick_ref[...] = (row // head == lane).astype(BF16)
    row = lax.broadcasted_iota(jnp.int32, spread_ref.shape, 0)
    lane = lax.broadcasted_iota(jnp.int32, spread_ref.shape, 1)
    spread_ref[...] = (lane // head == row).astype(BF16)
    row = lax.broadcasted_iota(jnp.int32, head_ref.shape, 0)
    factors = jnp.zeros(head_ref.shape, F32)
    for h in range(heads):
        factors = jnp.where(row == h, factor_ref[h], factors)
    head_ref[...] = jnp.where(row == round_up(heads, 8), offset_ref[0], factors)
    seq_index, pos_index = scalar_ref[0], scalar_ref[1]
    length = order_ref.shape[0]
    row = lax.broadcasted_iota(jnp.int32, (length, length), 0)
    lane = lax.broadcasted_iota(jnp.int32, (length, length), 1)
    order_ref[...] = (arrival_place(pos_index, row, stages, sites) == lane).astype(BF16)
    row = lax.broadcasted_iota(jnp.int32, own_ref.shape, 0)
    lane = lax.broadcasted_iota(jnp.int32, own_ref.shape, 1)
    own_ref[...] = (row + pos_index * sites == lane).astype(F32)
    row = lax.broadcasted_iota(jnp.int32, slab_ref.shape, 0)
    lane = lax.broadcasted_iota(jnp.int32, slab_ref.shape, 1)
    slab_ref[...] = (row == lane + seq_index * slab_ref.shape[1]).astype(F32)


def logits_kernel(part_count, *refs):
    q_ref, k_refs, done_refs, out_ref = refs[0], refs[1 : 1 + part_count], refs[1 + part_count : -1], refs[-1]
    rows, _, width = q_ref.shape
    blocks = k_refs[0].shape[2] // width
    span = q_ref.shape[1] // blocks
    for block in range(blocks):
        cols = slice(block * width, (block + 1) * width)
        lines = slice(block * span, (block + 1) * span)
        total = None
        for r in range(rows):
            keys = jnp.concatenate([k[r, :, cols] for k in k_refs], axis=0)
            term = dot_nt(q_ref[r, lines, :], keys)
            total = term if total is None else total + term
        out_ref[lines, :] = jnp.concatenate([done[lines, :] for done in done_refs] + [total], axis=1)


def softmax_kernel(factor, heads, *refs):
    parts, (head_ref, order_ref, w_ref, pair_ref, held) = refs[:-5], refs[-5:]
    rows, length = w_ref.shape
    sites = rows // heads
    logits = parts[0][...]
    for part in parts[1:]:
        logits = logits + part[...]
    logits = logits * factor
    exponent = jnp.exp(logits - jnp.max(logits, axis=1, keepdims=True))
    shares = (exponent / jnp.sum(exponent, axis=1, keepdims=True)).astype(BF16)
    w_ref[...] = shares
    shares = shares.astype(F32)
    row_sum = jnp.sum(shares, axis=1, keepdims=True)
    lane = lax.broadcasted_iota(jnp.int32, (rows, length), 1)
    row = lax.broadcasted_iota(jnp.int32, (rows, length), 0) % sites
    both = (shares + jnp.where(lane == row, row_sum, 0.0)).reshape(heads, sites, length)
    head_rows = round_up(heads, 8)
    held[...] = jnp.zeros_like(held)
    held[0:heads, :] = jnp.sum(both, axis=1)
    merged = None
    for h in range(heads):
        term = shares[h * sites : (h + 1) * sites, :] * head_ref[h : h + 1, 0:1]
        merged = term if merged is None else merged + term
    held[head_rows : head_rows + sites, :] = merged
    rest, ordered = held[...], None
    for _ in range(3):
        part = rest.astype(BF16)
        rest = rest - part.astype(F32)
        term = dot_nn(part, order_ref[...])
        ordered = term if ordered is None else ordered + term
    pair_ref[...] = jnp.broadcast_to(ordered[None], pair_ref.shape)


def mix_kernel(head, v_count, *refs):
    w_ref, v_refs = refs[0], refs[1 : 1 + v_count]
    closing_ref, skip_ref, gain_ref, hidden_ref, normed_ref, one_ref, mixed = refs[1 + v_count :]
    one_ref[...] = jnp.ones_like(one_ref)
    rows, sites, embed = skip_ref.shape
    width = lane_block(embed, head)
    group = width // head
    lane_head = lax.broadcasted_iota(jnp.int32, (sites, width), 1) // head
    for block in range(embed // width):
        cols = slice(block * width, (block + 1) * width)
        shares = w_ref[block * group * sites : (block + 1) * group * sites, :]
        for r in range(rows):
            values = jnp.concatenate([v[r, :, cols] for v in v_refs], axis=0)
            product = dot_nn(shares, values)
            own = product[0:sites, :]
            for g in range(1, group):
                own = jnp.where(lane_head == g, product[g * sites : (g + 1) * sites, :], own)
            mixed[r * sites : (r + 1) * sites, cols] = own
    hidden = skip_ref[...].astype(F32).reshape(rows * sites, embed) + dot_nn(mixed[...].astype(BF16), closing_ref[...])
    hidden_ref[...] = hidden
    centered = hidden - jnp.mean(hidden, axis=1, keepdims=True)
    spread = jnp.mean(centered * centered, axis=1, keepdims=True)
    normed_ref[...] = (centered * lax.rsqrt(spread + 1e-05) * gain_ref[...].reshape(1, embed)).astype(BF16)


def project_kernel(part_count, *refs):
    parts, (weight_ref, out_ref) = refs[:part_count], refs[part_count:]
    normed = jnp.concatenate([part[...] for part in parts], axis=0)
    out_ref[...] = dot_nn(normed, weight_ref[...]).astype(BF16)


def column_attend(
    factor, query, keys, values, hidden_ref, closing_ref, pick_ref, spread_ref, out_ref, products, mixed
):
    rows, sites, embed = out_ref.shape
    pick = pick_ref[...]
    padded = pick.shape[1]
    seqs = len(keys)
    for s in range(rows):
        for t in range(seqs):
            at = (s * seqs + t) * sites
            products[at : at + sites, :] = query[s * sites : (s + 1) * sites, :] * keys[t]
    product = products[...]
    high = product.astype(BF16)
    low = (product - high.astype(F32)).astype(BF16)
    scores = (dot_nn(high, pick) + dot_nn(low, pick)) * factor
    exponent = jnp.exp(scores).reshape(rows, seqs, sites, padded)
    shares = (exponent / jnp.sum(exponent, axis=1, keepdims=True)).astype(BF16)
    wide = dot_nn(shares.reshape(rows * seqs * sites, padded), spread_ref[...])
    for s in range(rows):
        total = None
        for t in range(seqs):
            at = (s * seqs + t) * sites
            term = wide[at : at + sites, :] * values[t]
            total = term if total is None else total + term
        mixed[s * sites : (s + 1) * sites, :] = total
    out = hidden_ref[...] + dot_nn(mixed[...].astype(BF16), closing_ref[...])
    out_ref[...] = out.reshape(rows, sites, embed).astype(BF16)


def column_kernel(factor, query_ref, kv_ref, *refs):
    rows, sites, embed = refs[4].shape
    kv = kv_ref[...].astype(F32)
    seqs = kv.shape[0] // sites
    keys = [kv[t * sites : (t + 1) * sites, 0:embed] for t in range(seqs)]
    values = [kv[t * sites : (t + 1) * sites, embed:] for t in range(seqs)]
    column_attend(factor, query_ref[...].astype(F32), keys, values, *refs)


def swapped_column_kernel(factor, own_ref, other_ref, *refs):
    rows, sites, embed = refs[4].shape
    cells, columns = own_ref.shape
    half = cells // 2

    def piece(first_is_own, start, stop, at, size):
        found = []
        for block in range(2):
            lo, hi = max(start, block * columns), min(stop, (block + 1) * columns)
            if lo < hi:
                cols = slice(lo - block * columns, hi - block * columns)
                if (block == 0) == first_is_own:
                    found.append(own_ref[at : at + size, cols])
                else:
                    turned = (at + half) % cells
                    found.append(other_ref[turned : turned + size, cols])
        return jnp.concatenate(found, axis=1).astype(F32)

    def attend(first_is_own):
        query = piece(first_is_own, 0, embed, 0, half)
        keys, values = [], []
        for at in (0, half):
            key = piece(first_is_own, embed, 2 * embed, at, half)
            value = piece(first_is_own, 2 * embed, 3 * embed, at, half)
            for t in range(half // sites):
                keys.append(key[t * sites : (t + 1) * sites, :])
                values.append(value[t * sites : (t + 1) * sites, :])
        column_attend(factor, query, keys, values, *refs)

    seq_index = lax.axis_index("seq")
    pl.when(seq_index == 0)(functools.partial(attend, True))
    pl.when(seq_index == 1)(functools.partial(attend, False))


def contact_kernel(heads, pair_ref, factor_ref, own_ref, slab_ref, out_ref, held):
    count, step, length = pair_ref.shape
    head_rows = round_up(heads, 8)
    sites = step - head_rows
    blocks = slab_ref.shape[1] // sites
    total = pair_ref[0, 0:head_rows, :]
    for n in range(1, count):
        total = total + pair_ref[n, 0:head_rows, :]
    held[0:head_rows, :] = total
    held[head_rows:step, :] = pair_ref[lax.axis_index("pos"), head_rows:step, :]
    first = lax.axis_index("seq") * blocks
    table = jnp.concatenate(
        [pair_ref[first + n, head_rows:step, :] for n in range(blocks)], axis=0
    )
    amount = jnp.sum(total, axis=1, keepdims=True)
    real = lax.broadcasted_iota(jnp.int32, (head_rows, 1), 0) < heads
    share = jnp.where(real, factor_ref[0:head_rows, 0:1] / jnp.where(real, amount, 1.0), 0.0)
    slab = dot_nn(held[...], slab_ref[...], HIGHEST)
    own = dot_nt(own_ref[...], total * share, HIGHEST)
    mirrored = dot_nt(own_ref[...], table, HIGHEST)
    adjuster = dot_nn(own, slab[0:head_rows, :], HIGHEST)
    out_ref[...] = jax.nn.sigmoid(
        slab[head_rows:step, :] + mirrored - adjuster + factor_ref[head_rows : head_rows + 1, 0:1]
    )


def call(kernel, out_shape, operands, smem=(), hbm=(), scratch=(), bytes_accessed=1000000):
    vmem = pl.BlockSpec(memory_space=pltpu.VMEM)
    held = sum(math.prod(a.shape) * a.dtype.itemsize for a in [*operands, *jax.tree.leaves(out_shape)])
    held += sum(
        math.prod(a.shape) * np.dtype(a.dtype).itemsize
        for a in scratch
        if a.memory_space == pltpu.VMEM
    )
    limit = 2 * held + 4 * 1024 * 1024
    specs = [
        pl.BlockSpec(memory_space=pltpu.SMEM if i in smem else pl.ANY if i in hbm else pltpu.VMEM)
        for i in range(len(operands))
    ]
    return pl.pallas_call(
        kernel,
        out_shape=out_shape,
        in_specs=specs,
        out_specs=jax.tree.map(lambda _: vmem, out_shape),
        scratch_shapes=list(scratch),
        compiler_params=pltpu.CompilerParams(vmem_limit_bytes=limit),
        cost_estimate=pl.CostEstimate(
            flops=1000000, bytes_accessed=bytes_accessed, transcendentals=0
        ),
    )(*operands)


def stages_of(count):
    stages, stride = [], 1
    while count > 1 and len(stages) < 2 and count % 2 == 0:
        stages.append((stride, 2))
        stride, count = stride * 2, count // 2
    if count > 1:
        stages.append((stride, count))
    return stages[::-1]


def send_pos(array, count, stride, size, delta):
    pairs = []
    for p in range(count):
        a = (p // stride) % size
        pairs.append((p, p + ((a + delta) % size - a) * stride))
    return lax.ppermute(array, "pos", pairs)


def send_all(parts, count, stage):
    stride, size = stage
    return [send_pos(part, count, stride, size, delta) for delta in range(1, size) for part in parts]


def lay_together(parts, order):
    size = parts[0].shape[1]
    whole = jnp.zeros((parts[0].shape[0], size * len(parts), parts[0].shape[2]), parts[0].dtype)
    for at in order:
        whole = lax.dynamic_update_slice(whole, parts[at], (0, at * size, 0))
    return whole


def after(array, *others):
    return lax.optimization_barrier((array, *others))[0]


def per_device(
    skip_stream_input,
    lateral_asking_vectors,
    lateral_matched_vectors,
    lateral_carried_vectors,
    lateral_closing_linear,
    upright_normalizer_multiplier,
    upright_threefold_linear,
    upright_closing_linear,
    regression_factors,
    regression_offset,
):
    rows, sites, embed = lateral_asking_vectors.shape
    heads = regression_factors.shape[0]
    head = embed // heads
    seq_count = lax.axis_size("seq")
    pos_count = lax.axis_size("pos")
    length = sites * pos_count
    slab_width = length // seq_count
    cells = rows * sites
    pos_index = lax.axis_index("pos").astype(jnp.int32)
    seq_index = lax.axis_index("seq").astype(jnp.int32)
    swap = [(s, 1 - s) for s in range(2)]
    columns = upright_threefold_linear.shape[1]
    swapped = seq_count == 2 and columns % 128 == 0

    stages = stages_of(pos_count)
    outer = stages[0]
    size = outer[1]
    middle = stages[1] if len(stages) > 1 else None

    scalars = jnp.stack([seq_index, pos_index])
    head_rows = round_up(heads, 8)
    width = lane_block(embed, head)
    key_first = [lateral_matched_vectors] + send_all([lateral_matched_vectors], pos_count, outer)
    key_parts = [lay_together(key_first, [0, 1, *range(3, size), *range(2, min(size, 3))])]
    value_first = [after(lateral_carried_vectors, key_parts[0])]
    value_first += [
        send_pos(lateral_carried_vectors, pos_count, *outer, delta) for delta in range(outer[1] - 1, 0, -1)
    ][::-1]
    masked = call(
        functools.partial(query_kernel, head),
        jax.ShapeDtypeStruct((rows, heads * sites, width), BF16),
        [after(lateral_asking_vectors, key_parts[0])],
        hbm=(0,),
        scratch=[pltpu.VMEM((rows, sites, embed), BF16), pltpu.SemaphoreType.DMA((1,))],
    )
    if middle:
        key_parts += send_all(key_parts, pos_count, middle)
    value_first[-1] = after(value_first[-1], masked)
    value_own = lay_together(
        value_first, [0, *range(size - 1, size - 2, -1), *range(1, size - 2), *range(max(size - 2, 1), size - 1)]
    )
    value_parts = [value_own]
    if middle:
        value_parts += send_all(value_parts, pos_count, middle)
    if len(stages) > 2:
        late_parts = [after(key_parts[0], *key_parts[1:])] + key_parts[1:]
        key_parts += send_all(late_parts, pos_count, stages[2])
    partial = call(
        functools.partial(logits_kernel, len(key_parts)),
        jax.ShapeDtypeStruct((heads * sites, length), F32),
        [masked, *key_parts],
    )
    padded = round_up(heads, 128)
    head_factors, order, own_select, slab_select, pick, spread = call(
        functools.partial(prepare_kernel, heads, sites, stages),
        (
            jax.ShapeDtypeStruct((head_rows + 8, 128), F32),
            jax.ShapeDtypeStruct((length, length), BF16),
            jax.ShapeDtypeStruct((sites, length), F32),
            jax.ShapeDtypeStruct((length, slab_width), F32),
            jax.ShapeDtypeStruct((embed, padded), BF16),
            jax.ShapeDtypeStruct((padded, embed), BF16),
        ),
        [after(scalars, partial), regression_factors, regression_offset],
        smem=(0, 1, 2),
    )
    if seq_count == 2:
        partials = [partial, after(lax.ppermute(partial, "seq", swap), order)]
    else:
        partials = [lax.psum(partial, "seq")]
    shares, pair_local = call(
        functools.partial(
            softmax_kernel, 1.0 / (math.sqrt(head) * math.sqrt(rows * seq_count)), heads
        ),
        (
            jax.ShapeDtypeStruct((heads * sites, length), BF16),
            jax.ShapeDtypeStruct((pos_count, head_rows + sites, length), F32),
        ),
        [*partials, head_factors, order],
        scratch=[pltpu.VMEM((head_rows + sites, length), F32)],
    )
    if len(stages) > 2:
        value_parts = value_parts[:1] + [after(part, pair_local) for part in value_parts[1:]]
        value_parts += send_all(value_parts, pos_count, stages[2])
    hidden, normed, one = call(
        functools.partial(mix_kernel, head, len(value_parts)),
        (
            jax.ShapeDtypeStruct((cells, embed), F32),
            jax.ShapeDtypeStruct((cells, embed), BF16),
            jax.ShapeDtypeStruct((1, columns), BF16),
        ),
        [
            shares,
            *value_parts,
            lateral_closing_linear,
            skip_stream_input,
            upright_normalizer_multiplier,
        ],
        scratch=[pltpu.VMEM((cells, embed), F32)],
    )
    pair_all = lax.all_to_all(pair_local, "pos", split_axis=0, concat_axis=0, tiled=True)
    pairing_chances = call(
        functools.partial(contact_kernel, heads),
        jax.ShapeDtypeStruct((sites, slab_width), F32),
        [pair_all, head_factors, own_select, slab_select],
        scratch=[pltpu.VMEM((head_rows + sites, length), F32)],
    )
    if swapped:
        normed_all = [normed, lax.ppermute(normed, "seq", swap)]
        weight = upright_threefold_linear * one
    else:
        normed_all = [normed]
        weight = lax.all_gather(upright_threefold_linear, "seq", axis=1, tiled=True)
    projected = call(
        functools.partial(project_kernel, len(normed_all)),
        jax.ShapeDtypeStruct((cells * len(normed_all), weight.shape[1]), BF16),
        [*normed_all, weight],
    )
    if swapped:
        column, column_inputs = swapped_column_kernel, [
            projected,
            lax.ppermute(projected, "seq", swap),
        ]
    else:
        key_value = lax.all_gather(projected[:, embed:], "seq", axis=0, tiled=True)
        column, column_inputs = column_kernel, [projected[:, :embed], key_value]
    alignment_output = call(
        functools.partial(column, 1.0 / math.sqrt(head)),
        jax.ShapeDtypeStruct((rows, sites, embed), BF16),
        [
            *column_inputs,
            hidden,
            after(upright_closing_linear, projected),
            pick,
            spread,
        ],
        scratch=[
            pltpu.VMEM((cells * rows * seq_count, embed), F32),
            pltpu.VMEM((cells, embed), F32),
        ],
    )
    return alignment_output, pairing_chances


def solution(mesh):
    cells = P("seq", "pos", None)
    return jax.shard_map(
        per_device,
        mesh=mesh,
        in_specs=(cells, cells, cells, cells, P(), P(), P(None, "seq"), P(), P(), P()),
        out_specs=(cells, P("pos", "seq")),
        check_vma=False,
    )
```

```python
import functools
import math

import jax
import jax.numpy as jnp
import numpy as np
from jax import lax
from jax.experimental import pallas as pl
from jax.experimental.pallas import tpu as pltpu
from jax.sharding import PartitionSpec as P

F32 = jnp.float32
BF16 = jnp.bfloat16
HIGHEST = lax.Precision.HIGHEST
LANE_BLOCK = 256


def dot_nn(a, b, precision=None):
    return lax.dot_general(
        a, b, (((1,), (0,)), ((), ())), precision=precision, preferred_element_type=F32
    )


def dot_nt(a, b, precision=None):
    return lax.dot_general(
        a, b, (((1,), (1,)), ((), ())), precision=precision, preferred_element_type=F32
    )


def round_up(n, m):
    return -(-n // m) * m


def lane_block(embed, head):
    return LANE_BLOCK if embed % LANE_BLOCK == 0 and LANE_BLOCK % head == 0 else head


def arrival_place(index, column, stages, sites):
    block, place, span = column // sites, column % sites, 1
    for stride, size in stages:
        digit = (block // span) % size
        place = place + ((index // stride) % size + size - digit) % size * (stride * sites)
        span *= size
    return place


def fetch(pairs, sems):
    copies = [pltpu.make_async_copy(src, dst, sems.at[i]) for i, (src, dst) in enumerate(pairs)]
    for copy in copies:
        copy.start()
    for copy in copies:
        copy.wait()


def query_kernel(head, q_hbm, masked_ref, q_ref, sems):
    rows, sites, embed = q_ref.shape
    width = masked_ref.shape[2]
    group = width // head
    span = group * sites
    fetch([(q_hbm, q_ref)], sems)
    lane_head = lax.broadcasted_iota(jnp.int32, (span, width), 1) // head
    row_head = lax.broadcasted_iota(jnp.int32, (span, width), 0) // sites
    own_head = lane_head == row_head
    for block in range(embed // width):
        for r in range(rows):
            q = q_ref[r, :, block * width : (block + 1) * width].astype(F32)
            q = jnp.where(own_head, jnp.concatenate([q] * group, axis=0), 0.0).astype(BF16)
            masked_ref[r, block * span : (block + 1) * span, :] = q


def prepare_kernel(heads, sites, stages, scalar_ref, factor_ref, offset_ref, *refs):
    head_ref, order_ref, own_ref, slab_ref, pick_ref, spread_ref = refs
    head = pick_ref.shape[0] // heads
    row = lax.broadcasted_iota(jnp.int32, pick_ref.shape, 0)
    lane = lax.broadcasted_iota(jnp.int32, pick_ref.shape, 1)
    pick_ref[...] = (row // head == lane).astype(BF16)
    row = lax.broadcasted_iota(jnp.int32, spread_ref.shape, 0)
    lane = lax.broadcasted_iota(jnp.int32, spread_ref.shape, 1)
    spread_ref[...] = (lane // head == row).astype(BF16)
    row = lax.broadcasted_iota(jnp.int32, head_ref.shape, 0)
    factors = jnp.zeros(head_ref.shape, F32)
    for h in range(heads):
        factors = jnp.where(row == h, factor_ref[h], factors)
    head_ref[...] = jnp.where(row == round_up(heads, 8), offset_ref[0], factors)
    seq_index, pos_index = scalar_ref[0], scalar_ref[1]
    length = order_ref.shape[0]
    row = lax.broadcasted_iota(jnp.int32, (length, length), 0)
    lane = lax.broadcasted_iota(jnp.int32, (length, length), 1)
    order_ref[...] = (arrival_place(pos_index, row, stages, sites) == lane).astype(BF16)
    row = lax.broadcasted_iota(jnp.int32, own_ref.shape, 0)
    lane = lax.broadcasted_iota(jnp.int32, own_ref.shape, 1)
    own_ref[...] = (row + pos_index * sites == lane).astype(F32)
    row = lax.broadcasted_iota(jnp.int32, slab_ref.shape, 0)
    lane = lax.broadcasted_iota(jnp.int32, slab_ref.shape, 1)
    slab_ref[...] = (row == lane + seq_index * slab_ref.shape[1]).astype(F32)


def logits_kernel(part_count, *refs):
    q_ref, k_refs, done_refs, out_ref = refs[0], refs[1 : 1 + part_count], refs[1 + part_count : -1], refs[-1]
    rows, _, width = q_ref.shape
    blocks = k_refs[0].shape[2] // width
    span = q_ref.shape[1] // blocks
    for block in range(blocks):
        cols = slice(block * width, (block + 1) * width)
        lines = slice(block * span, (block + 1) * span)
        total = None
        for r in range(rows):
            keys = jnp.concatenate([k[r, :, cols] for k in k_refs], axis=0)
            term = dot_nt(q_ref[r, lines, :], keys)
            total = term if total is None else total + term
        out_ref[lines, :] = jnp.concatenate([done[lines, :] for done in done_refs] + [total], axis=1)


def softmax_kernel(factor, heads, *refs):
    parts, (head_ref, order_ref, w_ref, pair_ref, held) = refs[:-5], refs[-5:]
    rows, length = w_ref.shape
    sites = rows // heads
    logits = parts[0][...]
    for part in parts[1:]:
        logits = logits + part[...]
    logits = logits * factor
    exponent = jnp.exp(logits - jnp.max(logits, axis=1, keepdims=True))
    shares = (exponent / jnp.sum(exponent, axis=1, keepdims=True)).astype(BF16)
    w_ref[...] = shares
    shares = shares.astype(F32)
    row_sum = jnp.sum(shares, axis=1, keepdims=True)
    lane = lax.broadcasted_iota(jnp.int32, (rows, length), 1)
    row = lax.broadcasted_iota(jnp.int32, (rows, length), 0) % sites
    both = (shares + jnp.where(lane == row, row_sum, 0.0)).reshape(heads, sites, length)
    head_rows = round_up(heads, 8)
    held[...] = jnp.zeros_like(held)
    held[0:heads, :] = jnp.sum(both, axis=1)
    merged = None
    for h in range(heads):
        term = shares[h * sites : (h + 1) * sites, :] * head_ref[h : h + 1, 0:1]
        merged = term if merged is None else merged + term
    held[head_rows : head_rows + sites, :] = merged
    rest, ordered = held[...], None
    for _ in range(3):
        part = rest.astype(BF16)
        rest = rest - part.astype(F32)
        term = dot_nn(part, order_ref[...])
        ordered = term if ordered is None else ordered + term
    pair_ref[...] = jnp.broadcast_to(ordered[None], pair_ref.shape)


def mix_kernel(head, v_count, *refs):
    w_ref, v_refs = refs[0], refs[1 : 1 + v_count]
    closing_ref, skip_ref, gain_ref, hidden_ref, normed_ref, one_ref, mixed = refs[1 + v_count :]
    one_ref[...] = jnp.ones_like(one_ref)
    rows, sites, embed = skip_ref.shape
    width = lane_block(embed, head)
    group = width // head
    lane_head = lax.broadcasted_iota(jnp.int32, (sites, width), 1) // head
    for block in range(embed // width):
        cols = slice(block * width, (block + 1) * width)
        shares = w_ref[block * group * sites : (block + 1) * group * sites, :]
        for r in range(rows):
            values = jnp.concatenate([v[r, :, cols] for v in v_refs], axis=0)
            product = dot_nn(shares, values)
            own = product[0:sites, :]
            for g in range(1, group):
                own = jnp.where(lane_head == g, product[g * sites : (g + 1) * sites, :], own)
            mixed[r * sites : (r + 1) * sites, cols] = own
    hidden = skip_ref[...].astype(F32).reshape(rows * sites, embed) + dot_nn(mixed[...].astype(BF16), closing_ref[...])
    hidden_ref[...] = hidden
    centered = hidden - jnp.mean(hidden, axis=1, keepdims=True)
    spread = jnp.mean(centered * centered, axis=1, keepdims=True)
    normed_ref[...] = (centered * lax.rsqrt(spread + 1e-05) * gain_ref[...].reshape(1, embed)).astype(BF16)


def project_kernel(part_count, *refs):
    parts, (weight_ref, out_ref) = refs[:part_count], refs[part_count:]
    normed = jnp.concatenate([part[...] for part in parts], axis=0)
    out_ref[...] = dot_nn(normed, weight_ref[...]).astype(BF16)


def column_attend(
    factor, query, keys, values, hidden_ref, closing_ref, pick_ref, spread_ref, out_ref, products, mixed
):
    rows, sites, embed = out_ref.shape
    pick = pick_ref[...]
    padded = pick.shape[1]
    seqs = len(keys)
    for s in range(rows):
        own = query[s * sites : (s + 1) * sites, :]
        product = jnp.concatenate([own * key for key in keys], axis=0)
        high = product.astype(BF16)
        low = (product - high.astype(F32)).astype(BF16)
        at = s * seqs * sites
        products[at : at + seqs * sites, 0:padded] = dot_nn(high, pick) + dot_nn(low, pick)
    scores = products[:, 0:padded] * factor
    exponent = jnp.exp(scores).reshape(rows, seqs, sites, padded)
    shares = (exponent / jnp.sum(exponent, axis=1, keepdims=True)).astype(BF16)
    wide = dot_nn(shares.reshape(rows * seqs * sites, padded), spread_ref[...])
    for s in range(rows):
        total = None
        for t in range(seqs):
            at = (s * seqs + t) * sites
            term = wide[at : at + sites, :] * values[t]
            total = term if total is None else total + term
        mixed[s * sites : (s + 1) * sites, :] = total
    out = hidden_ref[...] + dot_nn(mixed[...].astype(BF16), closing_ref[...])
    out_ref[...] = out.reshape(rows, sites, embed).astype(BF16)


def column_kernel(factor, query_ref, kv_ref, *refs):
    rows, sites, embed = refs[4].shape
    kv = kv_ref[...].astype(F32)
    seqs = kv.shape[0] // sites
    keys = [kv[t * sites : (t + 1) * sites, 0:embed] for t in range(seqs)]
    values = [kv[t * sites : (t + 1) * sites, embed:] for t in range(seqs)]
    column_attend(factor, query_ref[...].astype(F32), keys, values, *refs)


def swapped_column_kernel(factor, own_ref, other_ref, *refs):
    rows, sites, embed = refs[4].shape
    cells, columns = own_ref.shape
    half = cells // 2

    def piece(first_is_own, start, stop, at, size):
        found = []
        for block in range(2):
            lo, hi = max(start, block * columns), min(stop, (block + 1) * columns)
            if lo < hi:
                cols = slice(lo - block * columns, hi - block * columns)
                if (block == 0) == first_is_own:
                    found.append(own_ref[at : at + size, cols])
                else:
                    turned = (at + half) % cells
                    found.append(other_ref[turned : turned + size, cols])
        return jnp.concatenate(found, axis=1).astype(F32)

    def attend(first_is_own):
        query = piece(first_is_own, 0, embed, 0, half)
        keys, values = [], []
        for at in (0, half):
            key = piece(first_is_own, embed, 2 * embed, at, half)
            value = piece(first_is_own, 2 * embed, 3 * embed, at, half)
            for t in range(half // sites):
                keys.append(key[t * sites : (t + 1) * sites, :])
                values.append(value[t * sites : (t + 1) * sites, :])
        column_attend(factor, query, keys, values, *refs)

    seq_index = lax.axis_index("seq")
    pl.when(seq_index == 0)(functools.partial(attend, True))
    pl.when(seq_index == 1)(functools.partial(attend, False))


def contact_kernel(heads, pair_ref, factor_ref, own_ref, slab_ref, out_ref, held):
    count, step, length = pair_ref.shape
    head_rows = round_up(heads, 8)
    sites = step - head_rows
    blocks = slab_ref.shape[1] // sites
    total = pair_ref[0, 0:head_rows, :]
    for n in range(1, count):
        total = total + pair_ref[n, 0:head_rows, :]
    held[0:head_rows, :] = total
    held[head_rows:step, :] = pair_ref[lax.axis_index("pos"), head_rows:step, :]
    first = lax.axis_index("seq") * blocks
    table = jnp.concatenate(
        [pair_ref[first + n, head_rows:step, :] for n in range(blocks)], axis=0
    )
    amount = jnp.sum(total, axis=1, keepdims=True)
    real = lax.broadcasted_iota(jnp.int32, (head_rows, 1), 0) < heads
    share = jnp.where(real, factor_ref[0:head_rows, 0:1] / jnp.where(real, amount, 1.0), 0.0)
    slab = dot_nn(held[...], slab_ref[...], HIGHEST)
    own = dot_nt(own_ref[...], total * share, HIGHEST)
    mirrored = dot_nt(own_ref[...], table, HIGHEST)
    adjuster = dot_nn(own, slab[0:head_rows, :], HIGHEST)
    out_ref[...] = jax.nn.sigmoid(
        slab[head_rows:step, :] + mirrored - adjuster + factor_ref[head_rows : head_rows + 1, 0:1]
    )


def call(kernel, out_shape, operands, smem=(), hbm=(), scratch=(), bytes_accessed=1000000):
    vmem = pl.BlockSpec(memory_space=pltpu.VMEM)
    held = sum(math.prod(a.shape) * a.dtype.itemsize for a in [*operands, *jax.tree.leaves(out_shape)])
    held += sum(
        math.prod(a.shape) * np.dtype(a.dtype).itemsize
        for a in scratch
        if a.memory_space == pltpu.VMEM
    )
    limit = 2 * held + 4 * 1024 * 1024
    specs = [
        pl.BlockSpec(memory_space=pltpu.SMEM if i in smem else pl.ANY if i in hbm else pltpu.VMEM)
        for i in range(len(operands))
    ]
    return pl.pallas_call(
        kernel,
        out_shape=out_shape,
        in_specs=specs,
        out_specs=jax.tree.map(lambda _: vmem, out_shape),
        scratch_shapes=list(scratch),
        compiler_params=pltpu.CompilerParams(vmem_limit_bytes=limit),
        cost_estimate=pl.CostEstimate(
            flops=1000000, bytes_accessed=bytes_accessed, transcendentals=0
        ),
    )(*operands)


def stages_of(count):
    stages, stride = [], 1
    while count > 1 and len(stages) < 2 and count % 2 == 0:
        stages.append((stride, 2))
        stride, count = stride * 2, count // 2
    if count > 1:
        stages.append((stride, count))
    return stages[::-1]


def send_pos(array, count, stride, size, delta):
    pairs = []
    for p in range(count):
        a = (p // stride) % size
        pairs.append((p, p + ((a + delta) % size - a) * stride))
    return lax.ppermute(array, "pos", pairs)


def send_all(parts, count, stage):
    stride, size = stage
    return [send_pos(part, count, stride, size, delta) for delta in range(1, size) for part in parts]


def lay_together(parts, order):
    size = parts[0].shape[1]
    whole = jnp.zeros((parts[0].shape[0], size * len(parts), parts[0].shape[2]), parts[0].dtype)
    for at in order:
        whole = lax.dynamic_update_slice(whole, parts[at], (0, at * size, 0))
    return whole


def after(array, *others):
    return lax.optimization_barrier((array, *others))[0]


def per_device(
    skip_stream_input,
    lateral_asking_vectors,
    lateral_matched_vectors,
    lateral_carried_vectors,
    lateral_closing_linear,
    upright_normalizer_multiplier,
    upright_threefold_linear,
    upright_closing_linear,
    regression_factors,
    regression_offset,
):
    rows, sites, embed = lateral_asking_vectors.shape
    heads = regression_factors.shape[0]
    head = embed // heads
    seq_count = lax.axis_size("seq")
    pos_count = lax.axis_size("pos")
    length = sites * pos_count
    slab_width = length // seq_count
    cells = rows * sites
    pos_index = lax.axis_index("pos").astype(jnp.int32)
    seq_index = lax.axis_index("seq").astype(jnp.int32)
    swap = [(s, 1 - s) for s in range(2)]
    columns = upright_threefold_linear.shape[1]
    swapped = seq_count == 2 and columns % 128 == 0

    stages = stages_of(pos_count)
    outer = stages[0]
    size = outer[1]
    middle = stages[1] if len(stages) > 1 else None

    scalars = jnp.stack([seq_index, pos_index])
    head_rows = round_up(heads, 8)
    width = lane_block(embed, head)
    key_first = [lateral_matched_vectors] + send_all([lateral_matched_vectors], pos_count, outer)
    key_parts = [lay_together(key_first, [0, 1, *range(3, size), *range(2, min(size, 3))])]
    value_first = [after(lateral_carried_vectors, key_parts[0])]
    value_first += [
        send_pos(lateral_carried_vectors, pos_count, *outer, delta) for delta in range(outer[1] - 1, 0, -1)
    ][::-1]
    masked = call(
        functools.partial(query_kernel, head),
        jax.ShapeDtypeStruct((rows, heads * sites, width), BF16),
        [after(lateral_asking_vectors, key_parts[0])],
        hbm=(0,),
        scratch=[pltpu.VMEM((rows, sites, embed), BF16), pltpu.SemaphoreType.DMA((1,))],
    )
    if middle:
        key_parts += send_all(key_parts, pos_count, middle)
    value_first[-1] = after(value_first[-1], masked)
    value_own = lay_together(
        value_first, [0, *range(size - 1, size - 2, -1), *range(1, size - 2), *range(max(size - 2, 1), size - 1)]
    )
    value_parts = [value_own]
    if middle:
        value_parts += send_all(value_parts, pos_count, middle)
    if len(stages) > 2:
        late_parts = [after(key_parts[0], *key_parts[1:])] + key_parts[1:]
        key_parts += send_all(late_parts, pos_count, stages[2])
    partial = call(
        functools.partial(logits_kernel, len(key_parts)),
        jax.ShapeDtypeStruct((heads * sites, length), F32),
        [masked, *key_parts],
    )
    padded = round_up(heads, 128)
    head_factors, order, own_select, slab_select, pick, spread = call(
        functools.partial(prepare_kernel, heads, sites, stages),
        (
            jax.ShapeDtypeStruct((head_rows + 8, 128), F32),
            jax.ShapeDtypeStruct((length, length), BF16),
            jax.ShapeDtypeStruct((sites, length), F32),
            jax.ShapeDtypeStruct((length, slab_width), F32),
            jax.ShapeDtypeStruct((embed, padded), BF16),
            jax.ShapeDtypeStruct((padded, embed), BF16),
        ),
        [after(scalars, partial), regression_factors, regression_offset],
        smem=(0, 1, 2),
    )
    if seq_count == 2:
        partials = [partial, after(lax.ppermute(partial, "seq", swap), order)]
    else:
        partials = [lax.psum(partial, "seq")]
    shares, pair_local = call(
        functools.partial(
            softmax_kernel, 1.0 / (math.sqrt(head) * math.sqrt(rows * seq_count)), heads
        ),
        (
            jax.ShapeDtypeStruct((heads * sites, length), BF16),
            jax.ShapeDtypeStruct((pos_count, head_rows + sites, length), F32),
        ),
        [*partials, head_factors, order],
        scratch=[pltpu.VMEM((head_rows + sites, length), F32)],
    )
    if len(stages) > 2:
        value_parts = value_parts[:1] + [after(part, pair_local) for part in value_parts[1:]]
        value_parts += send_all(value_parts, pos_count, stages[2])
    hidden, normed, one = call(
        functools.partial(mix_kernel, head, len(value_parts)),
        (
            jax.ShapeDtypeStruct((cells, embed), F32),
            jax.ShapeDtypeStruct((cells, embed), BF16),
            jax.ShapeDtypeStruct((1, columns), BF16),
        ),
        [
            shares,
            *value_parts,
            lateral_closing_linear,
            skip_stream_input,
            upright_normalizer_multiplier,
        ],
        scratch=[pltpu.VMEM((cells, embed), F32)],
    )
    pair_all = lax.all_to_all(pair_local, "pos", split_axis=0, concat_axis=0, tiled=True)
    pairing_chances = call(
        functools.partial(contact_kernel, heads),
        jax.ShapeDtypeStruct((sites, slab_width), F32),
        [pair_all, head_factors, own_select, slab_select],
        scratch=[pltpu.VMEM((head_rows + sites, length), F32)],
    )
    if swapped:
        normed_all = [normed, lax.ppermute(normed, "seq", swap)]
        weight = upright_threefold_linear * one
    else:
        normed_all = [normed]
        weight = lax.all_gather(upright_threefold_linear, "seq", axis=1, tiled=True)
    projected = call(
        functools.partial(project_kernel, len(normed_all)),
        jax.ShapeDtypeStruct((cells * len(normed_all), weight.shape[1]), BF16),
        [*normed_all, weight],
    )
    if swapped:
        column, column_inputs = swapped_column_kernel, [
            projected,
            lax.ppermute(projected, "seq", swap),
        ]
    else:
        key_value = lax.all_gather(projected[:, embed:], "seq", axis=0, tiled=True)
        column, column_inputs = column_kernel, [projected[:, :embed], key_value]
    alignment_output = call(
        functools.partial(column, 1.0 / math.sqrt(head)),
        jax.ShapeDtypeStruct((rows, sites, embed), BF16),
        [
            *column_inputs,
            hidden,
            after(upright_closing_linear, projected),
            pick,
            spread,
        ],
        scratch=[
            pltpu.VMEM((cells * rows * seq_count, embed), F32),
            pltpu.VMEM((cells, embed), F32),
        ],
    )
    return alignment_output, pairing_chances


def solution(mesh):
    cells = P("seq", "pos", None)
    return jax.shard_map(
        per_device,
        mesh=mesh,
        in_specs=(cells, cells, cells, cells, P(), P(), P(None, "seq"), P(), P(), P()),
        out_specs=(cells, P("pos", "seq")),
        check_vma=False,
    )
```
